128 devices in a mesh: section: 2 (over z_hi), render: 4 (over z_lo, core), dp: 16 (over y, x).
Axes of the slice: x: 4, y: 4, z: 4 (z_hi: 2, z_lo: 2; z = z_hi * 2 + z_lo), core: 2. Of those that a mesh axis runs over, the one named last changes fastest.
Arguments:
- section_tokens: bfloat16 [2, 16, 512, 2048], P('section', 'dp', 'render'), may hold values from -60 to 60
- w_qkv: bfloat16 [2, 2048, 3072], P('section', 'dp'), may hold values from -0.5 to 0.5
- w_out: bfloat16 [2, 1024, 2048], P('section', 'dp'), may hold values from -0.1875 to 0.1875
- gains: float32 [2, 2048], P('section'), may hold values from 0.25 to 1.75
- cotangent: bfloat16 [16, 512, 2048], P('dp', 'render'), may hold values from -6 to 6
Outputs:
- token_grads: bfloat16 [2, 16, 512, 2048], P('section', 'dp', 'render')
- qkv_grads: float32 [2, 2048, 3072], P('section', 'dp')
- out_grads: float32 [2, 1024, 2048], P('section', 'dp')
- gain_grads: float32 [2, 2048], P('section')
The draws below stay inside these ranges and needn't reach their ends.
All inputs are finite; a program needn't handle non-finite values.
Results may differ from the reference program's by a relative error of at most 0.02.
Values may be sent and summed in bfloat16 or wider, within the bound.
No kernel may reach another device: no remote copies, remote signals or barrier semaphores. Data moves between devices by JAX's collectives and lax.ppermute only.
A program may use at most 192 MiB of HBM per device.

```python
import math
import jax
import jax.numpy as jnp
from jax import lax

D = 2048
HEADS = 8
HD = 128
ROWS = 128
HW = 1024
TOKS = 512
SCENES = 16
N_RENDER = 4


def draw_section_tokens(key, part):
    full_shape = (2, SCENES, TOKS, D)
    base_noise = jax.random.normal(jax.random.fold_in(key, 1), full_shape, jnp.float32)
    tokens = base_noise
    return jnp.clip(tokens, -60.0, 60.0).astype(jnp.bfloat16)


def draw_w_qkv(key, part):
    full_shape = (2, D, 3 * HEADS * HD)
    weight = jnp.clip(jax.random.normal(jax.random.fold_in(key, 5), full_shape, jnp.float32), -6.0, 6.0) / math.sqrt(D)
    return jnp.clip(weight, -0.5, 0.5).astype(jnp.bfloat16)


def level_of(stream_key, dims, cuts, low, largest):
    loudness = 1.0
    for dim, blocks in cuts:
        steps = jax.random.uniform(jax.random.fold_in(jax.random.fold_in(stream_key, 6), dim), (blocks,), jnp.float32, low / len(cuts), largest / len(cuts))
        loudness = loudness * jnp.repeat(jnp.exp(steps), dims[dim] // blocks).reshape((-1,) + (1,) * (len(dims) - 1 - dim))
    return loudness


def gaussian(own_key, extent, width, bound, split=(), dtype=jnp.bfloat16):
    entries = jax.random.normal(own_key, extent, jnp.float32) * width
    if len(split) > 0:
        entries = level_of(own_key, extent, split, -0.22, 0.18) * entries
    return jnp.clip(entries, min=-bound, max=bound).astype(dtype)


def setup_inputs(seed: int = 0) -> dict:
    key_of = jax.random.split(jax.random.key(seed), 6)
    section_tokens = draw_section_tokens(jax.random.fold_in(key_of[5], 71), 0)
    w_qkv = draw_w_qkv(jax.random.fold_in(key_of[5], 71), 0)
    w_out = gaussian(key_of[2], (2, HW, D), HW ** -0.5, 0.1875, ((0, 2), (1, 16)))
    gains = jnp.clip(1.0 + 0.15 * jax.random.normal(key_of[3], (2, D), jnp.float32), 0.25, 1.75)
    cotangent = gaussian(key_of[4], (SCENES, TOKS, D), 1.0, 6.0, ((0, 16), (1, 4)))
    return {"section_tokens": section_tokens, "w_qkv": w_qkv, "w_out": w_out, "gains": gains, "cotangent": cotangent}


NORM_EPSILON = 1e-06

def rms_norm(values, gain_row):
    wide_rows = values.astype(jnp.float32)
    row_scale = lax.rsqrt(lax.optimization_barrier(jnp.mean(wide_rows * wide_rows, axis=-1, keepdims=True)) + NORM_EPSILON)
    return ((wide_rows * row_scale * gain_row).astype(jnp.bfloat16), row_scale)

def norm_back(values, row_scale, gain_row, upstream):
    wide_rows = values.astype(jnp.float32)
    grad_wide = upstream.astype(jnp.float32)
    scaled = grad_wide * gain_row
    inner_sum = lax.optimization_barrier(jnp.sum(scaled * wide_rows, axis=-1, keepdims=True))
    result = row_scale * scaled - wide_rows * row_scale ** 3 * inner_sum / values.shape[-1]
    gain_term = lax.optimization_barrier(jnp.sum(grad_wide * wide_rows * row_scale, axis=0))
    return (result, gain_term)

def to_half(values):
    return lax.optimization_barrier(values.astype(jnp.bfloat16)).astype(jnp.float32)

def matmul(left, right):
    return jnp.dot(left, right, preferred_element_type=jnp.float32)

def split_heads(values):
    return values.astype(jnp.float32).reshape(values.shape[0], HEADS, HD)

def attend(queries, key_rows, value_rows):
    factor = HD ** (-0.5)
    scores = jnp.einsum('qhd,khd->hqk', split_heads(queries), split_heads(key_rows)) * factor
    row_top = lax.optimization_barrier(jnp.max(scores, axis=-1, keepdims=True))
    raised = jnp.exp(scores - row_top)
    row_total = lax.optimization_barrier(jnp.sum(raised, axis=-1, keepdims=True))
    attn_prob = raised / row_total
    mixed_heads = jnp.einsum('hqk,khd->qhd', to_half(attn_prob), split_heads(value_rows))
    return (mixed_heads.reshape(queries.shape[0], HEADS * HD).astype(jnp.bfloat16), attn_prob)

def attend_back(queries, key_rows, value_rows, attn_prob, upstream):
    factor = HD ** (-0.5)
    grad_prob = jnp.einsum('qhd,khd->hqk', split_heads(upstream), split_heads(value_rows))
    row_delta = lax.optimization_barrier(jnp.sum(grad_prob * attn_prob, axis=-1, keepdims=True))
    grad_score = to_half(attn_prob * (grad_prob - row_delta) * factor)
    grad_query = jnp.einsum('hqk,khd->qhd', grad_score, split_heads(key_rows)).reshape(queries.shape[0], HEADS * HD)
    grad_key = jnp.einsum('hqk,qhd->khd', grad_score, split_heads(queries)).reshape(key_rows.shape[0], HEADS * HD)
    grad_value = jnp.einsum('hqk,qhd->khd', to_half(attn_prob), split_heads(upstream)).reshape(key_rows.shape[0], HEADS * HD)
    return (grad_query, grad_key, grad_value)

def reference(section_tokens, w_qkv, w_out, gains, cotangent):
    head_width = HEADS * HD
    half_rows = ROWS // 2
    lat_rows = N_RENDER * half_rows
    scene_rows = N_RENDER * ROWS
    enc_qkv = w_qkv[0]
    dec_qkv = w_qkv[1]
    enc_out = w_out[0]
    dec_out = w_out[1]
    enc_gain = gains[0].astype(jnp.float32)
    dec_gain = gains[1].astype(jnp.float32)

    def scene_step(totals, inputs):
        enc_tokens, dec_tokens, upstream = inputs
        enc_norm, enc_scale = rms_norm(enc_tokens, enc_gain)
        enc_proj = matmul(enc_norm, enc_qkv).astype(jnp.bfloat16)
        blocked = enc_proj.reshape(N_RENDER, ROWS, 3 * head_width)
        lat_query = blocked[:, half_rows:, :head_width].reshape(lat_rows, head_width)
        lat_input = enc_tokens.reshape(N_RENDER, ROWS, D)[:, half_rows:].reshape(lat_rows, D)
        lat_norm_enc = enc_norm.reshape(N_RENDER, ROWS, D)[:, half_rows:].reshape(lat_rows, D)
        enc_keys = enc_proj[:, head_width:2 * head_width]
        enc_values = enc_proj[:, 2 * head_width:]
        enc_mixed, enc_prob = attend(lat_query, enc_keys, enc_values)
        latent = (lat_input.astype(jnp.float32) + matmul(enc_mixed, enc_out)).astype(jnp.bfloat16)
        lat_norm, lat_scale = rms_norm(latent, dec_gain)
        lat_kv = matmul(lat_norm, dec_qkv[:, head_width:]).astype(jnp.bfloat16)
        dec_norm, dec_scale = rms_norm(dec_tokens, dec_gain)
        dec_proj = matmul(dec_norm, dec_qkv).astype(jnp.bfloat16)
        lat_grad_sum = jnp.zeros((lat_rows, 2 * head_width), jnp.float32)
        dec_out_sum = jnp.zeros((head_width, D), jnp.float32)
        view_grads = []
        for view_index in range(N_RENDER):
            first = view_index * ROWS
            proj_view = dec_proj[first:first + ROWS]
            key_rows = jnp.concatenate([lat_kv[:, :head_width], proj_view[:, head_width:2 * head_width]], 0)
            value_rows = jnp.concatenate([lat_kv[:, head_width:], proj_view[:, 2 * head_width:]], 0)
            mixed_view, prob_view = attend(proj_view[:, :head_width], key_rows, value_rows)
            cot_view = upstream[first:first + ROWS]
            dec_out_sum = dec_out_sum + to_half(matmul(mixed_view.T, cot_view))
            grad_mixed = matmul(cot_view, dec_out.T).astype(jnp.bfloat16)
            grad_query, grad_key, grad_value = attend_back(proj_view[:, :head_width], key_rows, value_rows, prob_view, grad_mixed)
            lat_grad_sum = lat_grad_sum + jnp.concatenate([grad_key[:lat_rows], grad_value[:lat_rows]], 1)
            view_grads.append(jnp.concatenate([grad_query, grad_key[lat_rows:], grad_value[lat_rows:]], 1).astype(jnp.bfloat16))
        lat_grad = lat_grad_sum.astype(jnp.bfloat16)
        dec_grad_proj = jnp.concatenate(view_grads, 0)
        dec_qkv_sum = jnp.zeros((D, 3 * head_width), jnp.float32)
        for view_index in range(N_RENDER):
            first = view_index * ROWS
            lat_first = view_index * half_rows
            partial_sum = matmul(dec_norm[first:first + ROWS].T, dec_grad_proj[first:first + ROWS])
            extra_sum = matmul(lat_norm[lat_first:lat_first + half_rows].T, lat_grad[lat_first:lat_first + half_rows])
            partial_sum = partial_sum.at[:, head_width:].add(extra_sum)
            dec_qkv_sum = dec_qkv_sum + to_half(partial_sum)
        grad_dec_norm = matmul(dec_grad_proj, dec_qkv.T).astype(jnp.bfloat16)
        grad_lat_norm = matmul(lat_grad, dec_qkv[:, head_width:].T).astype(jnp.bfloat16)
        dec_back, dec_gain_first = norm_back(dec_tokens, dec_scale, dec_gain, grad_dec_norm)
        dec_result = (upstream.astype(jnp.float32) + dec_back).astype(jnp.bfloat16)
        lat_back, dec_gain_second = norm_back(latent, lat_scale, dec_gain, grad_lat_norm)
        lat_upstream = lat_back.astype(jnp.bfloat16)
        grad_enc_mixed = matmul(lat_upstream, enc_out.T).astype(jnp.bfloat16)
        grad_query, grad_key, grad_value = attend_back(lat_query, enc_keys, enc_values, enc_prob, grad_enc_mixed)
        query_grad = grad_query.astype(jnp.bfloat16)
        key_grad = jnp.concatenate([grad_key, grad_value], 1).astype(jnp.bfloat16)
        enc_out_sum = jnp.zeros((head_width, D), jnp.float32)
        enc_qkv_sum = jnp.zeros((D, 3 * head_width), jnp.float32)
        for view_index in range(N_RENDER):
            first = view_index * ROWS
            lat_first = view_index * half_rows
            enc_out_sum = enc_out_sum + to_half(matmul(enc_mixed[lat_first:lat_first + half_rows].T, lat_upstream[lat_first:lat_first + half_rows]))
            query_part = matmul(lat_norm_enc[lat_first:lat_first + half_rows].T, query_grad[lat_first:lat_first + half_rows])
            key_part = matmul(enc_norm[first:first + ROWS].T, key_grad[first:first + ROWS])
            enc_qkv_sum = enc_qkv_sum + to_half(jnp.concatenate([query_part, key_part], 1))
        grad_enc_norm = matmul(key_grad, enc_qkv[:, head_width:].T).reshape(N_RENDER, ROWS, D)
        query_back = matmul(query_grad, enc_qkv[:, :head_width].T).reshape(N_RENDER, half_rows, D)
        grad_enc_norm = grad_enc_norm.at[:, half_rows:].add(query_back).reshape(scene_rows, D).astype(jnp.bfloat16)
        enc_back, enc_gain_term = norm_back(enc_tokens, enc_scale, enc_gain, grad_enc_norm)
        residual = jnp.zeros((N_RENDER, ROWS, D), jnp.float32).at[:, half_rows:].set(lat_upstream.astype(jnp.float32).reshape(N_RENDER, half_rows, D))
        enc_result = (enc_back + residual.reshape(scene_rows, D)).astype(jnp.bfloat16)
        enc_qkv_total, dec_qkv_total, enc_out_total, dec_out_total, enc_gain_total, dec_gain_total = totals
        new_totals = (enc_qkv_total + enc_qkv_sum, dec_qkv_total + dec_qkv_sum, enc_out_total + enc_out_sum, dec_out_total + dec_out_sum, enc_gain_total + enc_gain_term, dec_gain_total + dec_gain_first + dec_gain_second)
        return (new_totals, (enc_result, dec_result))
    initial = (jnp.zeros((D, 3 * head_width), jnp.float32), jnp.zeros((D, 3 * head_width), jnp.float32), jnp.zeros((head_width, D), jnp.float32), jnp.zeros((head_width, D), jnp.float32), jnp.zeros((D,), jnp.float32), jnp.zeros((D,), jnp.float32))
    totals, results = lax.scan(scene_step, initial, (section_tokens[0], section_tokens[1], cotangent))
    token_grads = jnp.stack([results[0], results[1]])
    qkv_grads = jnp.stack([totals[0], totals[1]])
    out_grads = jnp.stack([totals[2], totals[3]])
    gain_grads = jnp.stack([totals[4], totals[5]])
    return (token_grads, qkv_grads, out_grads, gain_grads)
```

```python
import jax
import jax.numpy as jnp
from jax import lax
from jax.sharding import Mesh
from jax.sharding import PartitionSpec as P

HD = 128
MY = 2
MW = MY * HD
NORM_EPSILON = 1e-06
RENDER = ("zl", "core")
DP = ("y", "x")
SWAP = [(0, 1), (1, 0)]
DIAG = [(0, 3), (1, 2), (2, 1), (3, 0)]
bf16 = jnp.bfloat16
f32 = jnp.float32


def mm(left, right):
    return jnp.dot(left, right, preferred_element_type=f32)


def mm_tn(left, right):
    return lax.dot_general(left, right, (((0,), (0,)), ((), ())), preferred_element_type=f32)


def mm_nt(left, right):
    return lax.dot_general(left, right, (((1,), (1,)), ((), ())), preferred_element_type=f32)


def core_swap(t):
    return lax.ppermute(t, "core", SWAP)


def z_swap(t):
    return lax.ppermute(t, "zl", SWAP)


def gather_rel(t):
    z = z_swap(t)
    c = core_swap(t)
    return [t, c, z, core_swap(z)]


def spread_rel(b):
    return [b[0], core_swap(b[1]), z_swap(b[2]), lax.ppermute(b[3], RENDER, DIAG)]


def sum_rel(b0, b1, b2, b3):
    near, far = core_swap(b1), core_swap(b3)
    far = (b2.astype(f32) + far.astype(f32)).astype(bf16)
    return b0.astype(f32) + near.astype(f32) + z_swap(far).astype(f32)


def rows_of(j, t):
    n = t.shape[0] // 4
    return [t[(i ^ j) * n : ((i ^ j) + 1) * n] for i in range(4)]


def sum_dp(t):
    blocks = t.reshape(16, t.shape[0] // 16, t.shape[1])
    return lax.all_to_all(blocks, DP, 0, 0, tiled=True).astype(f32).sum(axis=0)


def rms_norm(values, gain_row):
    wide = values.astype(f32)
    scale = lax.rsqrt(jnp.mean(wide * wide, axis=-1, keepdims=True) + NORM_EPSILON)
    return (wide * scale * gain_row).astype(bf16), scale


def norm_back(values, scale, gain_row, upstream):
    wide = values.astype(f32)
    grad = upstream.astype(f32)
    scaled = grad * gain_row
    inner = jnp.sum(scaled * wide, axis=-1, keepdims=True)
    result = scale * scaled - wide * scale**3 * inner / values.shape[-1]
    return result, jnp.sum(grad * wide * scale, axis=0)


def heads(t):
    return [t[:, h * HD : (h + 1) * HD] for h in range(MY)]


FACTOR = HD**-0.5


def softmax(scores):
    top = jnp.max(scores, axis=-1, keepdims=True)
    raised = jnp.exp(scores - top)
    return raised / jnp.sum(raised, axis=-1, keepdims=True)


def encoder_forward(q, k, v):
    probs, outs = [], []
    for qh, kh, vh in zip(heads(q), heads(k), heads(v)):
        p = softmax(mm_nt(qh, kh) * FACTOR)
        probs.append(p)
        outs.append(mm(p.astype(bf16), vh).astype(bf16))
    return jnp.concatenate(outs, 1), jnp.stack(probs)


def encoder_backward(q, k, v, probs, up):
    dq, dk, dv = [], [], []
    for h, (qh, kh, vh, uh) in enumerate(zip(heads(q), heads(k), heads(v), heads(up))):
        p = probs[h]
        dp = mm_nt(uh, vh)
        delta = jnp.sum(dp * p, axis=-1, keepdims=True)
        ds = (p * (dp - delta) * FACTOR).astype(bf16)
        dq.append(mm(ds, kh).astype(bf16))
        dk.append(mm_tn(ds, qh).astype(bf16))
        dv.append(mm_tn(p.astype(bf16), uh).astype(bf16))
    return jnp.concatenate(dq, 1), jnp.concatenate(dk + dv, 1)


def decoder_attention(q, k, v, kz, vz, up):
    out, dq, dk, dv, dkz, dvz = [], [], [], [], [], []
    views = q.shape[0] // 128
    lat = kz.shape[0]

    def per_view(a, b):
        return lax.dot_general(
            a.reshape(views, 128, -1), b.reshape(views, 128, -1),
            (((2,), (2,)), ((0,), (0,))), preferred_element_type=f32,
        ).reshape(views * 128, 128)

    def own_mm(p, b):
        return lax.dot_general(
            p.reshape(views, 128, 128), b.reshape(views, 128, HD),
            (((2,), (1,)), ((0,), (0,))), preferred_element_type=f32,
        ).reshape(views * 128, HD)

    def own_tn(p, b):
        return lax.dot_general(
            p.reshape(views, 128, 128), b.reshape(views, 128, HD),
            (((1,), (1,)), ((0,), (0,))), preferred_element_type=f32,
        ).reshape(views * 128, HD)

    for qh, kh, vh, kzh, vzh, uh in zip(*map(heads, (q, k, v, kz, vz, up))):
        s = jnp.concatenate([mm_nt(qh, kzh), per_view(qh, kh)], 1) * FACTOR
        p = softmax(s)
        pb = p.astype(bf16)
        out.append((mm(pb[:, :lat], vzh) + own_mm(pb[:, lat:], vh)).astype(bf16))
        dp = jnp.concatenate([mm_nt(uh, vzh), per_view(uh, vh)], 1)
        delta = jnp.sum(dp * p, axis=-1, keepdims=True)
        ds = (p * (dp - delta) * FACTOR).astype(bf16)
        dq.append((mm(ds[:, :lat], kzh) + own_mm(ds[:, lat:], kh)).astype(bf16))
        dk.append(own_tn(ds[:, lat:], qh).astype(bf16))
        dv.append(own_tn(pb[:, lat:], uh).astype(bf16))
        dkz.append(mm_tn(ds[:, :lat], qh).astype(bf16))
        dvz.append(mm_tn(pb[:, :lat], uh).astype(bf16))
    cat = jnp.concatenate
    return cat(out, 1), cat(dq + dk + dv, 1), cat(dkz + dvz, 1)


def shards(section_tokens, w_qkv, w_out, gains, cotangent):
    tokens = section_tokens[0, 0]
    upstream = cotangent[0]
    gain_row = gains[0]
    width = tokens.shape[1]
    rank = lax.axis_index("zl") * 2 + lax.axis_index("core")
    is_encoder = lax.axis_index("section") == 0
    half = tokens.shape[0] // 2

    mine = w_qkv[0].reshape(-1, 3, 4, MW)
    mine = lax.dynamic_index_in_dim(mine, rank, 2, keepdims=False).reshape(-1, 3 * MW)
    w_h = lax.all_gather(mine, DP, axis=0, tiled=True)
    cols = width // 4
    out_mine = lax.dynamic_slice_in_dim(w_out[0], rank * cols, cols, 1)
    w_col = lax.all_gather(out_mine, DP, axis=0, tiled=True).reshape(4, MW, cols)
    w_rel = [lax.dynamic_index_in_dim(w_col, rank ^ j, 0, keepdims=False) for j in range(4)]
    order = [rank ^ j for j in range(4)]

    def absolute(blocks, dim):
        both = jnp.stack(blocks)
        return jnp.concatenate(
            [lax.dynamic_index_in_dim(both, i, 0, keepdims=False) for i in order], dim
        )

    rows = jnp.concatenate(gather_rel(tokens), 0)
    ups = jnp.concatenate(gather_rel(upstream), 0)
    normed, scales = rms_norm(rows, gain_row)
    scale = scales[: tokens.shape[0]]
    projected = mm(normed, w_h).astype(bf16)
    q, k, v = projected[:, :MW], projected[:, MW : 2 * MW], projected[:, 2 * MW :]
    w_row = absolute(spread_rel(w_rel), 1)

    def latents(t):
        return t.reshape(4, 2 * half, -1)[:, half:].reshape(4 * half, -1)

    lat_q = latents(q)
    enc_o, enc_p = lax.cond(
        is_encoder,
        lambda: encoder_forward(lat_q, k, v),
        lambda: (jnp.zeros((4 * half, MW), bf16), jnp.zeros((MY, 4 * half, k.shape[0]), f32)),
    )
    enc_all = [jnp.concatenate(rows_of(j, t), 0) for j, t in enumerate(gather_rel(enc_o))]
    lat_cols = lax.dynamic_slice_in_dim(latents(rows), rank * cols, cols, 1).astype(f32)
    z_cols = (
        lat_cols + mm(jnp.concatenate(enc_all, 1), jnp.concatenate(w_rel, 0))
    ).astype(bf16)
    z_cols = lax.ppermute(z_cols, "section", [(0, 1)])
    z_blocks = [jnp.concatenate(rows_of(j, t), 0) for j, t in enumerate(gather_rel(z_cols))]
    z = absolute(z_blocks, 1)
    up_o = mm_nt(ups, w_row).astype(bf16)

    def decoder():
        nz, z_scales = rms_norm(z, gain_row)
        kvz = mm(nz, w_h[:, MW:]).astype(bf16)
        o, d_proj, d_kvz = decoder_attention(q, k, v, kvz[:, :MW], kvz[:, MW:], up_o)
        d_nz = mm_nt(d_kvz, w_h[:, MW:]).astype(bf16)
        return o, d_proj, d_kvz, nz, z_scales[:half], d_nz

    dec_o, d_proj, d_kvz, nz, z_scale, d_nz = lax.cond(
        jnp.logical_not(is_encoder),
        decoder,
        lambda: (
            jnp.zeros((rows.shape[0], MW), bf16),
            jnp.zeros((rows.shape[0], 3 * MW), bf16),
            jnp.zeros((4 * half, 2 * MW), bf16),
            jnp.zeros((4 * half, width), bf16),
            jnp.zeros((half, 1), f32),
            jnp.zeros((4 * half, width), bf16),
        ),
    )
    d_nz = sum_rel(*[d_nz[j * half : (j + 1) * half] for j in range(4)]).astype(bf16)
    d_z, z_gain = norm_back(z[:half], z_scale, gain_row, d_nz)
    z_gain = jnp.where(is_encoder, 0.0, z_gain)
    d_z = lax.ppermute(d_z.astype(bf16), "section", [(1, 0)])
    d_z_all = jnp.concatenate(gather_rel(d_z), 0)

    dec_all = [jnp.concatenate(rows_of(j, t), 0) for j, t in enumerate(gather_rel(dec_o))]

    def encoder_back():
        up_e = mm_nt(d_z_all, w_row).astype(bf16)
        dq, dkv = encoder_backward(lat_q, k, v, enc_p, up_e)
        dq = jnp.pad(dq.reshape(4, half, MW), ((0, 0), (half, 0), (0, 0))).reshape(-1, MW)
        proj = jnp.concatenate([dq, dkv], 1)
        return proj, mm_tn(normed, proj).astype(bf16)

    def decoder_back():
        part = mm_tn(normed, d_proj)
        part = part.at[:, MW:].add(mm_tn(nz, d_kvz))
        return d_proj, part.astype(bf16)

    d_proj, qkv_part = lax.cond(is_encoder, encoder_back, decoder_back)

    def my_cols(t):
        return lax.dynamic_slice_in_dim(t, rank * cols, cols, 1)

    out_part = lax.cond(
        is_encoder,
        lambda: mm_tn(absolute(enc_all, 1), my_cols(d_z_all)).astype(bf16),
        lambda: mm_tn(absolute(dec_all, 1), my_cols(ups)).astype(bf16),
    )
    out_sum = sum_dp(out_part).astype(bf16)
    qkv_sum = sum_dp(qkv_part).astype(bf16)
    out_total = absolute(gather_rel(out_sum), 1).astype(f32)
    qkv_blocks = jnp.stack(gather_rel(qkv_sum)).reshape(4, -1, 3, MW)
    qkv_total = jnp.stack(
        [lax.dynamic_index_in_dim(qkv_blocks, i, 0, keepdims=False) for i in order], 2
    )
    qkv_total = qkv_total.reshape(-1, 12 * MW).astype(f32)

    d_n = mm_nt(d_proj, w_h).astype(bf16)
    n = tokens.shape[0]
    d_n = sum_rel(*[d_n[j * n : (j + 1) * n] for j in range(4)]).astype(bf16)
    back, gain_part = norm_back(tokens, scale, gain_row, d_n)
    residual = jnp.where(
        is_encoder,
        jnp.pad(d_z.astype(f32), ((half, 0), (0, 0))),
        upstream.astype(f32),
    )
    token_grad = (back + residual).astype(bf16)
    gain_total = lax.psum(gain_part + z_gain, RENDER + DP)
    return token_grad[None, None], qkv_total[None], out_total[None], gain_total[None]


def solution(mesh):
    fine = Mesh(mesh.devices.reshape(2, 2, 2, 4, 4), ("section", "zl", "core", "y", "x"))
    in_specs = (
        P("section", DP, RENDER, None),
        P("section", DP, None),
        P("section", DP, None),
        P("section", None),
        P(DP, RENDER, None),
    )
    out_specs = (
        P("section", DP, RENDER, None),
        P("section", DP, None),
        P("section", DP, None),
        P("section", None),
    )
    return jax.shard_map(shards, mesh=fine, in_specs=in_specs, out_specs=out_specs, check_vma=False)
```

```python
import jax
import jax.numpy as jnp
from jax import lax
from jax.experimental import pallas as pl
from jax.experimental.pallas import tpu as pltpu
from jax.sharding import Mesh
from jax.sharding import PartitionSpec as P

HD = 128
MY = 2
MW = MY * HD
NORM_EPSILON = 1e-06
RENDER = ("zl", "core")
DP = ("y", "x")
SWAP = [(0, 1), (1, 0)]
DIAG = [(0, 3), (1, 2), (2, 1), (3, 0)]
bf16 = jnp.bfloat16
f32 = jnp.float32


def mm(left, right):
    return jnp.dot(left, right, preferred_element_type=f32)


def mm_tn(left, right):
    return lax.dot_general(left, right, (((0,), (0,)), ((), ())), preferred_element_type=f32)


def mm_nt(left, right):
    return lax.dot_general(left, right, (((1,), (1,)), ((), ())), preferred_element_type=f32)


def core_swap(t):
    return lax.ppermute(t, "core", SWAP)


def z_swap(t):
    return lax.ppermute(t, "zl", SWAP)


def gather_rel(t):
    z = z_swap(t)
    c = core_swap(t)
    return [t, c, z, core_swap(z)]


def spread_rel(b):
    return [b[0], core_swap(b[1]), z_swap(b[2]), lax.ppermute(b[3], RENDER, DIAG)]


def sum_rel(b0, b1, b2, b3):
    near, far = core_swap(b1), core_swap(b3)
    far = (b2.astype(f32) + far.astype(f32)).astype(bf16)
    return b0.astype(f32) + near.astype(f32) + z_swap(far).astype(f32)


def rows_of(j, t):
    n = t.shape[0] // 4
    return [t[(i ^ j) * n : ((i ^ j) + 1) * n] for i in range(4)]


def sum_dp(t):
    blocks = t.reshape(16, t.shape[0] // 16, t.shape[1])
    return lax.all_to_all(blocks, DP, 0, 0, tiled=True).astype(f32).sum(axis=0)


def rms_norm(values, gain_row):
    wide = values.astype(f32)
    scale = lax.rsqrt(jnp.mean(wide * wide, axis=-1, keepdims=True) + NORM_EPSILON)
    return (wide * scale * gain_row).astype(bf16), scale


def norm_back(values, scale, gain_row, upstream):
    wide = values.astype(f32)
    grad = upstream.astype(f32)
    scaled = grad * gain_row
    inner = jnp.sum(scaled * wide, axis=-1, keepdims=True)
    result = scale * scaled - wide * scale**3 * inner / values.shape[-1]
    return result, jnp.sum(grad * wide * scale, axis=0)


FACTOR = HD**-0.5
VMEM = pl.BlockSpec(memory_space=pltpu.VMEM)


def kernel_call(body, inputs, outputs, flops, scratch=()):
    moved = sum(t.size * t.dtype.itemsize for t in inputs)
    moved += sum(t.size * t.dtype.itemsize for t in outputs)
    return pl.pallas_call(
        body,
        out_shape=outputs,
        in_specs=[VMEM] * len(inputs),
        out_specs=[VMEM] * len(outputs),
        scratch_shapes=scratch,
        compiler_params=pltpu.CompilerParams(vmem_limit_bytes=48 * 2**20),
        cost_estimate=pl.CostEstimate(flops=flops, bytes_accessed=moved, transcendentals=0),
    )(*inputs)


def shape(rows, cols, dtype=bf16):
    return jax.ShapeDtypeStruct((rows, cols), dtype)


def head(ref, part, h):
    at = part * MW + h * HD
    return slice(at, at + HD)


def latent_rows(ref, half, lanes):
    return jnp.concatenate(
        [ref[(2 * i + 1) * half : (2 * i + 2) * half, lanes] for i in range(4)], 0
    )


def softmax(scores):
    raised = jnp.exp(scores - jnp.max(scores, axis=-1, keepdims=True))
    return raised * (1.0 / jnp.sum(raised, axis=-1, keepdims=True))


def encoder_forward_body(proj, out):
    half = proj.shape[0] // 8
    for h in range(MY):
        q = latent_rows(proj, half, head(proj, 0, h))
        p = softmax(mm_nt(q, proj[:, head(proj, 1, h)]) * FACTOR)
        out[:, head(out, 0, h)] = mm(p.astype(bf16), proj[:, head(proj, 2, h)]).astype(bf16)


def encoder_back_body(d_z, w_row, proj, nt, d_proj, d_w, up):
    half = proj.shape[0] // 8
    up[...] = mm_nt(d_z[...], w_row[...]).astype(bf16)
    for h in range(MY):
        q = latent_rows(proj, half, head(proj, 0, h))
        k, v = proj[:, head(proj, 1, h)], proj[:, head(proj, 2, h)]
        u = up[:, head(up, 0, h)]
        p = softmax(mm_nt(q, k) * FACTOR)
        dp = mm_nt(u, v)
        delta = jnp.sum(dp * p, axis=-1, keepdims=True)
        ds = (p * (dp - delta) * FACTOR).astype(bf16)
        dq = mm(ds, k).astype(bf16)
        for i in range(4):
            at = 2 * i * half
            d_proj[at : at + half, head(d_proj, 0, h)] = jnp.zeros((half, HD), bf16)
            d_proj[at + half : at + 2 * half, head(d_proj, 0, h)] = dq[i * half : (i + 1) * half]
        d_proj[:, head(d_proj, 1, h)] = mm_tn(ds, q).astype(bf16)
        d_proj[:, head(d_proj, 2, h)] = mm_tn(p.astype(bf16), u).astype(bf16)
    step = 256
    for at in range(0, d_w.shape[0], step):
        d_w[at : at + step, :] = mm(nt[at : at + step, :], d_proj[...]).astype(bf16)


def decoder_body(z, gain, w, proj, up, out, d_proj, d_kvz, nz, scales, d_nz, kvz, acc):
    lat, width = z.shape
    for at in range(0, lat, 64):
        wide = z[at : at + 64, :].astype(f32)
        scale = lax.rsqrt(jnp.mean(wide * wide, axis=-1, keepdims=True) + NORM_EPSILON)
        nz[at : at + 64, :] = (wide * scale * gain[...]).astype(bf16)
        scales[at : at + 64, :] = scale
    kvz[...] = mm(nz[...], w[:, MW:]).astype(bf16)
    views = proj.shape[0] // 128
    for h in range(MY):
        kz, vz = kvz[:, head(kvz, 0, h)], kvz[:, head(kvz, 1, h)]
        for i in range(views):
            rows = slice(i * 128, (i + 1) * 128)
            q, k, v = [proj[rows, head(proj, part, h)] for part in range(3)]
            u = up[rows, head(up, 0, h)]
            s = mm_nt(q, kz) * FACTOR
            t = mm_nt(q, k) * FACTOR
            top = jnp.maximum(
                jnp.max(s, axis=-1, keepdims=True), jnp.max(t, axis=-1, keepdims=True)
            )
            s, t = jnp.exp(s - top), jnp.exp(t - top)
            total = jnp.sum(s, axis=-1, keepdims=True) + jnp.sum(t, axis=-1, keepdims=True)
            s, t = s * (1.0 / total), t * (1.0 / total)
            sb, tb = s.astype(bf16), t.astype(bf16)
            out[rows, head(out, 0, h)] = (mm(sb, vz) + mm(tb, v)).astype(bf16)
            ds, dt = mm_nt(u, vz), mm_nt(u, v)
            delta = jnp.sum(ds * s, axis=-1, keepdims=True) + jnp.sum(dt * t, axis=-1, keepdims=True)
            ds = (s * (ds - delta) * FACTOR).astype(bf16)
            dt = (t * (dt - delta) * FACTOR).astype(bf16)
            d_proj[rows, head(d_proj, 0, h)] = (mm(ds, kz) + mm(dt, k)).astype(bf16)
            d_proj[rows, head(d_proj, 1, h)] = mm_tn(dt, q).astype(bf16)
            d_proj[rows, head(d_proj, 2, h)] = mm_tn(tb, u).astype(bf16)
            dkz, dvz = mm_tn(ds, q), mm_tn(sb, u)
            if i > 0:
                dkz, dvz = dkz + acc[:, head(acc, 0, h)], dvz + acc[:, head(acc, 1, h)]
            acc[:, head(acc, 0, h)], acc[:, head(acc, 1, h)] = dkz, dvz
    d_kvz[...] = acc[...].astype(bf16)
    for at in range(0, width, 512):
        d_nz[:, at : at + 512] = mm_nt(d_kvz[...], w[at : at + 512, MW:]).astype(bf16)


def sum_everywhere(t):
    for axis, n in (("core", 2), ("zl", 2), ("x", 4), ("y", 4)):
        for bit in (1, 2)[: n // 2]:
            t = t + lax.ppermute(t, axis, [(i, i ^ bit) for i in range(n)])
    return t


def shards(section_tokens, w_qkv, w_out, gains, cotangent):
    tokens = section_tokens[0, 0]
    upstream = cotangent[0]
    gain_row = gains[0]
    width = tokens.shape[1]
    rank = lax.axis_index("zl") * 2 + lax.axis_index("core")
    is_encoder = lax.axis_index("section") == 0
    half = tokens.shape[0] // 2

    mine = w_qkv[0].reshape(-1, 3, 4, MW)
    mine = lax.dynamic_index_in_dim(mine, rank, 2, keepdims=False).reshape(-1, 3 * MW)
    w_h = lax.all_gather(mine, DP, axis=0, tiled=True)
    cols = width // 4
    out_mine = lax.dynamic_slice_in_dim(w_out[0], rank * cols, cols, 1)
    w_col = lax.all_gather(out_mine, DP, axis=0, tiled=True).reshape(4, MW, cols)
    w_rel = [lax.dynamic_index_in_dim(w_col, rank ^ j, 0, keepdims=False) for j in range(4)]
    order = [rank ^ j for j in range(4)]

    def absolute(blocks, dim):
        both = jnp.stack(blocks)
        return jnp.concatenate(
            [lax.dynamic_index_in_dim(both, i, 0, keepdims=False) for i in order], dim
        )

    rows = jnp.concatenate(gather_rel(tokens), 0)
    ups = jnp.concatenate(gather_rel(upstream), 0)
    normed, scales = rms_norm(rows, gain_row)
    scale = scales[: tokens.shape[0]]
    projected = mm(normed, w_h).astype(bf16)
    w_row = absolute(spread_rel(w_rel), 1)

    def latents(t):
        return t.reshape(4, 2 * half, -1)[:, half:].reshape(4 * half, -1)

    count, lat = rows.shape[0], 4 * half
    enc_o = lax.cond(
        is_encoder,
        lambda: kernel_call(
            encoder_forward_body, [projected], [shape(lat, MW)], 4 * lat * count * MW
        )[0],
        lambda: jnp.zeros((lat, MW), bf16),
    )
    enc_all = [jnp.concatenate(rows_of(j, t), 0) for j, t in enumerate(gather_rel(enc_o))]
    lat_cols = lax.dynamic_slice_in_dim(latents(rows), rank * cols, cols, 1).astype(f32)
    z_cols = (
        lat_cols + mm(jnp.concatenate(enc_all, 1), jnp.concatenate(w_rel, 0))
    ).astype(bf16)
    z_cols = lax.ppermute(z_cols, "section", [(0, 1)])
    z_blocks = [jnp.concatenate(rows_of(j, t), 0) for j, t in enumerate(gather_rel(z_cols))]
    z = absolute(z_blocks, 1)
    up_o = mm_nt(ups, w_row).astype(bf16)

    def decoder():
        return kernel_call(
            decoder_body,
            [z, gains, w_h, projected, up_o],
            [
                shape(count, MW), shape(count, 3 * MW), shape(lat, 2 * MW),
                shape(lat, width), shape(lat, 1, f32), shape(lat, width),
            ],
            8 * lat * width * MW + 12 * count * (lat + 128) * MW,
            [pltpu.VMEM((lat, 2 * MW), bf16), pltpu.VMEM((lat, 2 * MW), f32)],
        )

    dec_o, d_proj, d_kvz, nz, z_scale, d_nz = lax.cond(
        jnp.logical_not(is_encoder),
        decoder,
        lambda: (
            jnp.zeros((count, MW), bf16), jnp.zeros((count, 3 * MW), bf16),
            jnp.zeros((lat, 2 * MW), bf16), jnp.zeros((lat, width), bf16),
            jnp.zeros((lat, 1), f32), jnp.zeros((lat, width), bf16),
        ),
    )
    z_scale = z_scale[:half]
    d_nz = sum_rel(*[d_nz[j * half : (j + 1) * half] for j in range(4)]).astype(bf16)
    d_z, z_gain = norm_back(z[:half], z_scale, gain_row, d_nz)
    z_gain = jnp.where(is_encoder, 0.0, z_gain)
    d_z = lax.ppermute(d_z.astype(bf16), "section", [(1, 0)])
    d_z_all = jnp.concatenate(gather_rel(d_z), 0)

    dec_all = [jnp.concatenate(rows_of(j, t), 0) for j, t in enumerate(gather_rel(dec_o))]

    normed_t = normed.T

    def encoder_back():
        return kernel_call(
            encoder_back_body,
            [d_z_all, w_row, projected, normed_t],
            [shape(count, 3 * MW), shape(width, 3 * MW)],
            2 * lat * width * MW + 10 * lat * count * MW + 6 * width * count * MW,
            [pltpu.VMEM((lat, MW), bf16)],
        )

    def decoder_back():
        part = mm(normed_t, d_proj)
        part = part.at[:, MW:].add(mm_tn(nz, d_kvz))
        return d_proj, part.astype(bf16)

    d_proj, qkv_part = lax.cond(is_encoder, encoder_back, decoder_back)

    def my_cols(t):
        return lax.dynamic_slice_in_dim(t, rank * cols, cols, 1)

    out_part = lax.cond(
        is_encoder,
        lambda: mm_tn(absolute(enc_all, 1), my_cols(d_z_all)).astype(bf16),
        lambda: mm_tn(absolute(dec_all, 1), my_cols(ups)).astype(bf16),
    )
    out_sum = sum_dp(out_part).astype(bf16)
    qkv_sum = sum_dp(qkv_part).astype(bf16)
    out_total = absolute(gather_rel(out_sum), 1).astype(f32)
    qkv_blocks = jnp.stack(gather_rel(qkv_sum)).reshape(4, -1, 3, MW)
    qkv_total = jnp.stack(
        [lax.dynamic_index_in_dim(qkv_blocks, i, 0, keepdims=False) for i in order], 2
    )
    qkv_total = qkv_total.reshape(-1, 12 * MW).astype(f32)

    d_n = mm_nt(d_proj, w_h).astype(bf16)
    n = tokens.shape[0]
    d_n = sum_rel(*[d_n[j * n : (j + 1) * n] for j in range(4)]).astype(bf16)
    back, gain_part = norm_back(tokens, scale, gain_row, d_n)
    residual = jnp.where(
        is_encoder,
        jnp.pad(d_z.astype(f32), ((half, 0), (0, 0))),
        upstream.astype(f32),
    )
    token_grad = (back + residual).astype(bf16)
    gain_total = sum_everywhere(gain_part + z_gain)
    return token_grad[None, None], qkv_total[None], out_total[None], gain_total[None]


def solution(mesh):
    fine = Mesh(mesh.devices.reshape(2, 2, 2, 4, 4), ("section", "zl", "core", "y", "x"))
    in_specs = (
        P("section", DP, RENDER, None),
        P("section", DP, None),
        P("section", DP, None),
        P("section", None),
        P(DP, RENDER, None),
    )
    out_specs = (
        P("section", DP, RENDER, None),
        P("section", DP, None),
        P("section", DP, None),
        P("section", None),
    )
    return jax.shard_map(shards, mesh=fine, in_specs=in_specs, out_specs=out_specs, check_vma=False)
```

```python
import jax
import jax.numpy as jnp
from jax import lax
from jax.experimental import pallas as pl
from jax.experimental.pallas import tpu as pltpu
from jax.sharding import Mesh
from jax.sharding import PartitionSpec as P

HD = 128
MY = 2
MW = MY * HD
NORM_EPSILON = 1e-06
FACTOR = HD**-0.5
RENDER = ("zl", "core")
DP = ("y", "x")
SWAP = [(0, 1), (1, 0)]
DIAG = [(0, 3), (1, 2), (2, 1), (3, 0)]
bf16 = jnp.bfloat16
f32 = jnp.float32


def mm(left, right):
    return jnp.dot(left, right, preferred_element_type=f32)


def mm_tn(left, right):
    return lax.dot_general(left, right, (((0,), (0,)), ((), ())), preferred_element_type=f32)


def mm_nt(left, right):
    return lax.dot_general(left, right, (((1,), (1,)), ((), ())), preferred_element_type=f32)


def core_swap(t):
    return lax.ppermute(t, "core", SWAP)


def z_swap(t):
    return lax.ppermute(t, "zl", SWAP)


def gather_rel(t):
    z = z_swap(t)
    c = core_swap(t)
    return [t, c, z, core_swap(z)]


def spread_rel(b):
    return [b[0], core_swap(b[1]), z_swap(b[2]), lax.ppermute(b[3], RENDER, DIAG)]


def sum_rel(own, near):
    n = own.shape[0] // 2
    near = core_swap(near)
    far = (own[n:].astype(f32) + near[n:].astype(f32)).astype(bf16)
    return (own[:n].astype(f32) + near[:n].astype(f32) + z_swap(far).astype(f32)).astype(bf16)


def step(t, axis, k):
    return lax.ppermute(t, axis, [(i, (i + k) % 4) for i in range(4)])


def ring_gather(mine, first, second):
    t = jnp.concatenate([mine] + [step(mine, first, k) for k in (1, 2, 3)], 0)
    n = t.shape[0] // 2
    up, down = step(t, second, 1), step(t, second, -1)
    return [t, up, step(up[:n], second, 1), step(down[n:], second, -1), down]


def ring_sum(blocks, first, second):
    own, after, far, before = blocks
    n = far.shape[0] // 2
    up, down = step(far[:n], first, 1), step(far[n:], first, -1)
    after = jnp.concatenate([(after[:n].astype(f32) + up.astype(f32)).astype(bf16), after[n:]], 0)
    before = jnp.concatenate(
        [before[:n], (before[n:].astype(f32) + down.astype(f32)).astype(bf16)], 0
    )
    up, down = step(after, first, 1), step(before, first, -1)
    t = (own.astype(f32) + up.astype(f32) + down.astype(f32)).astype(bf16)
    n = t.shape[0] // 4
    parts = [t[:n]] + [step(t[k * n : (k + 1) * n], second, k) for k in (1, 2, 3)]
    return sum(p.astype(f32) for p in parts).astype(bf16)


def sum_everywhere(t):
    for axis, n in (("core", 2), ("zl", 2), ("x", 4), ("y", 4)):
        for bit in (1, 2)[: n // 2]:
            t = t + lax.ppermute(t, axis, [(i, i ^ bit) for i in range(n)])
    return t


def norm_back(values, scale, gain_row, upstream):
    wide = values.astype(f32)
    grad = upstream.astype(f32)
    scaled = grad * gain_row
    inner = jnp.sum(scaled * wide, axis=-1, keepdims=True)
    result = scale * scaled - wide * scale**3 * inner / values.shape[-1]
    return result, jnp.sum(grad * wide * scale, axis=0)


def kernel_call(body, place, inputs, outputs, flops, scratch=()):
    moved = sum(t.size * t.dtype.itemsize for t in list(inputs) + list(outputs))
    vmem = pl.BlockSpec(memory_space=pltpu.VMEM)
    return pl.pallas_call(
        body,
        out_shape=tuple(outputs),
        in_specs=[pl.BlockSpec(memory_space=pltpu.SMEM)] + [vmem] * len(inputs),
        out_specs=(vmem,) * len(outputs),
        scratch_shapes=scratch,
        compiler_params=pltpu.CompilerParams(vmem_limit_bytes=48 * 2**20),
        cost_estimate=pl.CostEstimate(flops=flops, bytes_accessed=moved, transcendentals=0),
    )(place, *inputs)


def shape(rows, cols, dtype=bf16):
    return jax.ShapeDtypeStruct((rows, cols), dtype)


def block(i, n):
    return pl.ds(pl.multiple_of(i * n, n), n)


def head(part, h):
    at = part * MW + h * HD
    return slice(at, at + HD)


def lay_out(dst, blocks, rank, permuted):
    wide = blocks[0].shape[1]
    for j, b in enumerate(blocks):
        n = b.shape[0] // 4
        for i in range(4):
            at = (i ^ j if permuted else i) * n
            dst[i * n : (i + 1) * n, block(rank ^ j, wide)] = b[at : at + n, :]


def norm_body(place, gain, t0, t1, t2, t3, normed, normed_t, scales):
    n = t0.shape[0]
    for j, t in enumerate((t0, t1, t2, t3)):
        wide = t[...].astype(f32)
        scale = lax.rsqrt(jnp.mean(wide * wide, axis=-1, keepdims=True) + NORM_EPSILON)
        out = (wide * scale * gain[...]).astype(bf16)
        normed[j * n : (j + 1) * n, :] = out
        normed_t[:, j * n : (j + 1) * n] = out.T
        if j == 0:
            scales[...] = scale


def project_body(place, normed, *refs):
    y, x = place[0], place[1]
    w, out = refs[10:]
    n, wide = refs[0].shape[0] // 4, refs[0].shape[1]
    for s in range(2):
        t, up, far_up, far_down, down = refs[5 * s : 5 * s + 5]
        for k in range(4):
            for m in range(4):
                if k == 2:
                    src, at = (far_up, m) if m < 2 else (far_down, m - 2)
                else:
                    src, at = (t, up, None, down)[k], m
                dy, dx = (k, m) if s == 0 else (m, k)
                to = ((y - dy) & 3) * 4 + ((x - dx) & 3)
                w[block(to, n), s * wide : (s + 1) * wide] = src[at * n : (at + 1) * n, :]
    for at in range(0, w.shape[1], 256):
        out[:, at : at + 256] = mm(normed[...], w[:, at : at + 256]).astype(bf16)


def upstream_body(place, u0, u1, u2, u3, b0, b1, b2, b3, up_o, w_row):
    lay_out(w_row, (b0, b1, b2, b3), place[2], False)
    n = u0.shape[0]
    for j, u in enumerate((u0, u1, u2, u3)):
        up_o[j * n : (j + 1) * n, :] = mm_nt(u[...], w_row[...]).astype(bf16)


def latent_rows(ref, lanes):
    half = ref.shape[0] // 8
    return jnp.concatenate(
        [ref[(2 * i + 1) * half : (2 * i + 2) * half, lanes] for i in range(4)], 0
    )


def softmax(scores):
    raised = jnp.exp(scores - jnp.max(scores, axis=-1, keepdims=True))
    return raised * (1.0 / jnp.sum(raised, axis=-1, keepdims=True))


def encoder_forward_body(place, proj, out):
    for h in range(MY):
        q = latent_rows(proj, head(0, h))
        p = softmax(mm_nt(q, proj[:, head(1, h)]) * FACTOR)
        out[:, head(0, h)] = mm(p.astype(bf16), proj[:, head(2, h)]).astype(bf16)


def latents_body(place, t0, t1, t2, t3, o0, o1, o2, o3, w_col, z, o_all):
    rank = place[2]
    lay_out(o_all, (o0, o1, o2, o3), rank, True)
    half, cols = t0.shape[0] // 2, z.shape[1]
    added = mm(o_all[...], w_col[...])
    for j, t in enumerate((t0, t1, t2, t3)):
        rows = slice(j * half, (j + 1) * half)
        z[rows, :] = (t[half:, block(rank, cols)].astype(f32) + added[rows]).astype(bf16)


def weight_parts(place, normed_t, d_proj, d_out, outs, extra):
    y, x = place[0], place[1]
    n = outs[0].shape[0] // 4
    wide = d_proj.shape[1] // 2
    m_out = n // 2
    for dy in range(4):
        for dx in range(4):
            to = ((y + dy) & 3) * 4 + ((x + dx) & 3)
            part = mm(normed_t[block(to, n), :], d_proj[...])
            if extra is not None:
                nz_t, d_kvz = extra
                more = mm(nz_t[block(to, n), :], d_kvz[...])
                part = jnp.concatenate([part[:, :MW], part[:, MW:] + more], 1)
            part = part.astype(bf16)
            for s, (k, m) in enumerate(((dy, dx), (dx, dy))):
                o = outs[4 * s + k]
                o[m * n : (m + 1) * n, :wide] = part[:, s * wide : (s + 1) * wide]
                for half in range(2):
                    at = (2 * s + half) * HD
                    o[m * n + half * m_out : m * n + (half + 1) * m_out, wide:] = d_out[
                        block(to, m_out), at : at + HD
                    ]


def encoder_back_body(place, d0, d1, d2, d3, w_row, proj, normed_t, o_all, *refs):
    d_proj, outs, (d_z, up, d_out) = refs[0], refs[1:9], refs[9:]
    lat = d_z.shape[0]
    half = lat // 4
    for j, d in enumerate((d0, d1, d2, d3)):
        d_z[j * half : (j + 1) * half, :] = d[...]
    up[...] = mm_nt(d_z[...], w_row[...]).astype(bf16)
    for h in range(MY):
        q = latent_rows(proj, head(0, h))
        k, v = proj[:, head(1, h)], proj[:, head(2, h)]
        u = up[:, head(0, h)]
        p = softmax(mm_nt(q, k) * FACTOR)
        dp = mm_nt(u, v)
        delta = jnp.sum(dp * p, axis=-1, keepdims=True)
        ds = (p * (dp - delta) * FACTOR).astype(bf16)
        dq = mm(ds, k).astype(bf16)
        for i in range(4):
            at = 2 * i * half
            d_proj[at : at + half, head(0, h)] = jnp.zeros((half, HD), bf16)
            d_proj[at + half : at + 2 * half, head(0, h)] = dq[i * half : (i + 1) * half]
        d_proj[:, head(1, h)] = mm_tn(ds, q).astype(bf16)
        d_proj[:, head(2, h)] = mm_tn(p.astype(bf16), u).astype(bf16)
    cols = d_out.shape[1]
    d_out[...] = mm_tn(o_all[...], d_z[:, block(place[2], cols)]).astype(bf16)
    weight_parts(place, normed_t, d_proj, d_out, outs, None)


def decoder_back_body(place, proj_grad, d_kvz, nz, normed_t, *refs):
    ups, os = refs[:4], refs[4:8]
    d_proj, outs, (nz_t, o_all, d_out, up) = refs[8], refs[9:17], refs[17:]
    d_proj[...] = proj_grad[...]
    for at in range(0, nz.shape[1], 512):
        nz_t[at : at + 512, :] = nz[:, at : at + 512].T
    lay_out(o_all, os, place[2], True)
    n, cols = ups[0].shape[0], d_out.shape[1]
    for j, u in enumerate(ups):
        up[j * n : (j + 1) * n, :] = u[:, block(place[2], cols)]
    d_out[...] = mm_tn(o_all[...], up[...]).astype(bf16)
    weight_parts(place, normed_t, d_proj, d_out, outs, (nz_t, d_kvz))


def decoder_body(place, gain, z0, z1, z2, z3, w, proj, up, *refs):
    out, d_proj, d_kvz, nz, scales, z_own, own, near, z, kvz, acc = refs
    lat, width = z.shape
    half = lat // 4
    lay_out(z, (z0, z1, z2, z3), place[2], True)
    z_own[...] = z[:half, :]
    for i in range(4):
        rows = slice(i * half, (i + 1) * half)
        wide = z[rows, :].astype(f32)
        scale = lax.rsqrt(jnp.mean(wide * wide, axis=-1, keepdims=True) + NORM_EPSILON)
        nz[rows, :] = (wide * scale * gain[...]).astype(bf16)
        if i == 0:
            scales[...] = scale
    kvz[...] = mm(nz[...], w[:, MW:]).astype(bf16)
    views = proj.shape[0] // 128
    for h in range(MY):
        kz, vz = kvz[:, head(0, h)], kvz[:, head(1, h)]
        for i in range(views):
            rows = slice(i * 128, (i + 1) * 128)
            q, k, v = [proj[rows, head(part, h)] for part in range(3)]
            u = up[rows, head(0, h)]
            s = mm_nt(q, kz) * FACTOR
            t = mm_nt(q, k) * FACTOR
            top = jnp.maximum(
                jnp.max(s, axis=-1, keepdims=True), jnp.max(t, axis=-1, keepdims=True)
            )
            s, t = jnp.exp(s - top), jnp.exp(t - top)
            total = jnp.sum(s, axis=-1, keepdims=True) + jnp.sum(t, axis=-1, keepdims=True)
            s, t = s * (1.0 / total), t * (1.0 / total)
            sb, tb = s.astype(bf16), t.astype(bf16)
            out[rows, head(0, h)] = (mm(sb, vz) + mm(tb, v)).astype(bf16)
            ds, dt = mm_nt(u, vz), mm_nt(u, v)
            delta = jnp.sum(ds * s, axis=-1, keepdims=True) + jnp.sum(dt * t, axis=-1, keepdims=True)
            ds = (s * (ds - delta) * FACTOR).astype(bf16)
            dt = (t * (dt - delta) * FACTOR).astype(bf16)
            d_proj[rows, head(0, h)] = (mm(ds, kz) + mm(dt, k)).astype(bf16)
            d_proj[rows, head(1, h)] = mm_tn(dt, q).astype(bf16)
            d_proj[rows, head(2, h)] = mm_tn(tb, u).astype(bf16)
            dkz, dvz = mm_tn(ds, q), mm_tn(sb, u)
            if i > 0:
                dkz, dvz = dkz + acc[:, head(0, h)], dvz + acc[:, head(1, h)]
            acc[:, head(0, h)], acc[:, head(1, h)] = dkz, dvz
    d_kvz[...] = acc[...].astype(bf16)
    sums_for_render(d_kvz, w, MW, own, near)


def sums_for_render(grads, w, first, own, near):
    n = grads.shape[0] // 4
    for at in range(0, w.shape[0], 512):
        cols = slice(at, at + 512)
        got = mm_nt(grads[...], w[cols, first:]).astype(bf16)
        for i in range(2):
            own[i * n : (i + 1) * n, cols] = got[2 * i * n : (2 * i + 1) * n]
            near[i * n : (i + 1) * n, cols] = got[(2 * i + 1) * n : (2 * i + 2) * n]


def input_grads_body(place, d_proj, w, own, near):
    sums_for_render(d_proj, w, 0, own, near)


def totals_body(place, t0, t1, t2, t3, qkv, out):
    wide = 3 * MW // 2
    half = out.shape[0]
    for j, t in enumerate((t0, t1, t2, t3)):
        rank = place[2] ^ j
        both = jnp.concatenate([t[:, :wide], t[:, wide + HD : 2 * wide + HD]], 1).astype(f32)
        for part in range(3):
            qkv[:, block(part * 4 + rank, MW)] = both[:, part * MW : (part + 1) * MW]
        for i in range(4):
            at = (i // 2) * (wide + HD) + wide
            rows = slice((i % 2) * half, (i % 2 + 1) * half)
            out[:, block(rank * 4 + i, HD)] = t[rows, at : at + HD].astype(f32)


def shards(section_tokens, w_qkv, w_out, gains, cotangent):
    tokens = section_tokens[0, 0]
    upstream = cotangent[0]
    rank = lax.axis_index("zl") * 2 + lax.axis_index("core")
    place = jnp.stack([lax.axis_index("y"), lax.axis_index("x"), rank]).astype(jnp.int32)
    is_encoder = lax.axis_index("section") == 0
    n, width = tokens.shape
    half, cols, count, lat = n // 2, width // 4, 4 * n, 2 * n

    mine = w_qkv[0].reshape(-1, 3, 4, MW)
    mine = lax.dynamic_index_in_dim(mine, rank, 2, keepdims=False).reshape(-1, 3 * MW)
    wide = 3 * MW // 2
    w_parts = ring_gather(mine[:, :wide], "x", "y") + ring_gather(mine[:, wide:], "y", "x")
    out_mine = lax.dynamic_slice_in_dim(w_out[0], rank * cols, cols, 1)
    w_col = lax.all_gather(out_mine, DP, axis=0, tiled=True)

    rows = gather_rel(tokens)
    normed, normed_t, scale = kernel_call(
        norm_body, place, [gains, *rows],
        [shape(count, width), shape(width, count), shape(n, 1, f32)], 8 * count * width,
    )
    w_h, projected = kernel_call(
        project_body, place, [normed, *w_parts],
        [shape(width, 3 * MW), shape(count, 3 * MW)], 6 * count * width * MW,
    )
    enc_o = lax.cond(
        is_encoder,
        lambda: kernel_call(
            encoder_forward_body, place, [projected], [shape(lat, MW)], 4 * lat * count * MW
        )[0],
        lambda: jnp.zeros((lat, MW), bf16),
    )
    z_cols, enc_all = kernel_call(
        latents_body, place, [*rows, *gather_rel(enc_o), w_col],
        [shape(lat, cols), shape(lat, 4 * MW)], 8 * lat * cols * MW,
    )
    z_blocks = gather_rel(lax.ppermute(z_cols, "section", [(0, 1)]))

    ups = gather_rel(upstream)
    w_rel = [lax.dynamic_slice_in_dim(w_col, (rank ^ j) * MW, MW, 0) for j in range(4)]
    up_o, w_row = kernel_call(
        upstream_body, place, [*ups, *spread_rel(w_rel)],
        [shape(count, MW), shape(MW, width)], 2 * count * width * MW,
    )
    decoder_shapes = [
        shape(count, MW), shape(count, 3 * MW), shape(lat, 2 * MW), shape(lat, width),
        shape(half, 1, f32), shape(half, width), shape(2 * half, width), shape(2 * half, width),
    ]
    dec_o, d_proj, d_kvz, nz, z_scale, z_own, own, near = lax.cond(
        is_encoder,
        lambda: tuple(jnp.zeros(s.shape, s.dtype) for s in decoder_shapes),
        lambda: tuple(kernel_call(
            decoder_body, place, [gains, *z_blocks, w_h, projected, up_o], decoder_shapes,
            8 * lat * width * MW + 12 * count * (lat + 128) * MW,
            [pltpu.VMEM((lat, width), bf16), pltpu.VMEM((lat, 2 * MW), bf16),
             pltpu.VMEM((lat, 2 * MW), f32)],
        )),
    )
    d_z, z_gain = norm_back(z_own, z_scale, gains[0], sum_rel(own, near))
    z_gain = jnp.where(is_encoder, 0.0, z_gain)
    d_z = lax.ppermute(d_z.astype(bf16), "section", [(1, 0)])
    d_z_blocks = gather_rel(d_z)
    dec_blocks = gather_rel(dec_o)

    back_shapes = [shape(count, 3 * MW)] + [shape(4 * n, wide + HD)] * 8
    back_flops = 6 * width * count * MW + 8 * lat * cols * MW
    d_proj, *parts = lax.cond(
        is_encoder,
        lambda: tuple(kernel_call(
            encoder_back_body, place, [*d_z_blocks, w_row, projected, normed_t, enc_all],
            back_shapes, back_flops + 2 * lat * width * MW + 10 * lat * count * MW,
            [pltpu.VMEM((lat, width), bf16), pltpu.VMEM((lat, MW), bf16),
             pltpu.VMEM((4 * MW, cols), bf16)],
        )),
        lambda: tuple(kernel_call(
            decoder_back_body, place, [d_proj, d_kvz, nz, normed_t, *ups, *dec_blocks],
            back_shapes, back_flops + 4 * lat * width * MW,
            [pltpu.VMEM((width, lat), bf16), pltpu.VMEM((count, 4 * MW), bf16),
             pltpu.VMEM((4 * MW, cols), bf16), pltpu.VMEM((count, cols), bf16)],
        )),
    )
    sums = jnp.concatenate(
        [ring_sum(parts[:4], "y", "x"), ring_sum(parts[4:], "x", "y")], 1
    )
    qkv_total, out_total = kernel_call(
        totals_body, place, gather_rel(sums),
        [shape(n, 12 * MW, f32), shape(half, width, f32)], n * width,
    )

    own, near = kernel_call(
        input_grads_body, place, [d_proj, w_h], [shape(2 * n, width)] * 2,
        6 * count * width * MW,
    )
    back, gain_part = norm_back(tokens, scale, gains[0], sum_rel(own, near))
    residual = jnp.where(
        is_encoder,
        jnp.pad(d_z.astype(f32), ((half, 0), (0, 0))),
        upstream.astype(f32),
    )
    token_grad = (back + residual).astype(bf16)
    gain_total = sum_everywhere(gain_part + z_gain)
    return token_grad[None, None], qkv_total[None], out_total[None], gain_total[None]


def solution(mesh):
    fine = Mesh(mesh.devices.reshape(2, 2, 2, 4, 4), ("section", "zl", "core", "y", "x"))
    in_specs = (
        P("section", DP, RENDER, None),
        P("section", DP, None),
        P("section", DP, None),
        P("section", None),
        P(DP, RENDER, None),
    )
    out_specs = (
        P("section", DP, RENDER, None),
        P("section", DP, None),
        P("section", DP, None),
        P("section", None),
    )
    return jax.shard_map(shards, mesh=fine, in_specs=in_specs, out_specs=out_specs, check_vma=False)
```

```python
import jax
import jax.numpy as jnp
from jax import lax
from jax.experimental import pallas as pl
from jax.experimental.pallas import tpu as pltpu
from jax.sharding import Mesh
from jax.sharding import PartitionSpec as P

HD = 128
MY = 2
MW = MY * HD
NORM_EPSILON = 1e-06
FACTOR = HD**-0.5
RENDER = ("zl", "core")
DP = ("y", "x")
SWAP = [(0, 1), (1, 0)]
DIAG = [(0, 3), (1, 2), (2, 1), (3, 0)]
bf16 = jnp.bfloat16
f32 = jnp.float32


def mm(left, right):
    return jnp.dot(left, right, preferred_element_type=f32)


def mm_tn(left, right):
    return lax.dot_general(left, right, (((0,), (0,)), ((), ())), preferred_element_type=f32)


def mm_nt(left, right):
    return lax.dot_general(left, right, (((1,), (1,)), ((), ())), preferred_element_type=f32)


def core_swap(t):
    return lax.ppermute(t, "core", SWAP)


def z_swap(t):
    return lax.ppermute(t, "zl", SWAP)


def gather_rel(t):
    z = z_swap(t)
    c = core_swap(t)
    return [t, c, z, core_swap(z)]


def spread_rel(b):
    return [b[0], core_swap(b[1]), z_swap(b[2]), lax.ppermute(b[3], RENDER, DIAG)]


def sum_rel(own, near):
    n = own.shape[0] // 2
    near = core_swap(near)
    far = (own[n:].astype(f32) + near[n:].astype(f32)).astype(bf16)
    return (own[:n].astype(f32) + near[:n].astype(f32) + z_swap(far).astype(f32)).astype(bf16)


def step(t, axis, k):
    return lax.ppermute(t, axis, [(i, (i + k) % 4) for i in range(4)])


def after(t, *others):
    return lax.optimization_barrier((t, *others))[0]


def gather_near(mine, axis):
    near, far, other = [step(mine, axis, k) for k in (1, 2, 3)]
    return jnp.concatenate([mine, near], 0), jnp.concatenate([far, other], 0)


def gather_far(t, axis):
    up = [step(h, axis, 1) for h in t]
    down = [step(h, axis, -1) for h in t[::-1]][::-1]
    return [*t, *up, step(up[0], axis, 1), step(down[1], axis, -1), *down]


def add(*terms):
    return sum(t.astype(f32) for t in terms).astype(bf16)


def ring_sum(blocks, first, second):
    own, after, far, before = blocks[:2], blocks[2:4], blocks[4:6], blocks[6:]
    far_up, far_down = step(far[0], first, 1), step(far[1], first, -1)
    up = [None, step(after[1], first, 1)]
    down = [step(before[0], first, -1), None]
    up[0] = step(add(after[0], far_up), first, 1)
    down[1] = step(add(before[1], far_down), first, -1)
    parts = []
    for m in range(4):
        n = own[0].shape[0] // 2
        rows = slice((m % 2) * n, (m % 2 + 1) * n)
        part = add(*[t[m // 2][rows] for t in (own, up, down)])
        parts.append(step(part, second, m) if m else part)
    return add(*parts)


def cross_section(t, source):
    pairs = [(source * 2 + i, (1 - source) * 2 + 1 - i) for i in range(2)]
    return lax.ppermute(t, ("section", "zl"), pairs)


def sum_everywhere(t):
    for axis, n in (("core", 2), ("zl", 2), ("x", 4), ("y", 4)):
        for bit in (1, 2)[: n // 2]:
            t = t + lax.ppermute(t, axis, [(i, i ^ bit) for i in range(n)])
    return t


def norm_back(values, scale, gain_row, upstream):
    wide = values.astype(f32)
    grad = upstream.astype(f32)
    scaled = grad * gain_row
    inner = jnp.sum(scaled * wide, axis=-1, keepdims=True)
    result = scale * scaled - wide * scale**3 * inner / values.shape[-1]
    return result, jnp.sum(grad * wide * scale, axis=0)


def kernel_call(body, place, inputs, outputs, flops, scratch=()):
    moved = sum(t.size * t.dtype.itemsize for t in list(inputs) + list(outputs))
    vmem = pl.BlockSpec(memory_space=pltpu.VMEM)
    return pl.pallas_call(
        body,
        out_shape=tuple(outputs),
        in_specs=[pl.BlockSpec(memory_space=pltpu.SMEM)] + [vmem] * len(inputs),
        out_specs=(vmem,) * len(outputs),
        scratch_shapes=scratch,
        compiler_params=pltpu.CompilerParams(vmem_limit_bytes=48 * 2**20),
        cost_estimate=pl.CostEstimate(flops=flops, bytes_accessed=moved, transcendentals=0),
    )(place, *inputs)


def shape(rows, cols, dtype=bf16):
    return jax.ShapeDtypeStruct((rows, cols), dtype)


def block(i, n):
    return pl.ds(pl.multiple_of(i * n, n), n)


def head(part, h):
    at = part * MW + h * HD
    return slice(at, at + HD)


def lay_out(dst, blocks, rank, permuted):
    wide = blocks[0].shape[1]
    for j, b in enumerate(blocks):
        n = b.shape[0] // 4
        lanes = slice(j * wide, (j + 1) * wide) if rank is None else block(rank ^ j, wide)
        for i in range(4):
            at = (i ^ j if permuted else i) * n
            dst[i * n : (i + 1) * n, lanes] = b[at : at + n, :]


def out_rows(to, rank):
    return ((to >> 2) ^ rank) * 4 + (to & 3)


def norm_body(place, gain, t0, t1, t2, t3, normed, normed_t, scales):
    n = t0.shape[0]
    for j, t in enumerate((t0, t1, t2, t3)):
        wide = t[...].astype(f32)
        scale = lax.rsqrt(jnp.mean(wide * wide, axis=-1, keepdims=True) + NORM_EPSILON)
        out = (wide * scale * gain[...]).astype(bf16)
        normed[j * n : (j + 1) * n, :] = out
        normed_t[:, j * n : (j + 1) * n] = out.T
        if j == 0:
            scales[...] = scale


def project_body(place, normed, *refs):
    y, x, rank = place[0], place[1], place[2]
    w, w_rel, out = refs[16:]
    n, wide = refs[0].shape[0] // 2, refs[0].shape[1] - HD
    for s in range(2):
        for k in range(4):
            for m in range(4):
                src, at = refs[8 * s + 2 * k + m // 2], m % 2
                dy, dx = (k, m) if s == 0 else (m, k)
                to = ((y - dy) & 3) * 4 + ((x - dx) & 3)
                w[block(to, n), s * wide : (s + 1) * wide] = src[at * n : (at + 1) * n, :wide]
                for i in range(2):
                    lanes = slice((2 * s + i) * HD, (2 * s + i + 1) * HD)
                    first = at * n + i * (n // 2)
                    w_rel[block(out_rows(to, rank), n // 2), lanes] = src[
                        first : first + n // 2, wide:
                    ]
    for at in range(0, w.shape[1], 256):
        out[:, at : at + 256] = mm(normed[...], w[:, at : at + 256]).astype(bf16)


def upstream_body(place, u0, u1, u2, u3, b0, b1, b2, b3, up_o, w_row):
    lay_out(w_row, (b0, b1, b2, b3), place[2], False)
    n = u0.shape[0]
    for j, u in enumerate((u0, u1, u2, u3)):
        up_o[j * n : (j + 1) * n, :] = mm_nt(u[...], w_row[...]).astype(bf16)


def latent_rows(ref, lanes):
    half = ref.shape[0] // 8
    return jnp.concatenate(
        [ref[(2 * i + 1) * half : (2 * i + 2) * half, lanes] for i in range(4)], 0
    )


def softmax(scores):
    raised = jnp.exp(scores - jnp.max(scores, axis=-1, keepdims=True))
    return raised * (1.0 / jnp.sum(raised, axis=-1, keepdims=True))


def encoder_forward_body(place, proj, out):
    for h in range(MY):
        q = latent_rows(proj, head(0, h))
        p = softmax(mm_nt(q, proj[:, head(1, h)]) * FACTOR)
        out[:, head(0, h)] = mm(p.astype(bf16), proj[:, head(2, h)]).astype(bf16)


def latents_body(place, t0, t1, t2, t3, o0, o1, o2, o3, w_rel, z, o_all):
    rank = place[2]
    lay_out(o_all, (o0, o1, o2, o3), None, True)
    half, cols = t0.shape[0] // 2, z.shape[1]
    added = mm(o_all[...], w_rel[...])
    for j, t in enumerate((t0, t1, t2, t3)):
        rows = slice(j * half, (j + 1) * half)
        z[rows, :] = (t[half:, block(rank, cols)].astype(f32) + added[rows]).astype(bf16)


def weight_parts(place, normed_t, d_proj, d_out, outs, extra):
    y, x = place[0], place[1]
    n = outs[0].shape[0] // 2
    wide = d_proj.shape[1] // 2
    m_out = n // 2
    for dy in range(4):
        for dx in range(4):
            to = ((y + dy) & 3) * 4 + ((x + dx) & 3)
            part = mm(normed_t[block(to, n), :], d_proj[...])
            if extra is not None:
                nz_t, d_kvz = extra
                more = mm(nz_t[block(to, n), :], d_kvz[...])
                part = jnp.concatenate([part[:, :MW], part[:, MW:] + more], 1)
            part = part.astype(bf16)
            for s, (k, m) in enumerate(((dy, dx), (dx, dy))):
                o, row = outs[8 * s + 2 * k + m // 2], (m % 2) * n
                o[row : row + n, :wide] = part[:, s * wide : (s + 1) * wide]
                for half in range(2):
                    at = (2 * s + half) * HD
                    o[row + half * m_out : row + (half + 1) * m_out, wide:] = d_out[
                        block(out_rows(to, place[2]), m_out), at : at + HD
                    ]


def encoder_back_body(place, d0, d1, d2, d3, w_row, proj, normed_t, o_all, *refs):
    d_proj, outs, (d_z, up, d_out) = refs[0], refs[1:17], refs[17:]
    lat = d_z.shape[0]
    half = lat // 4
    for j, d in enumerate((d0, d1, d2, d3)):
        d_z[j * half : (j + 1) * half, :] = d[...]
    up[...] = mm_nt(d_z[...], w_row[...]).astype(bf16)
    for h in range(MY):
        q = latent_rows(proj, head(0, h))
        k, v = proj[:, head(1, h)], proj[:, head(2, h)]
        u = up[:, head(0, h)]
        p = softmax(mm_nt(q, k) * FACTOR)
        dp = mm_nt(u, v)
        delta = jnp.sum(dp * p, axis=-1, keepdims=True)
        ds = (p * (dp - delta) * FACTOR).astype(bf16)
        dq = mm(ds, k).astype(bf16)
        for i in range(4):
            at = 2 * i * half
            d_proj[at : at + half, head(0, h)] = jnp.zeros((half, HD), bf16)
            d_proj[at + half : at + 2 * half, head(0, h)] = dq[i * half : (i + 1) * half]
        d_proj[:, head(1, h)] = mm_tn(ds, q).astype(bf16)
        d_proj[:, head(2, h)] = mm_tn(p.astype(bf16), u).astype(bf16)
    cols = d_out.shape[1]
    d_out[...] = mm_tn(o_all[...], d_z[:, block(place[2], cols)]).astype(bf16)
    weight_parts(place, normed_t, d_proj, d_out, outs, None)


def decoder_back_body(place, proj_grad, d_kvz, nz, normed_t, *refs):
    ups, os = refs[:4], refs[4:8]
    d_proj, outs, (nz_t, o_all, d_out, up) = refs[8], refs[9:25], refs[25:]
    d_proj[...] = proj_grad[...]
    for at in range(0, nz.shape[1], 512):
        nz_t[at : at + 512, :] = nz[:, at : at + 512].T
    lay_out(o_all, os, None, True)
    n, cols = ups[0].shape[0], d_out.shape[1]
    for j, u in enumerate(ups):
        up[j * n : (j + 1) * n, :] = u[:, block(place[2], cols)]
    d_out[...] = mm_tn(o_all[...], up[...]).astype(bf16)
    weight_parts(place, normed_t, d_proj, d_out, outs, (nz_t, d_kvz))


def decoder_body(place, gain, z0, z1, z2, z3, w, proj, up, *refs):
    out, d_proj, d_kvz, nz, scales, z_own, own, near, z, kvz, acc = refs
    lat, width = z.shape
    half = lat // 4
    lay_out(z, (z0, z1, z2, z3), place[2], True)
    z_own[...] = z[:half, :]
    for i in range(4):
        rows = slice(i * half, (i + 1) * half)
        wide = z[rows, :].astype(f32)
        scale = lax.rsqrt(jnp.mean(wide * wide, axis=-1, keepdims=True) + NORM_EPSILON)
        nz[rows, :] = (wide * scale * gain[...]).astype(bf16)
        if i == 0:
            scales[...] = scale
    kvz[...] = mm(nz[...], w[:, MW:]).astype(bf16)
    views = proj.shape[0] // 128
    for h in range(MY):
        kz, vz = kvz[:, head(0, h)], kvz[:, head(1, h)]
        for i in range(views):
            rows = slice(i * 128, (i + 1) * 128)
            q, k, v = [proj[rows, head(part, h)] for part in range(3)]
            u = up[rows, head(0, h)]
            s = mm_nt(q, kz) * FACTOR
            t = mm_nt(q, k) * FACTOR
            top = jnp.maximum(
                jnp.max(s, axis=-1, keepdims=True), jnp.max(t, axis=-1, keepdims=True)
            )
            s, t = jnp.exp(s - top), jnp.exp(t - top)
            total = jnp.sum(s, axis=-1, keepdims=True) + jnp.sum(t, axis=-1, keepdims=True)
            s, t = s * (1.0 / total), t * (1.0 / total)
            sb, tb = s.astype(bf16), t.astype(bf16)
            out[rows, head(0, h)] = (mm(sb, vz) + mm(tb, v)).astype(bf16)
            ds, dt = mm_nt(u, vz), mm_nt(u, v)
            delta = jnp.sum(ds * s, axis=-1, keepdims=True) + jnp.sum(dt * t, axis=-1, keepdims=True)
            ds = (s * (ds - delta) * FACTOR).astype(bf16)
            dt = (t * (dt - delta) * FACTOR).astype(bf16)
            d_proj[rows, head(0, h)] = (mm(ds, kz) + mm(dt, k)).astype(bf16)
            d_proj[rows, head(1, h)] = mm_tn(dt, q).astype(bf16)
            d_proj[rows, head(2, h)] = mm_tn(tb, u).astype(bf16)
            dkz, dvz = mm_tn(ds, q), mm_tn(sb, u)
            if i > 0:
                dkz, dvz = dkz + acc[:, head(0, h)], dvz + acc[:, head(1, h)]
            acc[:, head(0, h)], acc[:, head(1, h)] = dkz, dvz
    d_kvz[...] = acc[...].astype(bf16)
    sums_for_render(d_kvz, w, MW, own, near)


def sums_for_render(grads, w, first, own, near):
    n = grads.shape[0] // 4
    for at in range(0, w.shape[0], 512):
        cols = slice(at, at + 512)
        got = mm_nt(grads[...], w[cols, first:]).astype(bf16)
        for i in range(2):
            own[i * n : (i + 1) * n, cols] = got[2 * i * n : (2 * i + 1) * n]
            near[i * n : (i + 1) * n, cols] = got[(2 * i + 1) * n : (2 * i + 2) * n]


def input_grads_body(place, d_proj, w, own, near):
    sums_for_render(d_proj, w, 0, own, near)


def totals_body(place, t0, t1, t2, t3, qkv, out):
    wide = 3 * MW // 2
    half = out.shape[0]
    for j, t in enumerate((t0, t1, t2, t3)):
        rank = place[2] ^ j
        both = jnp.concatenate([t[:, :wide], t[:, wide + HD : 2 * wide + HD]], 1).astype(f32)
        for part in range(3):
            qkv[:, block(part * 4 + rank, MW)] = both[:, part * MW : (part + 1) * MW]
        for i in range(4):
            at = (i // 2) * (wide + HD) + wide
            rows = slice((i % 2) * half, (i % 2 + 1) * half)
            out[:, block(rank * 4 + i, HD)] = t[rows, at : at + HD].astype(f32)


def shards(section_tokens, w_qkv, w_out, gains, cotangent):
    tokens = section_tokens[0, 0]
    upstream = cotangent[0]
    rank = lax.axis_index("zl") * 2 + lax.axis_index("core")
    place = jnp.stack([lax.axis_index("y"), lax.axis_index("x"), rank]).astype(jnp.int32)
    is_encoder = lax.axis_index("section") == 0
    n, width = tokens.shape
    half, cols, count, lat = n // 2, width // 4, 4 * n, 2 * n

    mine = w_qkv[0].reshape(-1, 3, 4, MW)
    mine = lax.dynamic_index_in_dim(mine, rank, 2, keepdims=False).reshape(-1, 3 * MW)
    wide = 3 * MW // 2
    out_mine = lax.dynamic_slice_in_dim(w_out[0], rank * cols, cols, 1)

    def packed(s):
        lanes = [out_mine[:, (2 * s + i) * HD : (2 * s + i + 1) * HD] for i in range(2)]
        return jnp.concatenate(
            [mine[:, s * wide : (s + 1) * wide], jnp.concatenate(lanes, 0)], 1
        )

    w_x, w_y = gather_near(packed(0), "x"), gather_near(packed(1), "y")
    w_x, w_y, tokens_sent = lax.optimization_barrier((w_x, w_y, tokens))
    w_parts = gather_far(w_x, "y") + gather_far(w_y, "x")
    rows = gather_rel(tokens_sent)
    normed, normed_t, scale = kernel_call(
        norm_body, place, [gains, *rows],
        [shape(count, width), shape(width, count), shape(n, 1, f32)], 8 * count * width,
    )
    ups = gather_rel(after(upstream, rows[2]))
    w_h, w_rel, projected = kernel_call(
        project_body, place, [normed, *w_parts],
        [shape(width, 3 * MW), shape(4 * MW, cols), shape(count, 3 * MW)],
        6 * count * width * MW,
    )
    w_row_blocks = spread_rel([w_rel[j * MW : (j + 1) * MW] for j in range(4)])
    enc_o = lax.cond(
        is_encoder,
        lambda: kernel_call(
            encoder_forward_body, place, [projected], [shape(lat, MW)], 4 * lat * count * MW
        )[0],
        lambda: jnp.zeros((lat, MW), bf16),
    )
    enc_blocks, w_row_blocks, ups = lax.optimization_barrier(
        (gather_rel(enc_o), w_row_blocks, ups)
    )
    z_cols, enc_all = kernel_call(
        latents_body, place, [*rows, *enc_blocks, w_rel],
        [shape(lat, cols), shape(lat, 4 * MW)], 8 * lat * cols * MW,
    )
    z_blocks = gather_rel(cross_section(z_cols, 0))
    z_blocks = z_blocks[2:] + z_blocks[:2]

    up_o, w_row = kernel_call(
        upstream_body, place, [*ups, *w_row_blocks],
        [shape(count, MW), shape(MW, width)], 2 * count * width * MW,
    )
    decoder_shapes = [
        shape(count, MW), shape(count, 3 * MW), shape(lat, 2 * MW), shape(lat, width),
        shape(half, 1, f32), shape(half, width), shape(2 * half, width), shape(2 * half, width),
    ]
    dec_o, d_proj, d_kvz, nz, z_scale, z_own, own, near = lax.cond(
        is_encoder,
        lambda: tuple(jnp.zeros(s.shape, s.dtype) for s in decoder_shapes),
        lambda: tuple(kernel_call(
            decoder_body, place, [gains, *z_blocks, w_h, projected, up_o], decoder_shapes,
            8 * lat * width * MW + 12 * count * (lat + 128) * MW,
            [pltpu.VMEM((lat, width), bf16), pltpu.VMEM((lat, 2 * MW), bf16),
             pltpu.VMEM((lat, 2 * MW), f32)],
        )),
    )
    d_nz = sum_rel(own, near)
    d_z, z_gain = norm_back(z_own, z_scale, gains[0], d_nz)
    dec_blocks = gather_rel(after(dec_o, d_nz))
    z_gain = jnp.where(is_encoder, 0.0, z_gain)
    d_z = cross_section(d_z.astype(bf16), 1)
    d_z_blocks = gather_rel(after(d_z, *dec_blocks))
    d_z_blocks = d_z_blocks[2:] + d_z_blocks[:2]
    d_z = d_z_blocks[0]

    back_shapes = [shape(count, 3 * MW)] + [shape(2 * n, wide + HD)] * 16
    back_flops = 6 * width * count * MW + 8 * lat * cols * MW
    d_proj, *parts = lax.cond(
        is_encoder,
        lambda: tuple(kernel_call(
            encoder_back_body, place, [*d_z_blocks, w_row, projected, normed_t, enc_all],
            back_shapes, back_flops + 2 * lat * width * MW + 10 * lat * count * MW,
            [pltpu.VMEM((lat, width), bf16), pltpu.VMEM((lat, MW), bf16),
             pltpu.VMEM((4 * MW, cols), bf16)],
        )),
        lambda: tuple(kernel_call(
            decoder_back_body, place, [d_proj, d_kvz, nz, normed_t, *ups, *dec_blocks],
            back_shapes, back_flops + 4 * lat * width * MW,
            [pltpu.VMEM((width, lat), bf16), pltpu.VMEM((count, 4 * MW), bf16),
             pltpu.VMEM((4 * MW, cols), bf16), pltpu.VMEM((count, cols), bf16)],
        )),
    )
    sums = jnp.concatenate(
        [ring_sum(parts[:8], "y", "x"), ring_sum(parts[8:], "x", "y")], 1
    )
    qkv_total, out_total = kernel_call(
        totals_body, place, gather_rel(sums),
        [shape(n, 12 * MW, f32), shape(half, width, f32)], n * width,
    )

    own, near = kernel_call(
        input_grads_body, place, [d_proj, w_h], [shape(2 * n, width)] * 2,
        6 * count * width * MW,
    )
    back, gain_part = norm_back(tokens, scale, gains[0], sum_rel(own, near))
    residual = jnp.where(
        is_encoder,
        jnp.pad(d_z.astype(f32), ((half, 0), (0, 0))),
        upstream.astype(f32),
    )
    token_grad = (back + residual).astype(bf16)
    gain_total = sum_everywhere(gain_part + z_gain)
    return token_grad[None, None], qkv_total[None], out_total[None], gain_total[None]


def solution(mesh):
    fine = Mesh(mesh.devices.reshape(2, 2, 2, 4, 4), ("section", "zl", "core", "y", "x"))
    in_specs = (
        P("section", DP, RENDER, None),
        P("section", DP, None),
        P("section", DP, None),
        P("section", None),
        P(DP, RENDER, None),
    )
    out_specs = (
        P("section", DP, RENDER, None),
        P("section", DP, None),
        P("section", DP, None),
        P("section", None),
    )
    return jax.shard_map(shards, mesh=fine, in_specs=in_specs, out_specs=out_specs, check_vma=False)
```

```python
import math

import jax
import jax.numpy as jnp
from jax import lax
from jax.experimental import pallas as pl
from jax.experimental.pallas import tpu as pltpu
from jax.sharding import Mesh
from jax.sharding import PartitionSpec as P

HD = 128
MY = 2
MW = MY * HD
NORM_EPSILON = 1e-06
FACTOR = HD**-0.5
RENDER = ("zl", "core")
DP = ("y", "x")
SWAP = [(0, 1), (1, 0)]
DIAG = [(0, 3), (1, 2), (2, 1), (3, 0)]
bf16 = jnp.bfloat16
f32 = jnp.float32


def mm(left, right):
    return jnp.dot(left, right, preferred_element_type=f32)


def mm_tn(left, right):
    return lax.dot_general(left, right, (((0,), (0,)), ((), ())), preferred_element_type=f32)


def mm_nt(left, right):
    return lax.dot_general(left, right, (((1,), (1,)), ((), ())), preferred_element_type=f32)


def core_swap(t):
    return lax.ppermute(t, "core", SWAP)


def z_swap(t):
    return lax.ppermute(t, "zl", SWAP)


def gather_rel(t):
    z = z_swap(t)
    c = core_swap(t)
    return [t, c, z, core_swap(z)]


def spread_rel(b):
    return [b[0], core_swap(b[1]), z_swap(b[2]), lax.ppermute(b[3], RENDER, DIAG)]


def sum_rel(own, near):
    n = own.shape[0] // 2
    near = core_swap(near)
    far = (own[n:].astype(f32) + near[n:].astype(f32)).astype(bf16)
    return (own[:n].astype(f32) + near[:n].astype(f32) + z_swap(far).astype(f32)).astype(bf16)


def step(t, stage, k):
    pairs = []
    for core in range(2):
        for y in range(4):
            for x in range(4):
                to = (y, (x + k) % 4) if core == stage else ((y + k) % 4, x)
                pairs.append((core * 16 + y * 4 + x, core * 16 + to[0] * 4 + to[1]))
    return lax.ppermute(t, ("core", "y", "x"), pairs)


def after(t, *others):
    return lax.optimization_barrier((t, *others))[0]


def gather_near(mine):
    near, far, other = [step(mine, 0, k) for k in (1, 2, 3)]
    return jnp.concatenate([mine, near], 0), jnp.concatenate([far, other], 0)


def gather_far(t):
    up = [step(h, 1, 1) for h in t]
    down = [step(h, 1, -1) for h in t[::-1]][::-1]
    return [*t, *up, step(up[0], 1, 1), step(down[1], 1, -1), *down]


def add(*terms):
    return sum(t.astype(f32) for t in terms).astype(bf16)


def ring_sum(blocks):
    own, after, far, before = blocks[:2], blocks[2:4], blocks[4:6], blocks[6:]
    far_up, far_down = step(far[0], 1, 1), step(far[1], 1, -1)
    up = [None, step(after[1], 1, 1)]
    down = [step(before[0], 1, -1), None]
    up[0] = step(add(after[0], far_up), 1, 1)
    down[1] = step(add(before[1], far_down), 1, -1)
    parts = []
    for m in range(4):
        n = own[0].shape[0] // 2
        rows = slice((m % 2) * n, (m % 2 + 1) * n)
        part = add(*[t[m // 2][rows] for t in (own, up, down)])
        parts.append(step(part, 0, m) if m else part)
    return add(*parts)


def cross_section(t, source):
    pairs = [(source * 2 + i, (1 - source) * 2 + 1 - i) for i in range(2)]
    return lax.ppermute(t, ("section", "zl"), pairs)


def sum_everywhere(t):
    for axis, n in (("core", 2), ("zl", 2), ("x", 4), ("y", 4)):
        for bit in (1, 2)[: n // 2]:
            t = t + lax.ppermute(t, axis, [(i, i ^ bit) for i in range(n)])
    return t


def norm_back(values, scale, gain_row, upstream):
    wide = values.astype(f32)
    grad = upstream.astype(f32)
    scaled = grad * gain_row
    inner = jnp.sum(scaled * wide, axis=-1, keepdims=True)
    result = scale * scaled - wide * scale**3 * inner / values.shape[-1]
    return result, jnp.sum(grad * wide * scale, axis=0)


def kernel_call(body, place, inputs, outputs, flops, scratch=()):
    moved = sum(t.size * t.dtype.itemsize for t in list(inputs) + list(outputs))
    vmem = pl.BlockSpec(memory_space=pltpu.VMEM)
    held = moved + sum(math.prod(t.shape) * 4 for t in scratch)
    return pl.pallas_call(
        body,
        out_shape=tuple(outputs),
        in_specs=[pl.BlockSpec(memory_space=pltpu.SMEM)] + [vmem] * len(inputs),
        out_specs=(vmem,) * len(outputs),
        scratch_shapes=scratch,
        compiler_params=pltpu.CompilerParams(vmem_limit_bytes=held + 6 * 2**20),
        cost_estimate=pl.CostEstimate(flops=flops, bytes_accessed=moved, transcendentals=0),
    )(place, *inputs)


def shape(rows, cols, dtype=bf16):
    return jax.ShapeDtypeStruct((rows, cols), dtype)


def block(i, n):
    return pl.ds(pl.multiple_of(i * n, n), n)


def head(part, h):
    at = part * MW + h * HD
    return slice(at, at + HD)


def lay_out(dst, blocks, rank, permuted):
    wide = blocks[0].shape[1]
    for j, b in enumerate(blocks):
        n = b.shape[0] // 4
        lanes = slice(j * wide, (j + 1) * wide) if rank is None else block(rank ^ j, wide)
        for i in range(4):
            at = (i ^ j if permuted else i) * n
            dst[i * n : (i + 1) * n, lanes] = b[at : at + n, :]


def out_rows(to, rank):
    return ((to >> 2) ^ rank) * 4 + (to & 3)


def norm_body(place, gain, t0, t1, t2, t3, normed, normed_t, scales):
    n = t0.shape[0]
    for j, t in enumerate((t0, t1, t2, t3)):
        wide = t[...].astype(f32)
        scale = lax.rsqrt(jnp.mean(wide * wide, axis=-1, keepdims=True) + NORM_EPSILON)
        out = (wide * scale * gain[...]).astype(bf16)
        normed[j * n : (j + 1) * n, :] = out
        normed_t[:, j * n : (j + 1) * n] = out.T
        if j == 0:
            scales[...] = scale


def holder(place, k, m, sign):
    y, x, first = place[0], place[1], place[2] & 1
    dy, dx = jnp.where(first == 0, k, m), jnp.where(first == 0, m, k)
    return ((y + sign * dy) & 3) * 4 + ((x + sign * dx) & 3)


def project_body(place, normed, *refs):
    w, w_rel, out = refs[8:]
    n, wide = refs[0].shape[0] // 2, w.shape[1]
    for k in range(4):
        for m in range(4):
            src, row = refs[2 * k + m // 2], (m % 2) * n
            to = holder(place, k, m, -1)
            w[block(to, n), :] = src[row : row + n, :wide]
            for i in range(2):
                w_rel[block(out_rows(to, place[2]), n // 2), i * MW : (i + 1) * MW] = src[
                    row + i * (n // 2) : row + (i + 1) * (n // 2), wide:
                ]
    for at in range(0, w.shape[1], 256):
        out[:, at : at + 256] = mm(normed[...], w[:, at : at + 256]).astype(bf16)


def upstream_body(place, u0, u1, u2, u3, b0, b1, b2, b3, up_o, w_row):
    lay_out(w_row, (b0, b1, b2, b3), place[2], False)
    n = u0.shape[0]
    for j, u in enumerate((u0, u1, u2, u3)):
        up_o[j * n : (j + 1) * n, :] = mm_nt(u[...], w_row[...]).astype(bf16)


def latent_rows(ref, lanes):
    half = ref.shape[0] // 8
    return jnp.concatenate(
        [ref[(2 * i + 1) * half : (2 * i + 2) * half, lanes] for i in range(4)], 0
    )


def softmax(scores):
    raised = jnp.exp(scores - jnp.max(scores, axis=-1, keepdims=True))
    return raised * (1.0 / jnp.sum(raised, axis=-1, keepdims=True))


def encoder_forward_body(place, proj, out):
    for h in range(MY):
        q = latent_rows(proj, head(0, h))
        p = softmax(mm_nt(q, proj[:, head(1, h)]) * FACTOR)
        out[:, head(0, h)] = mm(p.astype(bf16), proj[:, head(2, h)]).astype(bf16)


def latents_body(place, t0, t1, t2, t3, o0, o1, o2, o3, w_rel, z, o_all):
    rank = place[2]
    lay_out(o_all, (o0, o1, o2, o3), None, True)
    half, cols = t0.shape[0] // 2, z.shape[1]
    added = mm(o_all[...], w_rel[...])
    for j, t in enumerate((t0, t1, t2, t3)):
        rows = slice(j * half, (j + 1) * half)
        z[rows, :] = (t[half:, block(rank, cols)].astype(f32) + added[rows]).astype(bf16)


def weight_parts(place, normed_t, d_proj, d_out, outs, extra):
    n = outs[0].shape[0] // 2
    wide, m_out = d_proj.shape[1], n // 2
    for k in range(4):
        for m in range(4):
            to = holder(place, k, m, 1)
            part = mm(normed_t[block(to, n), :], d_proj[...])
            o, row = outs[2 * k + m // 2], (m % 2) * n
            if extra is not None:
                nz_t, d_kvz = extra
                more = mm(nz_t[block(to, n), :], d_kvz[...])
                part = jnp.concatenate([part[:, :MW], part[:, MW:] + more], 1)
            o[row : row + n, :wide] = part.astype(bf16)
            for i in range(2):
                o[row + i * m_out : row + (i + 1) * m_out, wide:] = d_out[
                    block(out_rows(to, place[2]), m_out), i * MW : (i + 1) * MW
                ]


def encoder_back_body(place, d0, d1, d2, d3, w_row, proj, normed_t, o_all, *refs):
    d_proj, outs, (d_z, up, d_out) = refs[0], refs[1:9], refs[9:]
    lat = d_z.shape[0]
    half = lat // 4
    for j, d in enumerate((d0, d1, d2, d3)):
        d_z[j * half : (j + 1) * half, :] = d[...]
    up[...] = mm_nt(d_z[...], w_row[...]).astype(bf16)
    for h in range(MY):
        q = latent_rows(proj, head(0, h))
        k, v = proj[:, head(1, h)], proj[:, head(2, h)]
        u = up[:, head(0, h)]
        p = softmax(mm_nt(q, k) * FACTOR)
        dp = mm_nt(u, v)
        delta = jnp.sum(dp * p, axis=-1, keepdims=True)
        ds = (p * (dp - delta) * FACTOR).astype(bf16)
        dq = mm(ds, k).astype(bf16)
        for i in range(4):
            at = 2 * i * half
            d_proj[at : at + half, head(0, h)] = jnp.zeros((half, HD), bf16)
            d_proj[at + half : at + 2 * half, head(0, h)] = dq[i * half : (i + 1) * half]
        d_proj[:, head(1, h)] = mm_tn(ds, q).astype(bf16)
        d_proj[:, head(2, h)] = mm_tn(p.astype(bf16), u).astype(bf16)
    cols = d_out.shape[1]
    d_out[...] = mm_tn(o_all[...], d_z[:, block(place[2], cols)]).astype(bf16)
    weight_parts(place, normed_t, d_proj, d_out, outs, None)


def decoder_back_body(place, proj_grad, d_kvz, nz, normed_t, *refs):
    ups, os = refs[:4], refs[4:8]
    d_proj, outs, (nz_t, o_all, d_out, up) = refs[8], refs[9:17], refs[17:]
    d_proj[...] = proj_grad[...]
    for at in range(0, nz.shape[1], 512):
        nz_t[at : at + 512, :] = nz[:, at : at + 512].T
    lay_out(o_all, os, None, True)
    n, cols = ups[0].shape[0], d_out.shape[1]
    for j, u in enumerate(ups):
        up[j * n : (j + 1) * n, :] = u[:, block(place[2], cols)]
    d_out[...] = mm_tn(o_all[...], up[...]).astype(bf16)
    weight_parts(place, normed_t, d_proj, d_out, outs, (nz_t, d_kvz))


def decoder_body(place, gain, z0, z1, z2, z3, w, proj, up, *refs):
    out, d_proj, d_kvz, nz, scales, z_own, own, near, z, kvz, acc = refs
    lat, width = z.shape
    half = lat // 4
    lay_out(z, (z0, z1, z2, z3), place[2], True)
    z_own[...] = z[:half, :]
    for i in range(4):
        rows = slice(i * half, (i + 1) * half)
        wide = z[rows, :].astype(f32)
        scale = lax.rsqrt(jnp.mean(wide * wide, axis=-1, keepdims=True) + NORM_EPSILON)
        nz[rows, :] = (wide * scale * gain[...]).astype(bf16)
        if i == 0:
            scales[...] = scale
    kvz[...] = mm(nz[...], w[:, MW:]).astype(bf16)
    views = proj.shape[0] // 128
    for h in range(MY):
        kz, vz = kvz[:, head(0, h)], kvz[:, head(1, h)]
        for i in range(views):
            rows = slice(i * 128, (i + 1) * 128)
            q, k, v = [proj[rows, head(part, h)] for part in range(3)]
            u = up[rows, head(0, h)]
            s = mm_nt(q, kz) * FACTOR
            t = mm_nt(q, k) * FACTOR
            top = jnp.maximum(
                jnp.max(s, axis=-1, keepdims=True), jnp.max(t, axis=-1, keepdims=True)
            )
            s, t = jnp.exp(s - top), jnp.exp(t - top)
            total = jnp.sum(s, axis=-1, keepdims=True) + jnp.sum(t, axis=-1, keepdims=True)
            s, t = s * (1.0 / total), t * (1.0 / total)
            sb, tb = s.astype(bf16), t.astype(bf16)
            out[rows, head(0, h)] = (mm(sb, vz) + mm(tb, v)).astype(bf16)
            ds, dt = mm_nt(u, vz), mm_nt(u, v)
            delta = jnp.sum(ds * s, axis=-1, keepdims=True) + jnp.sum(dt * t, axis=-1, keepdims=True)
            ds = (s * (ds - delta) * FACTOR).astype(bf16)
            dt = (t * (dt - delta) * FACTOR).astype(bf16)
            d_proj[rows, head(0, h)] = (mm(ds, kz) + mm(dt, k)).astype(bf16)
            d_proj[rows, head(1, h)] = mm_tn(dt, q).astype(bf16)
            d_proj[rows, head(2, h)] = mm_tn(tb, u).astype(bf16)
            dkz, dvz = mm_tn(ds, q), mm_tn(sb, u)
            if i > 0:
                dkz, dvz = dkz + acc[:, head(0, h)], dvz + acc[:, head(1, h)]
            acc[:, head(0, h)], acc[:, head(1, h)] = dkz, dvz
    d_kvz[...] = acc[...].astype(bf16)
    sums_for_render(d_kvz, w, MW, own, near)


def sums_for_render(grads, w, first, own, near):
    n = grads.shape[0] // 4
    for at in range(0, w.shape[0], 512):
        cols = slice(at, at + 512)
        got = mm_nt(grads[...], w[cols, first:]).astype(bf16)
        for i in range(2):
            own[i * n : (i + 1) * n, cols] = got[2 * i * n : (2 * i + 1) * n]
            near[i * n : (i + 1) * n, cols] = got[(2 * i + 1) * n : (2 * i + 2) * n]


def input_grads_body(place, d_proj, w, own, near):
    sums_for_render(d_proj, w, 0, own, near)


def totals_body(place, t0, t1, t2, t3, qkv, out):
    half = out.shape[0]
    for j, t in enumerate((t0, t1, t2, t3)):
        rank = place[2] ^ j
        for part in range(3):
            qkv[:, block(part * 4 + rank, MW)] = t[:, part * MW : (part + 1) * MW].astype(f32)
        for i in range(2):
            rows = slice(i * half, (i + 1) * half)
            out[:, block(rank * 2 + i, MW)] = t[rows, 3 * MW :].astype(f32)


def shards(section_tokens, w_qkv, w_out, gains, cotangent):
    tokens = section_tokens[0, 0]
    upstream = cotangent[0]
    rank = lax.axis_index("zl") * 2 + lax.axis_index("core")
    place = jnp.stack([lax.axis_index("y"), lax.axis_index("x"), rank]).astype(jnp.int32)
    is_encoder = lax.axis_index("section") == 0
    n, width = tokens.shape
    half, cols, count, lat = n // 2, width // 4, 4 * n, 2 * n

    own_cols = [
        lax.dynamic_slice_in_dim(w_qkv[0], part * 4 * MW + rank * MW, MW, 1) for part in range(3)
    ]
    own_out = [lax.dynamic_slice_in_dim(w_out[0], rank * cols + i * MW, MW, 1) for i in range(2)]
    near = gather_near(jnp.concatenate([*own_cols, jnp.concatenate(own_out, 0)], 1))
    near, tokens_sent = lax.optimization_barrier((near, tokens))
    w_parts = gather_far(near)
    rows = gather_rel(tokens_sent)
    normed, normed_t, scale = kernel_call(
        norm_body, place, [gains, *rows],
        [shape(count, width), shape(width, count), shape(n, 1, f32)], 8 * count * width,
    )
    ups = gather_rel(after(upstream, rows[2]))
    w_h, w_rel, projected = kernel_call(
        project_body, place, [normed, *w_parts],
        [shape(width, 3 * MW), shape(4 * MW, cols), shape(count, 3 * MW)],
        6 * count * width * MW,
    )
    w_row_blocks = spread_rel([w_rel[j * MW : (j + 1) * MW] for j in range(4)])
    enc_o = lax.cond(
        is_encoder,
        lambda: kernel_call(
            encoder_forward_body, place, [projected], [shape(lat, MW)], 4 * lat * count * MW
        )[0],
        lambda: jnp.zeros((lat, MW), bf16),
    )
    enc_blocks, w_row_blocks[1], ups = lax.optimization_barrier(
        (gather_rel(enc_o), w_row_blocks[1], ups)
    )
    z_cols, enc_all = kernel_call(
        latents_body, place, [*rows, *enc_blocks, w_rel],
        [shape(lat, cols), shape(lat, 4 * MW)], 8 * lat * cols * MW,
    )
    z_blocks = gather_rel(cross_section(z_cols, 0))
    z_blocks = z_blocks[2:] + z_blocks[:2]

    up_o, w_row = kernel_call(
        upstream_body, place, [*ups, *w_row_blocks],
        [shape(count, MW), shape(MW, width)], 2 * count * width * MW,
    )
    decoder_shapes = [
        shape(count, MW), shape(count, 3 * MW), shape(lat, 2 * MW), shape(lat, width),
        shape(half, 1, f32), shape(half, width), shape(2 * half, width), shape(2 * half, width),
    ]
    dec_o, d_proj, d_kvz, nz, z_scale, z_own, own, near = lax.cond(
        is_encoder,
        lambda: tuple(jnp.zeros(s.shape, s.dtype) for s in decoder_shapes),
        lambda: tuple(kernel_call(
            decoder_body, place, [gains, *z_blocks, w_h, projected, up_o], decoder_shapes,
            8 * lat * width * MW + 12 * count * (lat + 128) * MW,
            [pltpu.VMEM((lat, width), bf16), pltpu.VMEM((lat, 2 * MW), bf16),
             pltpu.VMEM((lat, 2 * MW), f32)],
        )),
    )
    d_nz = sum_rel(own, near)
    d_z, z_gain = norm_back(z_own, z_scale, gains[0], d_nz)
    d_z = d_z.astype(bf16)
    dec_blocks = gather_rel(after(dec_o, d_z))
    z_gain = jnp.where(is_encoder, 0.0, z_gain)
    d_z = cross_section(d_z, 1)
    d_z_blocks = gather_rel(after(d_z, *dec_blocks))
    d_z_blocks = d_z_blocks[2:] + d_z_blocks[:2]
    d_z = d_z_blocks[0]

    back_shapes = [shape(count, 3 * MW)] + [shape(2 * n, width // 2)] * 8
    back_flops = 6 * width * count * MW + 8 * lat * cols * MW
    d_proj, *parts = lax.cond(
        is_encoder,
        lambda: tuple(kernel_call(
            encoder_back_body, place, [*d_z_blocks, w_row, projected, normed_t, enc_all],
            back_shapes, back_flops + 2 * lat * width * MW + 10 * lat * count * MW,
            [pltpu.VMEM((lat, width), bf16), pltpu.VMEM((lat, MW), bf16),
             pltpu.VMEM((4 * MW, cols), bf16)],
        )),
        lambda: tuple(kernel_call(
            decoder_back_body, place, [d_proj, d_kvz, nz, normed_t, *ups, *dec_blocks],
            back_shapes, back_flops + 4 * lat * width * MW,
            [pltpu.VMEM((width, lat), bf16), pltpu.VMEM((count, 4 * MW), bf16),
             pltpu.VMEM((4 * MW, cols), bf16), pltpu.VMEM((count, cols), bf16)],
        )),
    )
    qkv_total, out_total = kernel_call(
        totals_body, place, gather_rel(ring_sum(parts)),
        [shape(n, 12 * MW, f32), shape(half, width, f32)], n * width,
    )

    own, near = kernel_call(
        input_grads_body, place, [d_proj, w_h], [shape(2 * n, width)] * 2,
        6 * count * width * MW,
    )
    back, gain_part = norm_back(tokens, scale, gains[0], sum_rel(own, near))
    residual = jnp.where(
        is_encoder,
        jnp.pad(d_z.astype(f32), ((half, 0), (0, 0))),
        upstream.astype(f32),
    )
    token_grad = (back + residual).astype(bf16)
    gain_total = sum_everywhere(gain_part + z_gain)
    return token_grad[None, None], qkv_total[None], out_total[None], gain_total[None]


def solution(mesh):
    fine = Mesh(mesh.devices.reshape(2, 2, 2, 4, 4), ("section", "zl", "core", "y", "x"))
    in_specs = (
        P("section", DP, RENDER, None),
        P("section", DP, None),
        P("section", DP, None),
        P("section", None),
        P(DP, RENDER, None),
    )
    out_specs = (
        P("section", DP, RENDER, None),
        P("section", DP, None),
        P("section", DP, None),
        P("section", None),
    )
    return jax.shard_map(shards, mesh=fine, in_specs=in_specs, out_specs=out_specs, check_vma=False)
```

```python
import math

import jax
import jax.numpy as jnp
from jax import lax
from jax.experimental import pallas as pl
from jax.experimental.pallas import tpu as pltpu
from jax.sharding import Mesh
from jax.sharding import PartitionSpec as P

HD = 128
MY = 2
MW = MY * HD
NORM_EPSILON = 1e-06
FACTOR = HD**-0.5
RENDER = ("zl", "core")
DP = ("y", "x")
SWAP = [(0, 1), (1, 0)]
DIAG = [(0, 3), (1, 2), (2, 1), (3, 0)]
bf16 = jnp.bfloat16
f32 = jnp.float32


def mm(left, right):
    return jnp.dot(left, right, preferred_element_type=f32)


def mm_tn(left, right):
    return lax.dot_general(left, right, (((0,), (0,)), ((), ())), preferred_element_type=f32)


def mm_nt(left, right):
    return lax.dot_general(left, right, (((1,), (1,)), ((), ())), preferred_element_type=f32)


def core_swap(t):
    return lax.ppermute(t, "core", SWAP)


def z_swap(t):
    return lax.ppermute(t, "zl", SWAP)


def gather_rel(t):
    z = z_swap(t)
    c = core_swap(t)
    return [t, c, z, core_swap(z)]


def spread_rel(b):
    return [b[0], core_swap(b[1]), z_swap(b[2]), lax.ppermute(b[3], RENDER, DIAG)]


def sum_near(own, near):
    n = own.shape[0] // 2
    near = core_swap(near)
    return own[:n].astype(f32) + near[:n].astype(f32), add(own[n:], near[n:])


def sum_far(mine, far):
    return (mine + z_swap(far).astype(f32)).astype(bf16)


def add(*terms):
    return sum(t.astype(f32) for t in terms).astype(bf16)


def step(t, stage, k):
    pairs = []
    for core in range(2):
        for y in range(4):
            for x in range(4):
                to = (y, (x + k) % 4) if core == stage else ((y + k) % 4, x)
                pairs.append((core * 16 + y * 4 + x, core * 16 + to[0] * 4 + to[1]))
    return lax.ppermute(t, ("core", "y", "x"), pairs)


def after(t, *others):
    return lax.optimization_barrier((t, *others))[0]


def gather_near(mine):
    near, far, other = [step(mine, 0, k) for k in (1, 2, 3)]
    return jnp.concatenate([mine, near], 0), jnp.concatenate([far, other], 0)


def gather_far(t):
    up = [step(h, 1, 1) for h in t]
    down = [step(h, 1, -1) for h in t[::-1]][::-1]
    return [*t, *up, step(up[0], 1, 1), step(down[1], 1, -1), *down]


def ring_sum_far(blocks):
    own, after, far, before = blocks[:2], blocks[2:4], blocks[4:6], blocks[6:]
    far_up, far_down = step(far[0], 1, 1), step(far[1], 1, -1)
    up = [None, step(after[1], 1, 1)]
    down = [step(before[0], 1, -1), None]
    up[0] = step(add(after[0], far_up), 1, 1)
    down[1] = step(add(before[1], far_down), 1, -1)
    parts = []
    for m in range(4):
        n = own[0].shape[0] // 2
        rows = slice((m % 2) * n, (m % 2 + 1) * n)
        parts.append(add(*[t[m // 2][rows] for t in (own, up, down)]))
    return parts


def ring_sum_near(parts):
    return add(parts[0], *[step(parts[m], 0, m) for m in (1, 2, 3)])


def cross_section(t, source):
    pairs = [(source * 2 + i, (1 - source) * 2 + 1 - i) for i in range(2)]
    return lax.ppermute(t, ("section", "zl"), pairs)


def sum_everywhere(t):
    for axes in (RENDER, "x", "y"):
        one, two, three = [
            lax.ppermute(t, axes, [(i, i ^ bits) for i in range(4)]) for bits in (1, 2, 3)
        ]
        t = (t + one) + (two + three)
    return t


def norm_back(values, scale, gain_row, upstream):
    wide = values.astype(f32)
    grad = upstream.astype(f32)
    scaled = grad * gain_row
    inner = jnp.sum(scaled * wide, axis=-1, keepdims=True)
    result = scale * scaled - wide * scale**3 * inner / values.shape[-1]
    return result, jnp.sum(grad * wide * scale, axis=0)


def kernel_call(body, place, inputs, outputs, flops, scratch=()):
    moved = sum(t.size * t.dtype.itemsize for t in list(inputs) + list(outputs))
    vmem = pl.BlockSpec(memory_space=pltpu.VMEM)
    held = moved + sum(math.prod(t.shape) * 4 for t in scratch)
    return pl.pallas_call(
        body,
        out_shape=tuple(outputs),
        in_specs=[pl.BlockSpec(memory_space=pltpu.SMEM)] + [vmem] * len(inputs),
        out_specs=(vmem,) * len(outputs),
        scratch_shapes=scratch,
        compiler_params=pltpu.CompilerParams(vmem_limit_bytes=held + 6 * 2**20),
        cost_estimate=pl.CostEstimate(flops=flops, bytes_accessed=moved, transcendentals=0),
    )(place, *inputs)


def shape(rows, cols, dtype=bf16):
    return jax.ShapeDtypeStruct((rows, cols), dtype)


def block(i, n):
    return pl.ds(pl.multiple_of(i * n, n), n)


def head(part, h):
    at = part * MW + h * HD
    return slice(at, at + HD)


def lay_out(dst, blocks, rank, permuted):
    wide = blocks[0].shape[1]
    for j, b in enumerate(blocks):
        n = b.shape[0] // 4
        lanes = slice(j * wide, (j + 1) * wide) if rank is None else block(rank ^ j, wide)
        for i in range(4):
            at = (i ^ j if permuted else i) * n
            dst[i * n : (i + 1) * n, lanes] = b[at : at + n, :]


def out_rows(to, rank):
    return ((to >> 2) ^ rank) * 4 + (to & 3)


def norm_body(place, gain, t0, t1, t2, t3, normed, normed_t, scales):
    n = t0.shape[0]
    for j, t in enumerate((t0, t1, t2, t3)):
        wide = t[...].astype(f32)
        scale = lax.rsqrt(jnp.mean(wide * wide, axis=-1, keepdims=True) + NORM_EPSILON)
        out = (wide * scale * gain[...]).astype(bf16)
        normed[j * n : (j + 1) * n, :] = out
        normed_t[:, j * n : (j + 1) * n] = out.T
        if j == 0:
            scales[...] = scale


def holder(place, k, m, sign):
    y, x, first = place[0], place[1], place[2] & 1
    dy, dx = jnp.where(first == 0, k, m), jnp.where(first == 0, m, k)
    return ((y + sign * dy) & 3) * 4 + ((x + sign * dx) & 3)


def project_body(place, normed, *refs):
    w, w_rel, out, enc_o = refs[8:]
    n, wide = refs[0].shape[0] // 2, w.shape[1]
    for k in range(4):
        for m in range(4):
            src, row = refs[2 * k + m // 2], (m % 2) * n
            to = holder(place, k, m, -1)
            w[block(to, n), :] = src[row : row + n, :wide]
            for i in range(2):
                w_rel[block(out_rows(to, place[2]), n // 2), i * MW : (i + 1) * MW] = src[
                    row + i * (n // 2) : row + (i + 1) * (n // 2), wide:
                ]
    for at in range(0, w.shape[1], 256):
        out[:, at : at + 256] = mm(normed[...], w[:, at : at + 256]).astype(bf16)
    for h in range(MY):
        q = latent_rows(out, head(0, h))
        p = softmax(mm_nt(q, out[:, head(1, h)]) * FACTOR)
        enc_o[:, head(0, h)] = mm(p.astype(bf16), out[:, head(2, h)]).astype(bf16)


def upstream_body(place, u0, u1, u2, u3, b0, b1, b2, b3, up_o, w_row):
    lay_out(w_row, (b0, b1, b2, b3), place[2], False)
    n = u0.shape[0]
    for j, u in enumerate((u0, u1, u2, u3)):
        up_o[j * n : (j + 1) * n, :] = mm_nt(u[...], w_row[...]).astype(bf16)


def latent_rows(ref, lanes):
    half = ref.shape[0] // 8
    return jnp.concatenate(
        [ref[(2 * i + 1) * half : (2 * i + 2) * half, lanes] for i in range(4)], 0
    )


def softmax(scores):
    raised = jnp.exp(scores - jnp.max(scores, axis=-1, keepdims=True))
    return raised * (1.0 / jnp.sum(raised, axis=-1, keepdims=True))


def latents_body(place, t0, t1, t2, t3, o0, o1, o2, o3, w_rel, z, o_all):
    rank = place[2]
    lay_out(o_all, (o0, o1, o2, o3), None, True)
    half, cols = t0.shape[0] // 2, z.shape[1]
    added = mm(o_all[...], w_rel[...])
    for j, t in enumerate((t0, t1, t2, t3)):
        rows = slice(j * half, (j + 1) * half)
        z[rows, :] = (t[half:, block(rank, cols)].astype(f32) + added[rows]).astype(bf16)


def weight_parts(place, normed_t, d_proj, d_out, outs, extra):
    n = outs[0].shape[0] // 2
    wide, m_out = d_proj.shape[1], n // 2
    for k in range(4):
        for m in range(4):
            to = holder(place, k, m, 1)
            part = mm(normed_t[block(to, n), :], d_proj[...])
            o, row = outs[2 * k + m // 2], (m % 2) * n
            if extra is not None:
                nz_t, d_kvz = extra
                more = mm(nz_t[block(to, n), :], d_kvz[...])
                part = jnp.concatenate([part[:, :MW], part[:, MW:] + more], 1)
            o[row : row + n, :wide] = part.astype(bf16)
            for i in range(2):
                o[row + i * m_out : row + (i + 1) * m_out, wide:] = d_out[
                    block(out_rows(to, place[2]), m_out), i * MW : (i + 1) * MW
                ]


def encoder_back_body(place, d0, d1, d2, d3, w_row, proj, normed_t, o_all, *refs):
    d_proj, outs, (d_z, up, d_out) = refs[0], refs[1:9], refs[9:]
    lat = d_z.shape[0]
    half = lat // 4
    for j, d in enumerate((d0, d1, d2, d3)):
        d_z[j * half : (j + 1) * half, :] = d[...]
    up[...] = mm_nt(d_z[...], w_row[...]).astype(bf16)
    for h in range(MY):
        q = latent_rows(proj, head(0, h))
        k, v = proj[:, head(1, h)], proj[:, head(2, h)]
        u = up[:, head(0, h)]
        p = softmax(mm_nt(q, k) * FACTOR)
        dp = mm_nt(u, v)
        delta = jnp.sum(dp * p, axis=-1, keepdims=True)
        ds = (p * (dp - delta) * FACTOR).astype(bf16)
        dq = mm(ds, k).astype(bf16)
        for i in range(4):
            at = 2 * i * half
            d_proj[at : at + half, head(0, h)] = jnp.zeros((half, HD), bf16)
            d_proj[at + half : at + 2 * half, head(0, h)] = dq[i * half : (i + 1) * half]
        d_proj[:, head(1, h)] = mm_tn(ds, q).astype(bf16)
        d_proj[:, head(2, h)] = mm_tn(p.astype(bf16), u).astype(bf16)
    cols = d_out.shape[1]
    d_out[...] = mm_tn(o_all[...], d_z[:, block(place[2], cols)]).astype(bf16)
    weight_parts(place, normed_t, d_proj, d_out, outs, None)


def decoder_back_body(place, proj_grad, d_kvz, nz, normed_t, *refs):
    ups, os = refs[:4], refs[4:8]
    d_proj, outs, (nz_t, o_all, d_out, up) = refs[8], refs[9:17], refs[17:]
    d_proj[...] = proj_grad[...]
    for at in range(0, nz.shape[1], 512):
        nz_t[at : at + 512, :] = nz[:, at : at + 512].T
    lay_out(o_all, os, None, True)
    n, cols = ups[0].shape[0], d_out.shape[1]
    for j, u in enumerate(ups):
        up[j * n : (j + 1) * n, :] = u[:, block(place[2], cols)]
    d_out[...] = mm_tn(o_all[...], up[...]).astype(bf16)
    weight_parts(place, normed_t, d_proj, d_out, outs, (nz_t, d_kvz))


def decoder_body(place, gain, z0, z1, z2, z3, w, proj, up, *refs):
    out, d_proj, d_kvz, nz, scales, z_own, own, near, z, kvz, acc = refs
    lat, width = z.shape
    half = lat // 4
    lay_out(z, (z0, z1, z2, z3), place[2], True)
    z_own[...] = z[:half, :]
    for i in range(4):
        rows = slice(i * half, (i + 1) * half)
        wide = z[rows, :].astype(f32)
        scale = lax.rsqrt(jnp.mean(wide * wide, axis=-1, keepdims=True) + NORM_EPSILON)
        nz[rows, :] = (wide * scale * gain[...]).astype(bf16)
        if i == 0:
            scales[...] = scale
    kvz[...] = mm(nz[...], w[:, MW:]).astype(bf16)
    views = proj.shape[0] // 128
    for h in range(MY):
        kz, vz = kvz[:, head(0, h)], kvz[:, head(1, h)]
        for i in range(views):
            rows = slice(i * 128, (i + 1) * 128)
            q, k, v = [proj[rows, head(part, h)] for part in range(3)]
            u = up[rows, head(0, h)]
            s = mm_nt(q, kz) * FACTOR
            t = mm_nt(q, k) * FACTOR
            top = jnp.maximum(
                jnp.max(s, axis=-1, keepdims=True), jnp.max(t, axis=-1, keepdims=True)
            )
            s, t = jnp.exp(s - top), jnp.exp(t - top)
            total = jnp.sum(s, axis=-1, keepdims=True) + jnp.sum(t, axis=-1, keepdims=True)
            s, t = s * (1.0 / total), t * (1.0 / total)
            sb, tb = s.astype(bf16), t.astype(bf16)
            out[rows, head(0, h)] = (mm(sb, vz) + mm(tb, v)).astype(bf16)
            ds, dt = mm_nt(u, vz), mm_nt(u, v)
            delta = jnp.sum(ds * s, axis=-1, keepdims=True) + jnp.sum(dt * t, axis=-1, keepdims=True)
            ds = (s * (ds - delta) * FACTOR).astype(bf16)
            dt = (t * (dt - delta) * FACTOR).astype(bf16)
            d_proj[rows, head(0, h)] = (mm(ds, kz) + mm(dt, k)).astype(bf16)
            d_proj[rows, head(1, h)] = mm_tn(dt, q).astype(bf16)
            d_proj[rows, head(2, h)] = mm_tn(tb, u).astype(bf16)
            dkz, dvz = mm_tn(ds, q), mm_tn(sb, u)
            if i > 0:
                dkz, dvz = dkz + acc[:, head(0, h)], dvz + acc[:, head(1, h)]
            acc[:, head(0, h)], acc[:, head(1, h)] = dkz, dvz
    d_kvz[...] = acc[...].astype(bf16)
    sums_for_render(d_kvz, w, MW, own, near)


def sums_for_render(grads, w, first, own, near):
    n = grads.shape[0] // 4
    for at in range(0, w.shape[0], 512):
        cols = slice(at, at + 512)
        got = mm_nt(grads[...], w[cols, first:]).astype(bf16)
        for i in range(2):
            own[i * n : (i + 1) * n, cols] = got[2 * i * n : (2 * i + 1) * n]
            near[i * n : (i + 1) * n, cols] = got[(2 * i + 1) * n : (2 * i + 2) * n]


def input_grads_body(place, d_proj, w, own, near):
    sums_for_render(d_proj, w, 0, own, near)


def totals_body(place, t0, t1, t2, t3, qkv, out):
    half = out.shape[0]
    for j, t in enumerate((t0, t1, t2, t3)):
        rank = place[2] ^ j
        for part in range(3):
            qkv[:, block(part * 4 + rank, MW)] = t[:, part * MW : (part + 1) * MW].astype(f32)
        for i in range(2):
            rows = slice(i * half, (i + 1) * half)
            out[:, block(rank * 2 + i, MW)] = t[rows, 3 * MW :].astype(f32)


def shards(section_tokens, w_qkv, w_out, gains, cotangent):
    tokens = section_tokens[0, 0]
    upstream = cotangent[0]
    rank = lax.axis_index("zl") * 2 + lax.axis_index("core")
    place = jnp.stack([lax.axis_index("y"), lax.axis_index("x"), rank]).astype(jnp.int32)
    is_encoder = lax.axis_index("section") == 0
    n, width = tokens.shape
    half, cols, count, lat = n // 2, width // 4, 4 * n, 2 * n

    own_cols = [
        lax.dynamic_slice_in_dim(w_qkv[0], part * 4 * MW + rank * MW, MW, 1) for part in range(3)
    ]
    own_out = [lax.dynamic_slice_in_dim(w_out[0], rank * cols + i * MW, MW, 1) for i in range(2)]
    near = gather_near(jnp.concatenate([*own_cols, jnp.concatenate(own_out, 0)], 1))
    rows = gather_rel(tokens)
    near, rows[2] = lax.optimization_barrier((near, rows[2]))
    w_parts = gather_far(near)
    normed, normed_t, scale = kernel_call(
        norm_body, place, [gains, *rows],
        [shape(count, width), shape(width, count), shape(n, 1, f32)], 8 * count * width,
    )
    ups = gather_rel(after(upstream, rows[2]))
    w_h, w_rel, projected, enc_o = kernel_call(
        project_body, place, [normed, *w_parts],
        [shape(width, 3 * MW), shape(4 * MW, cols), shape(count, 3 * MW), shape(lat, MW)],
        6 * count * width * MW + 4 * lat * count * MW,
    )
    w_row_blocks = spread_rel([w_rel[j * MW : (j + 1) * MW] for j in range(4)])
    enc_o, w_row_blocks[1] = lax.optimization_barrier((enc_o, w_row_blocks[1]))
    enc_blocks = gather_rel(enc_o)
    enc_blocks[1], ups = lax.optimization_barrier((enc_blocks[1], ups))
    z_cols, enc_all = kernel_call(
        latents_body, place, [*rows, *enc_blocks, w_rel],
        [shape(lat, cols), shape(lat, 4 * MW)], 8 * lat * cols * MW,
    )
    z_cols, w_row_blocks = lax.optimization_barrier((z_cols, w_row_blocks))
    z_blocks = gather_rel(cross_section(z_cols, 0))
    z_blocks = z_blocks[2:] + z_blocks[:2]

    up_o, w_row = kernel_call(
        upstream_body, place, [*ups, *w_row_blocks],
        [shape(count, MW), shape(MW, width)], 2 * count * width * MW,
    )
    decoder_shapes = [
        shape(count, MW), shape(count, 3 * MW), shape(lat, 2 * MW), shape(lat, width),
        shape(half, 1, f32), shape(half, width), shape(2 * half, width), shape(2 * half, width),
    ]
    dec_o, d_proj, d_kvz, nz, z_scale, z_own, own, near = lax.cond(
        is_encoder,
        lambda: tuple(jnp.zeros(s.shape, s.dtype) for s in decoder_shapes),
        lambda: tuple(kernel_call(
            decoder_body, place, [gains, *z_blocks, w_h, projected, up_o], decoder_shapes,
            8 * lat * width * MW + 12 * count * (lat + 128) * MW,
            [pltpu.VMEM((lat, width), bf16), pltpu.VMEM((lat, 2 * MW), bf16),
             pltpu.VMEM((lat, 2 * MW), f32)],
        )),
    )
    d_nz = sum_far(*sum_near(own, near))
    d_z, z_gain = norm_back(z_own, z_scale, gains[0], d_nz)
    d_z = d_z.astype(bf16)
    dec_o = after(dec_o, d_z)
    dec_near = core_swap(dec_o)
    dec_far = z_swap(after(dec_o, dec_near))
    dec_blocks = [dec_o, dec_near, dec_far, core_swap(dec_far)]
    z_gain = jnp.where(is_encoder, 0.0, z_gain)
    d_z = cross_section(d_z, 1)
    d_z_blocks = gather_rel(after(d_z, *dec_blocks))
    d_z_blocks = d_z_blocks[2:] + d_z_blocks[:2]
    d_z = d_z_blocks[0]

    back_shapes = [shape(count, 3 * MW)] + [shape(2 * n, width // 2)] * 8
    back_flops = 6 * width * count * MW + 8 * lat * cols * MW
    d_proj, *parts = lax.cond(
        is_encoder,
        lambda: tuple(kernel_call(
            encoder_back_body, place, [*d_z_blocks, w_row, projected, normed_t, enc_all],
            back_shapes, back_flops + 2 * lat * width * MW + 10 * lat * count * MW,
            [pltpu.VMEM((lat, width), bf16), pltpu.VMEM((lat, MW), bf16),
             pltpu.VMEM((4 * MW, cols), bf16)],
        )),
        lambda: tuple(kernel_call(
            decoder_back_body, place, [d_proj, d_kvz, nz, normed_t, *ups, *dec_blocks],
            back_shapes, back_flops + 4 * lat * width * MW,
            [pltpu.VMEM((width, lat), bf16), pltpu.VMEM((count, 4 * MW), bf16),
             pltpu.VMEM((4 * MW, cols), bf16), pltpu.VMEM((count, cols), bf16)],
        )),
    )
    own, near = kernel_call(
        input_grads_body, place, [d_proj, w_h], [shape(2 * n, width)] * 2,
        6 * count * width * MW,
    )
    parts = ring_sum_far(parts)
    d_n, far = sum_near(own, near)
    parts, far = lax.optimization_barrier((parts, far))
    d_n = sum_far(d_n, far)
    qkv_total, out_total = kernel_call(
        totals_body, place, gather_rel(ring_sum_near(parts)),
        [shape(n, 12 * MW, f32), shape(half, width, f32)], n * width,
    )

    back, gain_part = norm_back(tokens, scale, gains[0], d_n)
    residual = jnp.where(
        is_encoder,
        jnp.pad(d_z.astype(f32), ((half, 0), (0, 0))),
        upstream.astype(f32),
    )
    token_grad = (back + residual).astype(bf16)
    gain_total = sum_everywhere(gain_part + z_gain)
    return token_grad[None, None], qkv_total[None], out_total[None], gain_total[None]


def solution(mesh):
    fine = Mesh(mesh.devices.reshape(2, 2, 2, 4, 4), ("section", "zl", "core", "y", "x"))
    in_specs = (
        P("section", DP, RENDER, None),
        P("section", DP, None),
        P("section", DP, None),
        P("section", None),
        P(DP, RENDER, None),
    )
    out_specs = (
        P("section", DP, RENDER, None),
        P("section", DP, None),
        P("section", DP, None),
        P("section", None),
    )
    return jax.shard_map(shards, mesh=fine, in_specs=in_specs, out_specs=out_specs, check_vma=False)
```

```python
import math

import jax
import jax.numpy as jnp
from jax import lax
from jax.experimental import pallas as pl
from jax.experimental.pallas import tpu as pltpu
from jax.sharding import Mesh
from jax.sharding import PartitionSpec as P

HD = 128
MY = 2
MW = MY * HD
NORM_EPSILON = 1e-06
FACTOR = HD**-0.5
RENDER = ("zl", "core")
DP = ("y", "x")
SWAP = [(0, 1), (1, 0)]
DIAG = [(0, 3), (1, 2), (2, 1), (3, 0)]
bf16 = jnp.bfloat16
f32 = jnp.float32


def mm(left, right):
    return jnp.dot(left, right, preferred_element_type=f32)


def mm_tn(left, right):
    return lax.dot_general(left, right, (((0,), (0,)), ((), ())), preferred_element_type=f32)


def mm_nt(left, right):
    return lax.dot_general(left, right, (((1,), (1,)), ((), ())), preferred_element_type=f32)


def core_swap(t):
    return lax.ppermute(t, "core", SWAP)


def z_swap(t):
    return lax.ppermute(t, "zl", SWAP)


def gather_rel(t):
    z = z_swap(t)
    c = core_swap(t)
    return [t, c, z, core_swap(z)]


def spread_far(b):
    return z_swap(jnp.concatenate(b[2:], 0))


def spread_near(b, far):
    n = far.shape[0] // 2
    near = core_swap(jnp.concatenate([b[1], far[n:]], 0))
    return [b[0], near[:n], far[:n], near[n:]]


def sum_near(own, near):
    n = own.shape[0] // 2
    near = core_swap(near)
    return own[:n].astype(f32) + near[:n].astype(f32), add(own[n:], near[n:])


def sum_far(mine, far):
    return (mine + z_swap(far).astype(f32)).astype(bf16)


def add(*terms):
    return sum(t.astype(f32) for t in terms).astype(bf16)


def step(t, stage, k):
    pairs = []
    for core in range(2):
        for y in range(4):
            for x in range(4):
                to = (y, (x + k) % 4) if core == stage else ((y + k) % 4, x)
                pairs.append((core * 16 + y * 4 + x, core * 16 + to[0] * 4 + to[1]))
    return lax.ppermute(t, ("core", "y", "x"), pairs)


def after(t, *others):
    return lax.optimization_barrier((t, *others))[0]


def gather_near(mine):
    near, far, other = [step(mine, 0, k) for k in (1, 2, 3)]
    return jnp.concatenate([mine, near], 0), jnp.concatenate([far, other], 0)


def gather_far(t):
    up = [step(h, 1, 1) for h in t]
    down = [step(h, 1, -1) for h in t[::-1]][::-1]
    return [*t, *up, step(up[0], 1, 1), step(down[1], 1, -1), *down]


def ring_sum_far(blocks):
    own, after, far, before = blocks[:2], blocks[2:4], blocks[4:6], blocks[6:]
    far_up, far_down = step(far[0], 1, 1), step(far[1], 1, -1)
    up = [None, step(after[1], 1, 1)]
    down = [step(before[0], 1, -1), None]
    up[0] = step(add(after[0], far_up), 1, 1)
    down[1] = step(add(before[1], far_down), 1, -1)
    parts = []
    for m in range(4):
        n = own[0].shape[0] // 2
        rows = slice((m % 2) * n, (m % 2 + 1) * n)
        parts.append(add(*[t[m // 2][rows] for t in (own, up, down)]))
    return parts


def ring_sum_near(parts):
    return [parts[0]] + [step(parts[m], 0, m) for m in (1, 2, 3)]


def to_owners(t):
    found = []
    for j in range(4):
        pairs = [
            (r * 16 + y * 4 + x, (x ^ j) * 16 + r * 4 + y)
            for r in range(4) for y in range(4) for x in range(4)
        ]
        found.append(lax.ppermute(t, RENDER + DP, pairs))
    return found


def cross_section(t, source):
    pairs = [(source * 2 + i, (1 - source) * 2 + 1 - i) for i in range(2)]
    return lax.ppermute(t, ("section", "zl"), pairs)


def sum_everywhere(t, other):
    for axes in (RENDER, "x", "y"):
        one, two, three = [
            lax.ppermute(t, axes, [(i, i ^ bits) for i in range(4)]) for bits in (1, 2, 3)
        ]
        t = after((t + one) + (two + three), other)
    return t


def norm_back(values, scale, gain_row, upstream):
    wide = values.astype(f32)
    grad = upstream.astype(f32)
    scaled = grad * gain_row
    inner = jnp.sum(scaled * wide, axis=-1, keepdims=True)
    result = scale * scaled - wide * scale**3 * inner / values.shape[-1]
    return result, jnp.sum(grad * wide * scale, axis=0)


def kernel_call(body, place, inputs, outputs, flops, scratch=()):
    moved = sum(t.size * t.dtype.itemsize for t in list(inputs) + list(outputs))
    vmem = pl.BlockSpec(memory_space=pltpu.VMEM)
    held = moved + sum(math.prod(t.shape) * 4 for t in scratch)
    return pl.pallas_call(
        body,
        out_shape=tuple(outputs),
        in_specs=[pl.BlockSpec(memory_space=pltpu.SMEM)] + [vmem] * len(inputs),
        out_specs=(vmem,) * len(outputs),
        scratch_shapes=scratch,
        compiler_params=pltpu.CompilerParams(vmem_limit_bytes=held + 6 * 2**20),
        cost_estimate=pl.CostEstimate(flops=flops, bytes_accessed=moved, transcendentals=0),
    )(place, *inputs)


def shape(rows, cols, dtype=bf16):
    return jax.ShapeDtypeStruct((rows, cols), dtype)


def block(i, n):
    return pl.ds(pl.multiple_of(i * n, n), n)


def head(part, h):
    at = part * MW + h * HD
    return slice(at, at + HD)


def lay_out(dst, blocks, rank, permuted):
    wide = blocks[0].shape[1]
    for j, b in enumerate(blocks):
        n = b.shape[0] // 4
        lanes = slice(j * wide, (j + 1) * wide) if rank is None else block(rank ^ j, wide)
        for i in range(4):
            at = (i ^ j if permuted else i) * n
            dst[i * n : (i + 1) * n, lanes] = b[at : at + n, :]


def out_rows(to, rank):
    return ((to >> 2) ^ rank) * 4 + (to & 3)


def norm_body(place, gain, t0, t1, t2, t3, normed, normed_t, scales):
    n = t0.shape[0]
    for j, t in enumerate((t0, t1, t2, t3)):
        wide = t[...].astype(f32)
        scale = lax.rsqrt(jnp.mean(wide * wide, axis=-1, keepdims=True) + NORM_EPSILON)
        out = (wide * scale * gain[...]).astype(bf16)
        normed[j * n : (j + 1) * n, :] = out
        normed_t[:, j * n : (j + 1) * n] = out.T
        if j == 0:
            scales[...] = scale


def holder(place, k, m, sign):
    y, x, first = place[0], place[1], place[2] & 1
    dy, dx = jnp.where(first == 0, k, m), jnp.where(first == 0, m, k)
    return ((y + sign * dy) & 3) * 4 + ((x + sign * dx) & 3)


def project_body(place, normed, *refs):
    w, w_rel, out, enc_o = refs[8:]
    n, wide = refs[0].shape[0] // 2, w.shape[1]
    for k in range(4):
        for m in range(4):
            src, row = refs[2 * k + m // 2], (m % 2) * n
            to = holder(place, k, m, -1)
            w[block(to, n), :] = src[row : row + n, :wide]
            for i in range(2):
                w_rel[block(out_rows(to, place[2]), n // 2), i * MW : (i + 1) * MW] = src[
                    row + i * (n // 2) : row + (i + 1) * (n // 2), wide:
                ]
    for at in range(0, w.shape[1], 256):
        out[:, at : at + 256] = mm(normed[...], w[:, at : at + 256]).astype(bf16)
    for h in range(MY):
        q = latent_rows(out, head(0, h))
        p = softmax(mm_nt(q, out[:, head(1, h)]) * FACTOR)
        enc_o[:, head(0, h)] = mm(p.astype(bf16), out[:, head(2, h)]).astype(bf16)


def upstream_body(place, u0, u1, u2, u3, w_rel, own, near):
    n, cols = u0.shape[0], w_rel.shape[1]
    for j, u in enumerate((u0, u1, u2, u3)):
        got = mm_nt(u[:, block(place[2], cols)], w_rel[...]).astype(bf16)
        for i in range(4):
            at = ((i // 2) * 4 + (i ^ j)) * n
            (near if i % 2 else own)[at : at + n, :] = got[:, i * MW : (i + 1) * MW]


def latent_rows(ref, lanes):
    half = ref.shape[0] // 8
    return jnp.concatenate(
        [ref[(2 * i + 1) * half : (2 * i + 2) * half, lanes] for i in range(4)], 0
    )


def softmax(scores):
    raised = jnp.exp(scores - jnp.max(scores, axis=-1, keepdims=True))
    return raised * (1.0 / jnp.sum(raised, axis=-1, keepdims=True))


def latents_body(place, t0, t1, t2, t3, o0, o1, o2, o3, w_rel, z, o_all):
    rank = place[2]
    lay_out(o_all, (o0, o1, o2, o3), None, True)
    half, cols = t0.shape[0] // 2, z.shape[1]
    added = mm(o_all[...], w_rel[...])
    for j, t in enumerate((t0, t1, t2, t3)):
        rows = slice(j * half, (j + 1) * half)
        z[rows, :] = (t[half:, block(rank, cols)].astype(f32) + added[rows]).astype(bf16)


def weight_parts(place, normed_t, d_proj, d_out, outs, extra):
    n = outs[0].shape[0] // 2
    wide, m_out = d_proj.shape[1], d_out.shape[0] // 16
    for k in range(4):
        for m in range(4):
            to = holder(place, k, m, 1)
            part = mm(normed_t[block(to, n), :], d_proj[...])
            o, row = outs[2 * k + m // 2], (m % 2) * n
            if extra is not None:
                nz_t, d_kvz = extra
                more = mm(nz_t[block(to, n), :], d_kvz[...])
                part = jnp.concatenate([part[:, :MW], part[:, MW:] + more], 1)
            o[row : row + n, :wide] = part.astype(bf16)
            for i in range(n // m_out):
                o[row + i * m_out : row + (i + 1) * m_out, wide:] = d_out[
                    block(to, m_out), i * MW : (i + 1) * MW
                ]


def encoder_back_body(place, d0, d1, d2, d3, r0, r1, r2, r3, proj, normed_t, w, o, *refs):
    own, near, outs, (d_proj, d_z, w_row, up, d_out) = refs[0], refs[1], refs[2:10], refs[10:]
    lay_out(w_row, (r0, r1, r2, r3), place[2], False)
    lat = d_z.shape[0]
    half = lat // 4
    for j, d in enumerate((d0, d1, d2, d3)):
        d_z[j * half : (j + 1) * half, :] = d[...]
    up[...] = mm_nt(d_z[...], w_row[...]).astype(bf16)
    for h in range(MY):
        q = latent_rows(proj, head(0, h))
        k, v = proj[:, head(1, h)], proj[:, head(2, h)]
        u = up[:, head(0, h)]
        p = softmax(mm_nt(q, k) * FACTOR)
        dp = mm_nt(u, v)
        delta = jnp.sum(dp * p, axis=-1, keepdims=True)
        ds = (p * (dp - delta) * FACTOR).astype(bf16)
        dq = mm(ds, k).astype(bf16)
        for i in range(4):
            at = 2 * i * half
            d_proj[at : at + half, head(0, h)] = jnp.zeros((half, HD), bf16)
            d_proj[at + half : at + 2 * half, head(0, h)] = dq[i * half : (i + 1) * half]
        d_proj[:, head(1, h)] = mm_tn(ds, q).astype(bf16)
        d_proj[:, head(2, h)] = mm_tn(p.astype(bf16), u).astype(bf16)
    d_out[...] = mm_tn(o[...], d_z[...]).astype(bf16)
    weight_parts(place, normed_t, d_proj, d_out, outs, None)
    sums_for_render(d_proj, w, 0, own, near)


def decoder_back_body(place, d_proj, d_kvz, nz, normed_t, w, *refs):
    ups, o, own, near = refs[:4], refs[4], refs[5], refs[6]
    outs, (nz_t, d_out, up) = refs[7:15], refs[15:]
    for at in range(0, nz.shape[1], 512):
        nz_t[at : at + 512, :] = nz[:, at : at + 512].T
    n = ups[0].shape[0]
    for j, u in enumerate(ups):
        up[j * n : (j + 1) * n, :] = u[...]
    d_out[...] = mm_tn(o[...], up[...]).astype(bf16)
    weight_parts(place, normed_t, d_proj, d_out, outs, (nz_t, d_kvz))
    sums_for_render(d_proj, w, 0, own, near)


def decoder_body(place, gain, z0, z1, z2, z3, w, proj, up, *refs):
    out, d_proj, d_kvz, nz, scales, z_own, own, near, z, kvz, acc = refs
    lat, width = z.shape
    half = lat // 4
    lay_out(z, (z0, z1, z2, z3), place[2], True)
    z_own[...] = z[:half, :]
    for i in range(4):
        rows = slice(i * half, (i + 1) * half)
        wide = z[rows, :].astype(f32)
        scale = lax.rsqrt(jnp.mean(wide * wide, axis=-1, keepdims=True) + NORM_EPSILON)
        nz[rows, :] = (wide * scale * gain[...]).astype(bf16)
        if i == 0:
            scales[...] = scale
    kvz[...] = mm(nz[...], w[:, MW:]).astype(bf16)
    views = proj.shape[0] // 128
    for h in range(MY):
        kz, vz = kvz[:, head(0, h)], kvz[:, head(1, h)]
        for i in range(views):
            rows = slice(i * 128, (i + 1) * 128)
            q, k, v = [proj[rows, head(part, h)] for part in range(3)]
            u = up[rows, head(0, h)]
            s = mm_nt(q, kz) * FACTOR
            t = mm_nt(q, k) * FACTOR
            top = jnp.maximum(
                jnp.max(s, axis=-1, keepdims=True), jnp.max(t, axis=-1, keepdims=True)
            )
            s, t = jnp.exp(s - top), jnp.exp(t - top)
            total = jnp.sum(s, axis=-1, keepdims=True) + jnp.sum(t, axis=-1, keepdims=True)
            s, t = s * (1.0 / total), t * (1.0 / total)
            sb, tb = s.astype(bf16), t.astype(bf16)
            out[rows, head(0, h)] = (mm(sb, vz) + mm(tb, v)).astype(bf16)
            ds, dt = mm_nt(u, vz), mm_nt(u, v)
            delta = jnp.sum(ds * s, axis=-1, keepdims=True) + jnp.sum(dt * t, axis=-1, keepdims=True)
            ds = (s * (ds - delta) * FACTOR).astype(bf16)
            dt = (t * (dt - delta) * FACTOR).astype(bf16)
            d_proj[rows, head(0, h)] = (mm(ds, kz) + mm(dt, k)).astype(bf16)
            d_proj[rows, head(1, h)] = mm_tn(dt, q).astype(bf16)
            d_proj[rows, head(2, h)] = mm_tn(tb, u).astype(bf16)
            dkz, dvz = mm_tn(ds, q), mm_tn(sb, u)
            if i > 0:
                dkz, dvz = dkz + acc[:, head(0, h)], dvz + acc[:, head(1, h)]
            acc[:, head(0, h)], acc[:, head(1, h)] = dkz, dvz
    d_kvz[...] = acc[...].astype(bf16)
    sums_for_render(d_kvz, w, MW, own, near)


def sums_for_render(grads, w, first, own, near):
    n = grads.shape[0] // 4
    for at in range(0, w.shape[0], 512):
        cols = slice(at, at + 512)
        got = mm_nt(grads[...], w[cols, first:]).astype(bf16)
        for i in range(2):
            own[i * n : (i + 1) * n, cols] = got[2 * i * n : (2 * i + 1) * n]
            near[i * n : (i + 1) * n, cols] = got[(2 * i + 1) * n : (2 * i + 2) * n]


def totals_body(place, t0, t1, t2, t3, o0, o1, o2, o3, qkv, out):
    for j, (t, o) in enumerate(((t0, o0), (t1, o1), (t2, o2), (t3, o3))):
        rank = place[2] ^ j
        for part in range(3):
            qkv[:, block(part * 4 + rank, MW)] = t[:, part * MW : (part + 1) * MW].astype(f32)
        n = out.shape[0] // 4
        for i in range(o.shape[0] // n):
            out[block(rank, n), i * MW : (i + 1) * MW] = o[i * n : (i + 1) * n, :].astype(f32)


def shards(section_tokens, w_qkv, w_out, gains, cotangent):
    tokens = section_tokens[0, 0]
    upstream = cotangent[0]
    rank = lax.axis_index("zl") * 2 + lax.axis_index("core")
    place = jnp.stack([lax.axis_index("y"), lax.axis_index("x"), rank]).astype(jnp.int32)
    is_encoder = lax.axis_index("section") == 0
    n, width = tokens.shape
    half, cols, count, lat = n // 2, width // 4, 4 * n, 2 * n

    own_cols = [
        lax.dynamic_slice_in_dim(w_qkv[0], part * 4 * MW + rank * MW, MW, 1) for part in range(3)
    ]
    own_out = [lax.dynamic_slice_in_dim(w_out[0], rank * cols + i * MW, MW, 1) for i in range(2)]
    near = gather_near(jnp.concatenate([*own_cols, jnp.concatenate(own_out, 0)], 1))
    rows = gather_rel(tokens)
    near, rows[2] = lax.optimization_barrier((near, rows[2]))
    w_parts = gather_far(near)
    normed, normed_t, scale = kernel_call(
        norm_body, place, [gains, *rows],
        [shape(count, width), shape(width, count), shape(n, 1, f32)], 8 * count * width,
    )
    ups = gather_rel(after(upstream, rows[2]))
    w_h, w_rel, projected, enc_o = kernel_call(
        project_body, place, [normed, *w_parts],
        [shape(width, 3 * MW), shape(4 * MW, cols), shape(count, 3 * MW), shape(lat, MW)],
        6 * count * width * MW + 4 * lat * count * MW,
    )
    enc_blocks = gather_rel(enc_o)
    z_cols = kernel_call(
        latents_body, place, [*rows, *enc_blocks, w_rel], [shape(lat, cols)],
        8 * lat * cols * MW, [pltpu.VMEM((lat, 4 * MW), bf16)],
    )[0]
    z_crossed = cross_section(z_cols, 0)
    up_own, up_near = kernel_call(
        upstream_body, place, [*ups, after(w_rel, enc_blocks[1])], [shape(2 * count, MW)] * 2,
        8 * count * cols * MW,
    )
    up_o = sum_far(*sum_near(up_own, up_near))
    z_blocks = gather_rel(z_crossed)
    w_row_blocks = [after(w_rel, z_blocks[2])[j * MW : (j + 1) * MW] for j in range(4)]
    w_row_far = spread_far(w_row_blocks)
    z_blocks = z_blocks[2:] + z_blocks[:2]

    decoder_shapes = [
        shape(count, MW), shape(count, 3 * MW), shape(lat, 2 * MW), shape(lat, width),
        shape(half, 1, f32), shape(half, width), shape(2 * half, width), shape(2 * half, width),
    ]
    dec_o, d_proj, d_kvz, nz, z_scale, z_own, own, near = lax.cond(
        is_encoder,
        lambda: tuple(jnp.zeros(s.shape, s.dtype) for s in decoder_shapes),
        lambda: tuple(kernel_call(
            decoder_body, place, [gains, *z_blocks, w_h, projected, up_o], decoder_shapes,
            8 * lat * width * MW + 12 * count * (lat + 128) * MW,
            [pltpu.VMEM((lat, width), bf16), pltpu.VMEM((lat, 2 * MW), bf16),
             pltpu.VMEM((lat, 2 * MW), f32)],
        )),
    )
    near, w_row_far = lax.optimization_barrier((near, w_row_far))
    w_row_blocks = spread_near(w_row_blocks, w_row_far)
    d_nz = sum_far(*sum_near(own, near))
    d_z, z_gain = norm_back(z_own, z_scale, gains[0], d_nz)
    d_z = d_z.astype(bf16)
    z_gain = jnp.where(is_encoder, 0.0, z_gain)
    d_z = cross_section(d_z, 1)
    d_z_blocks = gather_rel(d_z)
    d_z_blocks = d_z_blocks[2:] + d_z_blocks[:2]
    d_z = d_z_blocks[0]

    back_shapes = [shape(2 * n, width)] * 2 + [shape(2 * n, width // 2)] * 8
    back_flops = 12 * width * count * MW + 2 * lat * width * MW
    own, near, *parts = lax.cond(
        is_encoder,
        lambda: tuple(kernel_call(
            encoder_back_body, place, [*d_z_blocks, *w_row_blocks, projected, normed_t, w_h, enc_o],
            back_shapes, back_flops + 2 * lat * width * MW + 10 * lat * count * MW,
            [pltpu.VMEM((count, 3 * MW), bf16), pltpu.VMEM((lat, width), bf16),
             pltpu.VMEM((MW, width), bf16), pltpu.VMEM((lat, MW), bf16), pltpu.VMEM((MW, width), bf16)],
        )),
        lambda: tuple(kernel_call(
            decoder_back_body, place, [d_proj, d_kvz, nz, normed_t, w_h, *ups, dec_o],
            back_shapes, back_flops + 4 * lat * width * MW,
            [pltpu.VMEM((width, lat), bf16), pltpu.VMEM((MW, width), bf16),
             pltpu.VMEM((count, width), bf16)],
        )),
    )
    d_n = sum_far(*sum_near(own, near))
    back, gain_part = norm_back(tokens, scale, gains[0], d_n)
    parts = ring_sum_near(ring_sum_far(parts))
    parts[0], gain_part = lax.optimization_barrier((parts[0], gain_part))
    qkv_sum = add(*[t[:, : 3 * MW] for t in parts])
    qkv_blocks = gather_rel(qkv_sum)
    out_blocks = to_owners(add(*[t[:, 3 * MW :] for t in parts]))
    qkv_total, out_total = kernel_call(
        totals_body, place, [*qkv_blocks, *out_blocks],
        [shape(n, 12 * MW, f32), shape(half, width, f32)], n * width,
    )
    residual = jnp.where(
        is_encoder,
        jnp.pad(d_z.astype(f32), ((half, 0), (0, 0))),
        upstream.astype(f32),
    )
    token_grad = (back + residual).astype(bf16)
    gain_total = sum_everywhere(gain_part + z_gain, qkv_sum)
    return token_grad[None, None], qkv_total[None], out_total[None], gain_total[None]


def solution(mesh):
    fine = Mesh(mesh.devices.reshape(2, 2, 2, 4, 4), ("section", "zl", "core", "y", "x"))
    in_specs = (
        P("section", DP, RENDER, None),
        P("section", DP, None),
        P("section", DP, None),
        P("section", None),
        P(DP, RENDER, None),
    )
    out_specs = (
        P("section", DP, RENDER, None),
        P("section", DP, None),
        P("section", DP, None),
        P("section", None),
    )
    return jax.shard_map(shards, mesh=fine, in_specs=in_specs, out_specs=out_specs, check_vma=False)
```

```python
import math

import jax
import jax.numpy as jnp
from jax import lax
from jax.experimental import pallas as pl
from jax.experimental.pallas import tpu as pltpu
from jax.sharding import Mesh
from jax.sharding import PartitionSpec as P

HD = 128
MY = 2
MW = MY * HD
NORM_EPSILON = 1e-06
FACTOR = HD**-0.5
RENDER = ("zl", "core")
DP = ("y", "x")
SWAP = [(0, 1), (1, 0)]
DIAG = [(0, 3), (1, 2), (2, 1), (3, 0)]
bf16 = jnp.bfloat16
f32 = jnp.float32


def mm(left, right):
    return jnp.dot(left, right, preferred_element_type=f32)


def mm_tn(left, right):
    return lax.dot_general(left, right, (((0,), (0,)), ((), ())), preferred_element_type=f32)


def mm_nt(left, right):
    return lax.dot_general(left, right, (((1,), (1,)), ((), ())), preferred_element_type=f32)


def core_swap(t):
    return lax.ppermute(t, "core", SWAP)


def z_swap(t):
    return lax.ppermute(t, "zl", SWAP)


def gather_rel(t):
    z = z_swap(t)
    c = core_swap(t)
    return [t, c, z, core_swap(z)]


def spread_rel(b):
    return [b[0], core_swap(b[1]), z_swap(b[2]), lax.ppermute(b[3], RENDER, DIAG)]


def sum_near(own, near):
    n = own.shape[0] // 2
    near = core_swap(near)
    return own[:n].astype(f32) + near[:n].astype(f32), add(own[n:], near[n:])


def sum_far(mine, far):
    return (mine + z_swap(far).astype(f32)).astype(bf16)


def add(*terms):
    return sum(t.astype(f32) for t in terms).astype(bf16)


def step(t, stage, k):
    pairs = []
    for core in range(2):
        for y in range(4):
            for x in range(4):
                to = (y, (x + k) % 4) if core == stage else ((y + k) % 4, x)
                pairs.append((core * 16 + y * 4 + x, core * 16 + to[0] * 4 + to[1]))
    return lax.ppermute(t, ("core", "y", "x"), pairs)


def after(t, *others):
    return lax.optimization_barrier((t, *others))[0]


def gather_near(mine):
    near, far, other = [step(mine, 0, k) for k in (1, 2, 3)]
    return jnp.concatenate([mine, near], 0), jnp.concatenate([far, other], 0)


def gather_far(t):
    up = [step(h, 1, 1) for h in t]
    down = [step(h, 1, -1) for h in t[::-1]][::-1]
    return [*t, *up, step(up[0], 1, 1), step(down[1], 1, -1), *down]


def ring_sum_far(blocks):
    own, after, far, before = blocks[:2], blocks[2:4], blocks[4:6], blocks[6:]
    far_up, far_down = step(far[0], 1, 1), step(far[1], 1, -1)
    up = [None, step(after[1], 1, 1)]
    down = [step(before[0], 1, -1), None]
    up[0] = step(add(after[0], far_up), 1, 1)
    down[1] = step(add(before[1], far_down), 1, -1)
    parts = []
    for m in range(4):
        n = own[0].shape[0] // 2
        rows = slice((m % 2) * n, (m % 2 + 1) * n)
        parts.append(add(*[t[m // 2][rows] for t in (own, up, down)]))
    return parts, (up[1], down[0])


def ring_sum_near(parts):
    return [parts[0]] + [step(parts[m], 0, m) for m in (1, 2, 3)]


def to_owners(t):
    found = []
    for j in range(4):
        pairs = [
            (r * 16 + y * 4 + x, (x ^ j) * 16 + r * 4 + y)
            for r in range(4) for y in range(4) for x in range(4)
        ]
        found.append(lax.ppermute(t, RENDER + DP, pairs))
    return found


def cross_section(t, source):
    pairs = [(source * 2 + i, (1 - source) * 2 + 1 - i) for i in range(2)]
    return lax.ppermute(t, ("section", "zl"), pairs)


def sum_everywhere(t):
    for axes in (RENDER, "x", "y"):
        one, two, three = [
            lax.ppermute(t, axes, [(i, i ^ bits) for i in range(4)]) for bits in (1, 2, 3)
        ]
        t = (t + one) + (two + three)
    return t


def norm_back(values, scale, gain_row, upstream):
    wide = values.astype(f32)
    grad = upstream.astype(f32)
    scaled = grad * gain_row
    inner = jnp.sum(scaled * wide, axis=-1, keepdims=True)
    result = scale * scaled - wide * scale**3 * inner / values.shape[-1]
    return result


def kernel_call(body, place, inputs, outputs, flops, scratch=()):
    moved = sum(t.size * t.dtype.itemsize for t in list(inputs) + list(outputs))
    vmem = pl.BlockSpec(memory_space=pltpu.VMEM)
    held = moved + sum(math.prod(t.shape) * 4 for t in scratch)
    return pl.pallas_call(
        body,
        out_shape=tuple(outputs),
        in_specs=[pl.BlockSpec(memory_space=pltpu.SMEM)] + [vmem] * len(inputs),
        out_specs=(vmem,) * len(outputs),
        scratch_shapes=scratch,
        compiler_params=pltpu.CompilerParams(vmem_limit_bytes=held + 6 * 2**20),
        cost_estimate=pl.CostEstimate(flops=flops, bytes_accessed=moved, transcendentals=0),
    )(place, *inputs)


def shape(rows, cols, dtype=bf16):
    return jax.ShapeDtypeStruct((rows, cols), dtype)


def block(i, n):
    return pl.ds(pl.multiple_of(i * n, n), n)


def head(part, h):
    at = part * MW + h * HD
    return slice(at, at + HD)


def lay_out(dst, blocks, rank, permuted):
    wide = blocks[0].shape[1]
    for j, b in enumerate(blocks):
        n = b.shape[0] // 4
        lanes = slice(j * wide, (j + 1) * wide) if rank is None else block(rank ^ j, wide)
        for i in range(4):
            at = (i ^ j if permuted else i) * n
            dst[i * n : (i + 1) * n, lanes] = b[at : at + n, :]


def out_rows(to, rank):
    return ((to >> 2) ^ rank) * 4 + (to & 3)


def norm_body(place, gain, t0, t1, t2, t3, normed, normed_t, scales):
    n = t0.shape[0]
    for j, t in enumerate((t0, t1, t2, t3)):
        wide = t[...].astype(f32)
        scale = lax.rsqrt(jnp.mean(wide * wide, axis=-1, keepdims=True) + NORM_EPSILON)
        out = (wide * scale * gain[...]).astype(bf16)
        normed[j * n : (j + 1) * n, :] = out
        normed_t[:, j * n : (j + 1) * n] = out.T
        scales[j * n : (j + 1) * n, :] = scale


def holder(place, k, m, sign):
    y, x, first = place[0], place[1], place[2] & 1
    dy, dx = jnp.where(first == 0, k, m), jnp.where(first == 0, m, k)
    return ((y + sign * dy) & 3) * 4 + ((x + sign * dx) & 3)


def project_body(place, normed, *refs):
    w, w_rel, out, enc_o = refs[8:]
    n, wide = refs[0].shape[0] // 2, w.shape[1]
    for k in range(4):
        for m in range(4):
            src, row = refs[2 * k + m // 2], (m % 2) * n
            to = holder(place, k, m, -1)
            w[block(to, n), :] = src[row : row + n, :wide]
            for i in range(2):
                w_rel[block(out_rows(to, place[2]), n // 2), i * MW : (i + 1) * MW] = src[
                    row + i * (n // 2) : row + (i + 1) * (n // 2), wide:
                ]
    for at in range(0, w.shape[1], 256):
        out[:, at : at + 256] = mm(normed[...], w[:, at : at + 256]).astype(bf16)
    for h in range(MY):
        q = latent_rows(out, head(0, h))
        p = softmax(mm_nt(q, out[:, head(1, h)]) * FACTOR)
        enc_o[:, head(0, h)] = mm(p.astype(bf16), out[:, head(2, h)]).astype(bf16)


def upstream_body(place, u0, u1, u2, u3, b0, b1, b2, b3, up_o, w_row):
    lay_out(w_row, (b0, b1, b2, b3), place[2], False)
    n = u0.shape[0]
    for j, u in enumerate((u0, u1, u2, u3)):
        up_o[j * n : (j + 1) * n, :] = mm_nt(u[...], w_row[...]).astype(bf16)


def latent_rows(ref, lanes):
    half = ref.shape[0] // 8
    return jnp.concatenate(
        [ref[(2 * i + 1) * half : (2 * i + 2) * half, lanes] for i in range(4)], 0
    )


def softmax(scores):
    raised = jnp.exp(scores - jnp.max(scores, axis=-1, keepdims=True))
    return raised * (1.0 / jnp.sum(raised, axis=-1, keepdims=True))


def latents_body(place, t0, t1, t2, t3, o0, o1, o2, o3, w_rel, z, o_all):
    rank = place[2]
    lay_out(o_all, (o0, o1, o2, o3), None, True)
    half, cols = t0.shape[0] // 2, z.shape[1]
    added = mm(o_all[...], w_rel[...])
    for j, t in enumerate((t0, t1, t2, t3)):
        rows = slice(j * half, (j + 1) * half)
        z[rows, :] = (t[half:, block(rank, cols)].astype(f32) + added[rows]).astype(bf16)


def weight_parts(place, normed_t, d_proj, d_out, outs, extra):
    n = outs[0].shape[0] // 2
    wide, m_out = d_proj.shape[1], d_out.shape[0] // 16
    for k in range(4):
        for m in range(4):
            to = holder(place, k, m, 1)
            part = mm(normed_t[block(to, n), :], d_proj[...])
            o, row = outs[2 * k + m // 2], (m % 2) * n
            if extra is not None:
                nz_t, d_kvz = extra
                more = mm(nz_t[block(to, n), :], d_kvz[...])
                part = jnp.concatenate([part[:, :MW], part[:, MW:] + more], 1)
            o[row : row + n, :wide] = part.astype(bf16)
            for i in range(n // m_out):
                o[row + i * m_out : row + (i + 1) * m_out, wide:] = d_out[
                    block(to, m_out), i * MW : (i + 1) * MW
                ]


def encoder_back_body(place, d0, d1, d2, d3, w_row, proj, normed_t, w, o, scales, *refs):
    rows, own, near, gain, outs = refs[:4], refs[4], refs[5], refs[6], refs[7:15]
    d_proj, d_z, up, d_out = refs[15:]
    lat = d_z.shape[0]
    half = lat // 4
    for j, d in enumerate((d0, d1, d2, d3)):
        d_z[j * half : (j + 1) * half, :] = d[...]
    up[...] = mm_nt(d_z[...], w_row[...]).astype(bf16)
    for h in range(MY):
        q = latent_rows(proj, head(0, h))
        k, v = proj[:, head(1, h)], proj[:, head(2, h)]
        u = up[:, head(0, h)]
        p = softmax(mm_nt(q, k) * FACTOR)
        dp = mm_nt(u, v)
        delta = jnp.sum(dp * p, axis=-1, keepdims=True)
        ds = (p * (dp - delta) * FACTOR).astype(bf16)
        dq = mm(ds, k).astype(bf16)
        for i in range(4):
            at = 2 * i * half
            d_proj[at : at + half, head(0, h)] = jnp.zeros((half, HD), bf16)
            d_proj[at + half : at + 2 * half, head(0, h)] = dq[i * half : (i + 1) * half]
        d_proj[:, head(1, h)] = mm_tn(ds, q).astype(bf16)
        d_proj[:, head(2, h)] = mm_tn(p.astype(bf16), u).astype(bf16)
    d_out[...] = mm_tn(o[...], d_z[...]).astype(bf16)
    weight_parts(place, normed_t, d_proj, d_out, outs, None)
    gain[...] = jnp.zeros(gain.shape, f32)
    sums_for_render(d_proj, w, 0, own, near, rows, scales, gain)


def decoder_back_body(place, d_proj, d_kvz, nz, normed_t, w, *refs):
    ups, o, z_gain, scales, rows = refs[:4], refs[4], refs[5], refs[6], refs[7:11]
    own, near, gain, outs, (nz_t, d_out, up) = *refs[11:14], refs[14:22], refs[22:]
    for at in range(0, nz.shape[1], 512):
        nz_t[at : at + 512, :] = nz[:, at : at + 512].T
    n = ups[0].shape[0]
    for j, u in enumerate(ups):
        up[j * n : (j + 1) * n, :] = u[...]
    d_out[...] = mm_tn(o[...], up[...]).astype(bf16)
    weight_parts(place, normed_t, d_proj, d_out, outs, (nz_t, d_kvz))
    gain[...] = z_gain[...]
    sums_for_render(d_proj, w, 0, own, near, rows, scales, gain)


def decoder_body(place, gain, z0, z1, z2, z3, w, proj, up, *refs):
    out, d_proj, d_kvz, nz, scales, z_own, own, near, z_gain, z, kvz, acc = refs
    lat, width = z.shape
    half = lat // 4
    lay_out(z, (z0, z1, z2, z3), place[2], True)
    z_own[...] = z[:half, :]
    for i in range(4):
        rows = slice(i * half, (i + 1) * half)
        wide = z[rows, :].astype(f32)
        scale = lax.rsqrt(jnp.mean(wide * wide, axis=-1, keepdims=True) + NORM_EPSILON)
        nz[rows, :] = (wide * scale * gain[...]).astype(bf16)
        scales[rows, :] = scale
    kvz[...] = mm(nz[...], w[:, MW:]).astype(bf16)
    views = proj.shape[0] // 128
    for h in range(MY):
        kz, vz = kvz[:, head(0, h)], kvz[:, head(1, h)]
        for i in range(views):
            rows = slice(i * 128, (i + 1) * 128)
            q, k, v = [proj[rows, head(part, h)] for part in range(3)]
            u = up[rows, head(0, h)]
            s = mm_nt(q, kz) * FACTOR
            t = mm_nt(q, k) * FACTOR
            top = jnp.maximum(
                jnp.max(s, axis=-1, keepdims=True), jnp.max(t, axis=-1, keepdims=True)
            )
            s, t = jnp.exp(s - top), jnp.exp(t - top)
            total = jnp.sum(s, axis=-1, keepdims=True) + jnp.sum(t, axis=-1, keepdims=True)
            s, t = s * (1.0 / total), t * (1.0 / total)
            sb, tb = s.astype(bf16), t.astype(bf16)
            out[rows, head(0, h)] = (mm(sb, vz) + mm(tb, v)).astype(bf16)
            ds, dt = mm_nt(u, vz), mm_nt(u, v)
            delta = jnp.sum(ds * s, axis=-1, keepdims=True) + jnp.sum(dt * t, axis=-1, keepdims=True)
            ds = (s * (ds - delta) * FACTOR).astype(bf16)
            dt = (t * (dt - delta) * FACTOR).astype(bf16)
            d_proj[rows, head(0, h)] = (mm(ds, kz) + mm(dt, k)).astype(bf16)
            d_proj[rows, head(1, h)] = mm_tn(dt, q).astype(bf16)
            d_proj[rows, head(2, h)] = mm_tn(tb, u).astype(bf16)
            dkz, dvz = mm_tn(ds, q), mm_tn(sb, u)
            if i > 0:
                dkz, dvz = dkz + acc[:, head(0, h)], dvz + acc[:, head(1, h)]
            acc[:, head(0, h)], acc[:, head(1, h)] = dkz, dvz
    d_kvz[...] = acc[...].astype(bf16)
    z_gain[...] = jnp.zeros(z_gain.shape, f32)
    z_rows = [z.at[i * half : (i + 1) * half, :] for i in range(4)]
    sums_for_render(d_kvz, w, MW, own, near, z_rows, scales, z_gain)


def sums_for_render(grads, w, first, own, near, rows, scales, gain):
    n = grads.shape[0] // 4
    for at in range(0, w.shape[0], 512):
        cols = slice(at, at + 512)
        got = mm_nt(grads[...], w[cols, first:])
        for i, r in enumerate(rows):
            part = got[i * n : (i + 1) * n]
            term = part * (r[:, cols].astype(f32) * scales[i * n : (i + 1) * n, :])
            gain[:, cols] += jnp.sum(term, axis=0, keepdims=True)
            half = slice(i // 2 * n, (i // 2 + 1) * n)
            (near if i % 2 else own)[half, cols] = part.astype(bf16)


def totals_body(place, t0, t1, t2, t3, o0, o1, o2, o3, qkv, out):
    for j, (t, o) in enumerate(((t0, o0), (t1, o1), (t2, o2), (t3, o3))):
        rank = place[2] ^ j
        for part in range(3):
            qkv[:, block(part * 4 + rank, MW)] = t[:, part * MW : (part + 1) * MW].astype(f32)
        n = out.shape[0] // 4
        for i in range(o.shape[0] // n):
            out[block(rank, n), i * MW : (i + 1) * MW] = o[i * n : (i + 1) * n, :].astype(f32)


def shards(section_tokens, w_qkv, w_out, gains, cotangent):
    tokens = section_tokens[0, 0]
    upstream = cotangent[0]
    rank = lax.axis_index("zl") * 2 + lax.axis_index("core")
    place = jnp.stack([lax.axis_index("y"), lax.axis_index("x"), rank]).astype(jnp.int32)
    is_encoder = lax.axis_index("section") == 0
    n, width = tokens.shape
    half, cols, count, lat = n // 2, width // 4, 4 * n, 2 * n

    own_cols = [
        lax.dynamic_slice_in_dim(w_qkv[0], part * 4 * MW + rank * MW, MW, 1) for part in range(3)
    ]
    own_out = [lax.dynamic_slice_in_dim(w_out[0], rank * cols + i * MW, MW, 1) for i in range(2)]
    near = gather_near(jnp.concatenate([*own_cols, jnp.concatenate(own_out, 0)], 1))
    rows = gather_rel(tokens)
    near, rows[2] = lax.optimization_barrier((near, rows[2]))
    w_parts = gather_far(near)
    normed, normed_t, scales = kernel_call(
        norm_body, place, [gains, *rows],
        [shape(count, width), shape(width, count), shape(count, 1, f32)], 8 * count * width,
    )
    ups = gather_rel(after(upstream, w_parts[2]))
    w_h, w_rel, projected, enc_o = kernel_call(
        project_body, place, [normed, *w_parts],
        [shape(width, 3 * MW), shape(4 * MW, cols), shape(count, 3 * MW), shape(lat, MW)],
        6 * count * width * MW + 4 * lat * count * MW,
    )
    w_row_blocks = spread_rel([w_rel[j * MW : (j + 1) * MW] for j in range(4)])
    enc_blocks = gather_rel(enc_o)
    enc_blocks[1], ups = lax.optimization_barrier((enc_blocks[1], ups))
    z_cols = kernel_call(
        latents_body, place, [*rows, *enc_blocks, w_rel], [shape(lat, cols)],
        8 * lat * cols * MW, [pltpu.VMEM((lat, 4 * MW), bf16)],
    )[0]
    z_crossed = cross_section(z_cols, 0)
    up_o, w_row = kernel_call(
        upstream_body, place, [*ups, *w_row_blocks],
        [shape(count, MW), shape(MW, width)], 2 * count * width * MW,
    )
    z_blocks = gather_rel(after(z_crossed, up_o))
    z_blocks = z_blocks[2:] + z_blocks[:2]

    decoder_shapes = [
        shape(count, MW), shape(count, 3 * MW), shape(lat, 2 * MW), shape(lat, width),
        shape(lat, 1, f32), shape(half, width), shape(2 * half, width), shape(2 * half, width),
        shape(1, width, f32),
    ]
    dec_o, d_proj, d_kvz, nz, z_scale, z_own, own, near, z_gain = lax.cond(
        is_encoder,
        lambda: tuple(jnp.zeros(s.shape, s.dtype) for s in decoder_shapes),
        lambda: tuple(kernel_call(
            decoder_body, place, [gains, *z_blocks, w_h, projected, up_o], decoder_shapes,
            8 * lat * width * MW + 12 * count * (lat + 128) * MW,
            [pltpu.VMEM((lat, width), bf16), pltpu.VMEM((lat, 2 * MW), bf16),
             pltpu.VMEM((lat, 2 * MW), f32)],
        )),
    )
    d_nz = sum_far(*sum_near(own, near))
    d_z = norm_back(z_own, z_scale[:half], gains[0], d_nz)
    d_z = d_z.astype(bf16)
    d_z = cross_section(d_z, 1)
    d_z_blocks = gather_rel(d_z)
    d_z_blocks = d_z_blocks[2:] + d_z_blocks[:2]
    d_z = d_z_blocks[0]

    back_shapes = [shape(2 * n, width)] * 2 + [shape(1, width, f32)] + [shape(2 * n, width // 2)] * 8
    back_flops = 12 * width * count * MW + 2 * lat * width * MW
    own, near, gain_part, *parts = lax.cond(
        is_encoder,
        lambda: tuple(kernel_call(
            encoder_back_body, place, [*d_z_blocks, w_row, projected, normed_t, w_h, enc_o, scales, *rows],
            back_shapes, back_flops + 2 * lat * width * MW + 10 * lat * count * MW,
            [pltpu.VMEM((count, 3 * MW), bf16), pltpu.VMEM((lat, width), bf16),
             pltpu.VMEM((lat, MW), bf16), pltpu.VMEM((MW, width), bf16)],
        )),
        lambda: tuple(kernel_call(
            decoder_back_body, place, [d_proj, d_kvz, nz, normed_t, w_h, *ups, dec_o, z_gain, scales, *rows],
            back_shapes, back_flops + 4 * lat * width * MW,
            [pltpu.VMEM((width, lat), bf16), pltpu.VMEM((MW, width), bf16),
             pltpu.VMEM((count, width), bf16)],
        )),
    )
    d_n = sum_far(*sum_near(own, near))
    back = norm_back(tokens, scales[:n], gains[0], d_n)
    parts, first = ring_sum_far(parts)
    gain_total = sum_everywhere(after(gain_part, *first))
    parts = ring_sum_near(parts)
    parts[0], gain_total, d_n = lax.optimization_barrier((parts[0], gain_total, d_n))
    qkv_sum = add(*[t[:, : 3 * MW] for t in parts])
    qkv_blocks = gather_rel(qkv_sum)
    out_blocks = to_owners(add(*[t[:, 3 * MW :] for t in parts]))
    qkv_total, out_total = kernel_call(
        totals_body, place, [*qkv_blocks, *out_blocks],
        [shape(n, 12 * MW, f32), shape(half, width, f32)], n * width,
    )
    residual = jnp.where(
        is_encoder,
        jnp.pad(d_z.astype(f32), ((half, 0), (0, 0))),
        upstream.astype(f32),
    )
    token_grad = (back + residual).astype(bf16)
    return token_grad[None, None], qkv_total[None], out_total[None], gain_total


def solution(mesh):
    fine = Mesh(mesh.devices.reshape(2, 2, 2, 4, 4), ("section", "zl", "core", "y", "x"))
    in_specs = (
        P("section", DP, RENDER, None),
        P("section", DP, None),
        P("section", DP, None),
        P("section", None),
        P(DP, RENDER, None),
    )
    out_specs = (
        P("section", DP, RENDER, None),
        P("section", DP, None),
        P("section", DP, None),
        P("section", None),
    )
    return jax.shard_map(shards, mesh=fine, in_specs=in_specs, out_specs=out_specs, check_vma=False)
```

```python
import math

import jax
import jax.numpy as jnp
from jax import lax
from jax.experimental import pallas as pl
from jax.experimental.pallas import tpu as pltpu
from jax.sharding import Mesh
from jax.sharding import PartitionSpec as P

HD = 128
MY = 2
MW = MY * HD
NORM_EPSILON = 1e-06
FACTOR = HD**-0.5
RENDER = ("zl", "core")
DP = ("y", "x")
SWAP = [(0, 1), (1, 0)]
DIAG = [(0, 3), (1, 2), (2, 1), (3, 0)]
bf16 = jnp.bfloat16
f32 = jnp.float32


def mm(left, right):
    return jnp.dot(left, right, preferred_element_type=f32)


def mm_tn(left, right):
    return lax.dot_general(left, right, (((0,), (0,)), ((), ())), preferred_element_type=f32)


def mm_nt(left, right):
    return lax.dot_general(left, right, (((1,), (1,)), ((), ())), preferred_element_type=f32)


def core_swap(t):
    return lax.ppermute(t, "core", SWAP)


def z_swap(t):
    return lax.ppermute(t, "zl", SWAP)


def gather_rel(t):
    z = z_swap(t)
    c = core_swap(t)
    return [t, c, z, core_swap(z)]


def spread_rel(b):
    return [b[0], core_swap(b[1]), z_swap(b[2]), lax.ppermute(b[3], RENDER, DIAG)]


def sum_near(own, near):
    n = own.shape[0] // 2
    near = core_swap(near)
    return own[:n].astype(f32) + near[:n].astype(f32), add(own[n:], near[n:])


def sum_far(mine, far):
    return (mine + z_swap(far).astype(f32)).astype(bf16)


def add(*terms):
    return sum(t.astype(f32) for t in terms).astype(bf16)


def step(t, stage, k):
    pairs = []
    for core in range(2):
        for y in range(4):
            for x in range(4):
                to = (y, (x + k) % 4) if core == stage else ((y + k) % 4, x)
                pairs.append((core * 16 + y * 4 + x, core * 16 + to[0] * 4 + to[1]))
    return lax.ppermute(t, ("core", "y", "x"), pairs)


def after(t, *others):
    return lax.optimization_barrier((t, *others))[0]


def gather_near(mine):
    near, far, other = [step(mine, 0, k) for k in (1, 2, 3)]
    return jnp.concatenate([mine, near], 0), jnp.concatenate([far, other], 0)


def gather_far(t):
    up = [step(h, 1, 1) for h in t]
    down = [step(h, 1, -1) for h in t[::-1]][::-1]
    return [*t, *up, step(up[0], 1, 1), step(down[1], 1, -1), *down]


def ring_sum_far(blocks):
    own, after, far, before = blocks[:2], blocks[2:4], blocks[4:6], blocks[6:]
    far_up, far_down = step(far[0], 1, 1), step(far[1], 1, -1)
    up = [None, step(after[1], 1, 1)]
    down = [step(before[0], 1, -1), None]
    up[0] = step(add(after[0], far_up), 1, 1)
    down[1] = step(add(before[1], far_down), 1, -1)
    parts = []
    for m in range(4):
        n = own[0].shape[0] // 2
        rows = slice((m % 2) * n, (m % 2 + 1) * n)
        parts.append(add(*[t[m // 2][rows] for t in (own, up, down)]))
    return parts, (up[1], down[0])


def ring_sum_near(parts):
    return add(parts[0], *[step(parts[m], 0, m) for m in (1, 2, 3)])


def cross_section(t, source):
    pairs = [(source * 2 + i, (1 - source) * 2 + 1 - i) for i in range(2)]
    return lax.ppermute(t, ("section", "zl"), pairs)


def sum_everywhere(t):
    peers = 64
    blocks = jnp.broadcast_to(t[None], (peers, *t.shape))
    return lax.all_to_all(blocks, RENDER + DP, 0, 0, tiled=True).sum(axis=0)


def norm_back(values, scale, gain_row, upstream):
    wide = values.astype(f32)
    grad = upstream.astype(f32)
    scaled = grad * gain_row
    inner = jnp.sum(scaled * wide, axis=-1, keepdims=True)
    result = scale * scaled - wide * scale**3 * inner / values.shape[-1]
    return result


def kernel_call(body, place, inputs, outputs, flops, scratch=()):
    moved = sum(t.size * t.dtype.itemsize for t in list(inputs) + list(outputs))
    vmem = pl.BlockSpec(memory_space=pltpu.VMEM)
    held = moved + sum(math.prod(t.shape) * 4 for t in scratch)
    return pl.pallas_call(
        body,
        out_shape=tuple(outputs),
        in_specs=[pl.BlockSpec(memory_space=pltpu.SMEM)] + [vmem] * len(inputs),
        out_specs=(vmem,) * len(outputs),
        scratch_shapes=scratch,
        compiler_params=pltpu.CompilerParams(vmem_limit_bytes=held + 6 * 2**20),
        cost_estimate=pl.CostEstimate(flops=flops, bytes_accessed=moved, transcendentals=0),
    )(place, *inputs)


def shape(rows, cols, dtype=bf16):
    return jax.ShapeDtypeStruct((rows, cols), dtype)


def block(i, n):
    return pl.ds(pl.multiple_of(i * n, n), n)


def head(part, h):
    at = part * MW + h * HD
    return slice(at, at + HD)


def lay_out(dst, blocks, rank, permuted):
    wide = blocks[0].shape[1]
    for j, b in enumerate(blocks):
        n = b.shape[0] // 4
        lanes = slice(j * wide, (j + 1) * wide) if rank is None else block(rank ^ j, wide)
        for i in range(4):
            at = (i ^ j if permuted else i) * n
            dst[i * n : (i + 1) * n, lanes] = b[at : at + n, :]


def out_rows(to, rank):
    return ((to >> 2) ^ rank) * 4 + (to & 3)


def norm_body(place, gain, t0, t1, t2, t3, normed, normed_t, scales):
    n = t0.shape[0]
    for j, t in enumerate((t0, t1, t2, t3)):
        wide = t[...].astype(f32)
        scale = lax.rsqrt(jnp.mean(wide * wide, axis=-1, keepdims=True) + NORM_EPSILON)
        out = (wide * scale * gain[...]).astype(bf16)
        normed[j * n : (j + 1) * n, :] = out
        normed_t[:, j * n : (j + 1) * n] = out.T
        scales[j * n : (j + 1) * n, :] = scale


def holder(place, k, m, sign):
    y, x, first = place[0], place[1], place[2] & 1
    dy, dx = jnp.where(first == 0, k, m), jnp.where(first == 0, m, k)
    return ((y + sign * dy) & 3) * 4 + ((x + sign * dx) & 3)


def project_body(place, normed, *refs):
    w, w_rel, out, enc_o = refs[8:]
    n, wide = refs[0].shape[0] // 2, w.shape[1]
    for k in range(4):
        for m in range(4):
            src, row = refs[2 * k + m // 2], (m % 2) * n
            to = holder(place, k, m, -1)
            w[block(to, n), :] = src[row : row + n, :wide]
            for i in range(2):
                w_rel[block(out_rows(to, place[2]), n // 2), i * MW : (i + 1) * MW] = src[
                    row + i * (n // 2) : row + (i + 1) * (n // 2), wide:
                ]
    for at in range(0, w.shape[1], 256):
        out[:, at : at + 256] = mm(normed[...], w[:, at : at + 256]).astype(bf16)
    for h in range(MY):
        q = latent_rows(out, head(0, h))
        p = softmax(mm_nt(q, out[:, head(1, h)]) * FACTOR)
        enc_o[:, head(0, h)] = mm(p.astype(bf16), out[:, head(2, h)]).astype(bf16)


def upstream_body(place, u0, u1, u2, u3, b0, b1, b2, b3, up_o, w_row):
    lay_out(w_row, (b0, b1, b2, b3), place[2], False)
    n = u0.shape[0]
    for j, u in enumerate((u0, u1, u2, u3)):
        up_o[j * n : (j + 1) * n, :] = mm_nt(u[...], w_row[...]).astype(bf16)


def latent_rows(ref, lanes):
    half = ref.shape[0] // 8
    return jnp.concatenate(
        [ref[(2 * i + 1) * half : (2 * i + 2) * half, lanes] for i in range(4)], 0
    )


def softmax(scores):
    raised = jnp.exp(scores - jnp.max(scores, axis=-1, keepdims=True))
    return raised * (1.0 / jnp.sum(raised, axis=-1, keepdims=True))


def latents_body(place, t0, t1, t2, t3, o0, o1, o2, o3, w_rel, z, o_all):
    rank = place[2]
    lay_out(o_all, (o0, o1, o2, o3), None, True)
    half, cols = t0.shape[0] // 2, z.shape[1]
    added = mm(o_all[...], w_rel[...])
    for j, t in enumerate((t0, t1, t2, t3)):
        rows = slice(j * half, (j + 1) * half)
        z[rows, :] = (t[half:, block(rank, cols)].astype(f32) + added[rows]).astype(bf16)


def weight_parts(place, normed_t, d_proj, d_out, outs, extra):
    n = outs[0].shape[0] // 2
    wide, m_out = d_proj.shape[1], n // 2
    for k in range(4):
        for m in range(4):
            to = holder(place, k, m, 1)
            part = mm(normed_t[block(to, n), :], d_proj[...])
            o, row = outs[2 * k + m // 2], (m % 2) * n
            if extra is not None:
                nz_t, d_kvz = extra
                more = mm(nz_t[block(to, n), :], d_kvz[...])
                part = jnp.concatenate([part[:, :MW], part[:, MW:] + more], 1)
            o[row : row + n, :wide] = part.astype(bf16)
            for i in range(2):
                o[row + i * m_out : row + (i + 1) * m_out, wide:] = d_out[
                    block(out_rows(to, place[2]), m_out), i * MW : (i + 1) * MW
                ]


def encoder_back_body(place, d0, d1, d2, d3, w_row, proj, normed_t, w, o_all, scales, *refs):
    rows, own, near, gain, outs = refs[:4], refs[4], refs[5], refs[6], refs[7:15]
    d_proj, d_z, up, d_out = refs[15:]
    lat = d_z.shape[0]
    half = lat // 4
    for j, d in enumerate((d0, d1, d2, d3)):
        d_z[j * half : (j + 1) * half, :] = d[...]
    up[...] = mm_nt(d_z[...], w_row[...]).astype(bf16)
    for h in range(MY):
        q = latent_rows(proj, head(0, h))
        k, v = proj[:, head(1, h)], proj[:, head(2, h)]
        u = up[:, head(0, h)]
        p = softmax(mm_nt(q, k) * FACTOR)
        dp = mm_nt(u, v)
        delta = jnp.sum(dp * p, axis=-1, keepdims=True)
        ds = (p * (dp - delta) * FACTOR).astype(bf16)
        dq = mm(ds, k).astype(bf16)
        for i in range(4):
            at = 2 * i * half
            d_proj[at : at + half, head(0, h)] = jnp.zeros((half, HD), bf16)
            d_proj[at + half : at + 2 * half, head(0, h)] = dq[i * half : (i + 1) * half]
        d_proj[:, head(1, h)] = mm_tn(ds, q).astype(bf16)
        d_proj[:, head(2, h)] = mm_tn(p.astype(bf16), u).astype(bf16)
    d_out[...] = mm_tn(o_all[...], d_z[:, block(place[2], d_out.shape[1])]).astype(bf16)
    weight_parts(place, normed_t, d_proj, d_out, outs, None)
    gain[...] = jnp.zeros(gain.shape, f32)
    sums_for_render(d_proj, w, 0, own, near, rows, scales, gain)


def decoder_back_body(place, d_proj, d_kvz, nz, normed_t, w, *refs):
    ups, os, z_gain, scales, rows = refs[:4], refs[4:8], refs[8], refs[9], refs[10:14]
    own, near, gain, outs, (nz_t, o_all, d_out, up) = *refs[14:17], refs[17:25], refs[25:]
    for at in range(0, nz.shape[1], 512):
        nz_t[at : at + 512, :] = nz[:, at : at + 512].T
    lay_out(o_all, os, None, True)
    n, cols = ups[0].shape[0], d_out.shape[1]
    for j, u in enumerate(ups):
        up[j * n : (j + 1) * n, :] = u[:, block(place[2], cols)]
    d_out[...] = mm_tn(o_all[...], up[...]).astype(bf16)
    weight_parts(place, normed_t, d_proj, d_out, outs, (nz_t, d_kvz))
    gain[...] = z_gain[...]
    sums_for_render(d_proj, w, 0, own, near, rows, scales, gain)


def decoder_body(place, gain, z0, z1, z2, z3, w, proj, up, *refs):
    out, d_proj, d_kvz, nz, scales, z_own, own, near, z_gain, z, kvz, acc = refs
    lat, width = z.shape
    half = lat // 4
    lay_out(z, (z0, z1, z2, z3), place[2], True)
    z_own[...] = z[:half, :]
    for i in range(4):
        rows = slice(i * half, (i + 1) * half)
        wide = z[rows, :].astype(f32)
        scale = lax.rsqrt(jnp.mean(wide * wide, axis=-1, keepdims=True) + NORM_EPSILON)
        nz[rows, :] = (wide * scale * gain[...]).astype(bf16)
        scales[rows, :] = scale
    kvz[...] = mm(nz[...], w[:, MW:]).astype(bf16)
    views = proj.shape[0] // 128
    for h in range(MY):
        kz, vz = kvz[:, head(0, h)], kvz[:, head(1, h)]
        for i in range(views):
            rows = slice(i * 128, (i + 1) * 128)
            q, k, v = [proj[rows, head(part, h)] for part in range(3)]
            u = up[rows, head(0, h)]
            s = mm_nt(q, kz) * FACTOR
            t = mm_nt(q, k) * FACTOR
            top = jnp.maximum(
                jnp.max(s, axis=-1, keepdims=True), jnp.max(t, axis=-1, keepdims=True)
            )
            s, t = jnp.exp(s - top), jnp.exp(t - top)
            total = jnp.sum(s, axis=-1, keepdims=True) + jnp.sum(t, axis=-1, keepdims=True)
            s, t = s * (1.0 / total), t * (1.0 / total)
            sb, tb = s.astype(bf16), t.astype(bf16)
            out[rows, head(0, h)] = (mm(sb, vz) + mm(tb, v)).astype(bf16)
            ds, dt = mm_nt(u, vz), mm_nt(u, v)
            delta = jnp.sum(ds * s, axis=-1, keepdims=True) + jnp.sum(dt * t, axis=-1, keepdims=True)
            ds = (s * (ds - delta) * FACTOR).astype(bf16)
            dt = (t * (dt - delta) * FACTOR).astype(bf16)
            d_proj[rows, head(0, h)] = (mm(ds, kz) + mm(dt, k)).astype(bf16)
            d_proj[rows, head(1, h)] = mm_tn(dt, q).astype(bf16)
            d_proj[rows, head(2, h)] = mm_tn(tb, u).astype(bf16)
            dkz, dvz = mm_tn(ds, q), mm_tn(sb, u)
            if i > 0:
                dkz, dvz = dkz + acc[:, head(0, h)], dvz + acc[:, head(1, h)]
            acc[:, head(0, h)], acc[:, head(1, h)] = dkz, dvz
    d_kvz[...] = acc[...].astype(bf16)
    z_gain[...] = jnp.zeros(z_gain.shape, f32)
    z_rows = [z.at[i * half : (i + 1) * half, :] for i in range(4)]
    sums_for_render(d_kvz, w, MW, own, near, z_rows, scales, z_gain)


def sums_for_render(grads, w, first, own, near, rows, scales, gain):
    n = grads.shape[0] // 4
    for at in range(0, w.shape[0], 512):
        cols = slice(at, at + 512)
        got = mm_nt(grads[...], w[cols, first:])
        for i, r in enumerate(rows):
            part = got[i * n : (i + 1) * n]
            term = part * (r[:, cols].astype(f32) * scales[i * n : (i + 1) * n, :])
            gain[:, cols] += jnp.sum(term, axis=0, keepdims=True)
            half = slice(i // 2 * n, (i // 2 + 1) * n)
            (near if i % 2 else own)[half, cols] = part.astype(bf16)


def totals_body(place, t0, t1, t2, t3, qkv, out):
    half = out.shape[0]
    for j, t in enumerate((t0, t1, t2, t3)):
        rank = place[2] ^ j
        for part in range(3):
            qkv[:, block(part * 4 + rank, MW)] = t[:, part * MW : (part + 1) * MW].astype(f32)
        for i in range(2):
            rows = slice(i * half, (i + 1) * half)
            out[:, block(rank * 2 + i, MW)] = t[rows, 3 * MW :].astype(f32)


def shards(section_tokens, w_qkv, w_out, gains, cotangent):
    tokens = section_tokens[0, 0]
    upstream = cotangent[0]
    rank = lax.axis_index("zl") * 2 + lax.axis_index("core")
    place = jnp.stack([lax.axis_index("y"), lax.axis_index("x"), rank]).astype(jnp.int32)
    is_encoder = lax.axis_index("section") == 0
    n, width = tokens.shape
    half, cols, count, lat = n // 2, width // 4, 4 * n, 2 * n

    own_cols = [
        lax.dynamic_slice_in_dim(w_qkv[0], part * 4 * MW + rank * MW, MW, 1) for part in range(3)
    ]
    own_out = [lax.dynamic_slice_in_dim(w_out[0], rank * cols + i * MW, MW, 1) for i in range(2)]
    near = gather_near(jnp.concatenate([*own_cols, jnp.concatenate(own_out, 0)], 1))
    rows = gather_rel(tokens)
    near, rows[2] = lax.optimization_barrier((near, rows[2]))
    w_parts = gather_far(near)
    normed, normed_t, scales = kernel_call(
        norm_body, place, [gains, *rows],
        [shape(count, width), shape(width, count), shape(count, 1, f32)], 8 * count * width,
    )
    ups = gather_rel(after(upstream, w_parts[2]))
    w_h, w_rel, projected, enc_o = kernel_call(
        project_body, place, [normed, *w_parts],
        [shape(width, 3 * MW), shape(4 * MW, cols), shape(count, 3 * MW), shape(lat, MW)],
        6 * count * width * MW + 4 * lat * count * MW,
    )
    w_row_blocks = spread_rel([w_rel[j * MW : (j + 1) * MW] for j in range(4)])
    enc_blocks = gather_rel(enc_o)
    enc_blocks[1], ups = lax.optimization_barrier((enc_blocks[1], ups))
    z_cols, enc_all = kernel_call(
        latents_body, place, [*rows, *enc_blocks, w_rel],
        [shape(lat, cols), shape(lat, 4 * MW)], 8 * lat * cols * MW,
    )
    z_crossed = cross_section(z_cols, 0)
    up_o, w_row = kernel_call(
        upstream_body, place, [*ups, *w_row_blocks],
        [shape(count, MW), shape(MW, width)], 2 * count * width * MW,
    )
    z_blocks = gather_rel(after(z_crossed, up_o))
    z_blocks = z_blocks[2:] + z_blocks[:2]

    decoder_shapes = [
        shape(count, MW), shape(count, 3 * MW), shape(lat, 2 * MW), shape(lat, width),
        shape(lat, 1, f32), shape(half, width), shape(2 * half, width), shape(2 * half, width),
        shape(1, width, f32),
    ]
    dec_o, d_proj, d_kvz, nz, z_scale, z_own, own, near, z_gain = lax.cond(
        is_encoder,
        lambda: tuple(jnp.zeros(s.shape, s.dtype) for s in decoder_shapes),
        lambda: tuple(kernel_call(
            decoder_body, place, [gains, *z_blocks, w_h, projected, up_o], decoder_shapes,
            8 * lat * width * MW + 12 * count * (lat + 128) * MW,
            [pltpu.VMEM((lat, width), bf16), pltpu.VMEM((lat, 2 * MW), bf16),
             pltpu.VMEM((lat, 2 * MW), f32)],
        )),
    )
    d_nz = sum_far(*sum_near(own, near))
    d_z = norm_back(z_own, z_scale[:half], gains[0], d_nz)
    d_z = d_z.astype(bf16)
    dec_blocks = gather_rel(after(dec_o, d_z))
    d_z = cross_section(d_z, 1)
    d_z_blocks = gather_rel(after(d_z, *dec_blocks))
    d_z_blocks = d_z_blocks[2:] + d_z_blocks[:2]
    d_z = d_z_blocks[0]

    back_shapes = [shape(2 * n, width)] * 2 + [shape(1, width, f32)] + [shape(2 * n, width // 2)] * 8
    back_flops = 12 * width * count * MW + 2 * lat * width * MW
    own, near, gain_part, *parts = lax.cond(
        is_encoder,
        lambda: tuple(kernel_call(
            encoder_back_body, place, [*d_z_blocks, w_row, projected, normed_t, w_h, enc_all, scales, *rows],
            back_shapes, back_flops + 2 * lat * width * MW + 10 * lat * count * MW,
            [pltpu.VMEM((count, 3 * MW), bf16), pltpu.VMEM((lat, width), bf16),
             pltpu.VMEM((lat, MW), bf16), pltpu.VMEM((4 * MW, cols), bf16)],
        )),
        lambda: tuple(kernel_call(
            decoder_back_body, place, [d_proj, d_kvz, nz, normed_t, w_h, *ups, *dec_blocks, z_gain, scales, *rows],
            back_shapes, back_flops + 4 * lat * width * MW,
            [pltpu.VMEM((width, lat), bf16), pltpu.VMEM((count, 4 * MW), bf16),
             pltpu.VMEM((4 * MW, cols), bf16), pltpu.VMEM((count, cols), bf16)],
        )),
    )
    d_n, far = sum_near(own, near)
    d_n = sum_far(d_n, far)
    back = norm_back(tokens, scales[:n], gains[0], d_n)
    parts, first = ring_sum_far(parts)
    gain_total = sum_everywhere(after(gain_part, far, *first))
    sums = ring_sum_near(parts)
    sums, gain_total, d_n = lax.optimization_barrier((sums, gain_total, d_n))
    qkv_total, out_total = kernel_call(
        totals_body, place, gather_rel(sums),
        [shape(n, 12 * MW, f32), shape(half, width, f32)], n * width,
    )
    residual = jnp.where(
        is_encoder,
        jnp.pad(d_z.astype(f32), ((half, 0), (0, 0))),
        upstream.astype(f32),
    )
    token_grad = (back + residual).astype(bf16)
    return token_grad[None, None], qkv_total[None], out_total[None], gain_total


def solution(mesh):
    fine = Mesh(mesh.devices.reshape(2, 2, 2, 4, 4), ("section", "zl", "core", "y", "x"))
    in_specs = (
        P("section", DP, RENDER, None),
        P("section", DP, None),
        P("section", DP, None),
        P("section", None),
        P(DP, RENDER, None),
    )
    out_specs = (
        P("section", DP, RENDER, None),
        P("section", DP, None),
        P("section", DP, None),
        P("section", None),
    )
    return jax.shard_map(shards, mesh=fine, in_specs=in_specs, out_specs=out_specs, check_vma=False)
```

```python
import math

import jax
import jax.numpy as jnp
from jax import lax
from jax.experimental import pallas as pl
from jax.experimental.pallas import tpu as pltpu
from jax.sharding import Mesh
from jax.sharding import PartitionSpec as P

HD = 128
MY = 2
MW = MY * HD
NORM_EPSILON = 1e-06
FACTOR = HD**-0.5
RENDER = ("zl", "core")
DP = ("y", "x")
SWAP = [(0, 1), (1, 0)]
DIAG = [(0, 3), (1, 2), (2, 1), (3, 0)]
bf16 = jnp.bfloat16
f32 = jnp.float32


def mm(left, right):
    return jnp.dot(left, right, preferred_element_type=f32)


def mm_tn(left, right):
    return lax.dot_general(left, right, (((0,), (0,)), ((), ())), preferred_element_type=f32)


def mm_nt(left, right):
    return lax.dot_general(left, right, (((1,), (1,)), ((), ())), preferred_element_type=f32)


def core_swap(t):
    return lax.ppermute(t, "core", SWAP)


def z_swap(t):
    return lax.ppermute(t, "zl", SWAP)


def gather_rel(t):
    z = z_swap(t)
    c = core_swap(t)
    return [t, c, z, core_swap(z)]


def spread_rel(b):
    return [b[0], core_swap(b[1]), z_swap(b[2]), lax.ppermute(b[3], RENDER, DIAG)]


def sum_near(own, near):
    n = own.shape[0] // 2
    near = core_swap(near)
    return own[:n].astype(f32) + near[:n].astype(f32), add(own[n:], near[n:])


def sum_far(mine, far):
    return (mine + z_swap(far).astype(f32)).astype(bf16)


def add(*terms):
    return sum(t.astype(f32) for t in terms).astype(bf16)


def step(t, stage, k):
    pairs = []
    for core in range(2):
        for y in range(4):
            for x in range(4):
                to = (y, (x + k) % 4) if core == stage else ((y + k) % 4, x)
                pairs.append((core * 16 + y * 4 + x, core * 16 + to[0] * 4 + to[1]))
    return lax.ppermute(t, ("core", "y", "x"), pairs)


def after(t, *others):
    return lax.optimization_barrier((t, *others))[0]


def gather_near(mine):
    near, far, other = [step(mine, 0, k) for k in (1, 2, 3)]
    return jnp.concatenate([mine, near], 0), jnp.concatenate([far, other], 0)


def gather_far(t):
    up = [step(h, 1, 1) for h in t]
    down = [step(h, 1, -1) for h in t[::-1]][::-1]
    return [*t, *up, step(up[0], 1, 1), step(down[1], 1, -1), *down]


def ring_sum_far(blocks):
    own, after, far, before = blocks[:2], blocks[2:4], blocks[4:6], blocks[6:]
    far_up, far_down = step(far[0], 1, 1), step(far[1], 1, -1)
    up = [None, step(after[1], 1, 1)]
    down = [step(before[0], 1, -1), None]
    up[0] = step(add(after[0], far_up), 1, 1)
    down[1] = step(add(before[1], far_down), 1, -1)
    parts = []
    for m in range(4):
        n = own[0].shape[0] // 2
        rows = slice((m % 2) * n, (m % 2 + 1) * n)
        parts.append(add(*[t[m // 2][rows] for t in (own, up, down)]))
    return parts, (up[1], down[0])


def ring_sum_near(parts):
    return add(parts[0], *[step(parts[m], 0, m) for m in (1, 2, 3)])


def cross_section(t, source):
    pairs = [(source * 2 + i, (1 - source) * 2 + 1 - i) for i in range(2)]
    return lax.ppermute(t, ("section", "zl"), pairs)


def sum_everywhere(t):
    peers = 64
    blocks = jnp.broadcast_to(t[None], (peers, *t.shape))
    return lax.all_to_all(blocks, RENDER + DP, 0, 0, tiled=True).sum(axis=0)


def norm_back(values, scale, gain_row, upstream):
    wide = values.astype(f32)
    grad = upstream.astype(f32)
    scaled = grad * gain_row
    inner = jnp.sum(scaled * wide, axis=-1, keepdims=True)
    result = scale * scaled - wide * scale**3 * inner / values.shape[-1]
    return result


def kernel_call(body, place, inputs, outputs, flops, scratch=()):
    moved = sum(t.size * t.dtype.itemsize for t in list(inputs) + list(outputs))
    vmem = pl.BlockSpec(memory_space=pltpu.VMEM)
    held = moved + sum(math.prod(t.shape) * 4 for t in scratch)
    return pl.pallas_call(
        body,
        out_shape=tuple(outputs),
        in_specs=[pl.BlockSpec(memory_space=pltpu.SMEM)] + [vmem] * len(inputs),
        out_specs=(vmem,) * len(outputs),
        scratch_shapes=scratch,
        compiler_params=pltpu.CompilerParams(vmem_limit_bytes=held + 6 * 2**20),
        cost_estimate=pl.CostEstimate(flops=flops, bytes_accessed=moved, transcendentals=0),
    )(place, *inputs)


def shape(rows, cols, dtype=bf16):
    return jax.ShapeDtypeStruct((rows, cols), dtype)


def block(i, n):
    return pl.ds(pl.multiple_of(i * n, n), n)


def head(part, h):
    at = part * MW + h * HD
    return slice(at, at + HD)


def lay_out(dst, blocks, rank, permuted):
    wide = blocks[0].shape[1]
    for j, b in enumerate(blocks):
        n = b.shape[0] // 4
        lanes = slice(j * wide, (j + 1) * wide) if rank is None else block(rank ^ j, wide)
        for i in range(4):
            at = (i ^ j if permuted else i) * n
            dst[i * n : (i + 1) * n, lanes] = b[at : at + n, :]


def out_rows(to, rank):
    return ((to >> 2) ^ rank) * 4 + (to & 3)


def norm_body(place, gain, t0, t1, t2, t3, normed, normed_t, scales):
    n = t0.shape[0]
    for j, t in enumerate((t0, t1, t2, t3)):
        wide = t[...].astype(f32)
        scale = lax.rsqrt(jnp.mean(wide * wide, axis=-1, keepdims=True) + NORM_EPSILON)
        out = (wide * scale * gain[...]).astype(bf16)
        normed[j * n : (j + 1) * n, :] = out
        normed_t[:, j * n : (j + 1) * n] = out.T
        scales[j * n : (j + 1) * n, :] = scale


def holder(place, k, m, sign):
    y, x, first = place[0], place[1], place[2] & 1
    dy, dx = jnp.where(first == 0, k, m), jnp.where(first == 0, m, k)
    return ((y + sign * dy) & 3) * 4 + ((x + sign * dx) & 3)


def project_body(place, normed, *refs):
    w, w_rel, out, enc_o = refs[8:]
    n, wide = refs[0].shape[0] // 2, w.shape[1]
    for k in range(4):
        for m in range(4):
            src, row = refs[2 * k + m // 2], (m % 2) * n
            to = holder(place, k, m, -1)
            w[block(to, n), :] = src[row : row + n, :wide]
            for i in range(2):
                w_rel[block(out_rows(to, place[2]), n // 2), i * MW : (i + 1) * MW] = src[
                    row + i * (n // 2) : row + (i + 1) * (n // 2), wide:
                ]
    for at in range(0, w.shape[1], 256):
        out[:, at : at + 256] = mm(normed[...], w[:, at : at + 256]).astype(bf16)
    for h in range(MY):
        q = latent_rows(out, head(0, h))
        p = softmax(mm_nt(q, out[:, head(1, h)]) * FACTOR)
        enc_o[:, head(0, h)] = mm(p.astype(bf16), out[:, head(2, h)]).astype(bf16)


def upstream_body(place, u0, u1, u2, u3, b0, b1, b2, b3, up_o, w_row):
    lay_out(w_row, (b0, b1, b2, b3), place[2], False)
    n = u0.shape[0]
    for j, u in enumerate((u0, u1, u2, u3)):
        up_o[j * n : (j + 1) * n, :] = mm_nt(u[...], w_row[...]).astype(bf16)


def latent_rows(ref, lanes):
    half = ref.shape[0] // 8
    return jnp.concatenate(
        [ref[(2 * i + 1) * half : (2 * i + 2) * half, lanes] for i in range(4)], 0
    )


def softmax(scores):
    raised = jnp.exp(scores - jnp.max(scores, axis=-1, keepdims=True))
    return raised * (1.0 / jnp.sum(raised, axis=-1, keepdims=True))


def latents_body(place, t0, t1, t2, t3, o0, o1, o2, o3, w_rel, z, o_all):
    rank = place[2]
    lay_out(o_all, (o0, o1, o2, o3), None, True)
    half, cols = t0.shape[0] // 2, z.shape[1]
    added = mm(o_all[...], w_rel[...])
    for j, t in enumerate((t0, t1, t2, t3)):
        rows = slice(j * half, (j + 1) * half)
        z[rows, :] = (t[half:, block(rank, cols)].astype(f32) + added[rows]).astype(bf16)


def weight_parts(place, normed_t, d_proj, d_out, outs, extra):
    n = outs[0].shape[0] // 2
    wide, m_out = d_proj.shape[1], n // 2
    for k in range(4):
        for m in range(4):
            to = holder(place, k, m, 1)
            part = mm(normed_t[block(to, n), :], d_proj[...])
            o, row = outs[2 * k + m // 2], (m % 2) * n
            if extra is not None:
                nz_t, d_kvz = extra
                more = mm(nz_t[block(to, n), :], d_kvz[...])
                part = jnp.concatenate([part[:, :MW], part[:, MW:] + more], 1)
            o[row : row + n, :wide] = part.astype(bf16)
            for i in range(2):
                o[row + i * m_out : row + (i + 1) * m_out, wide:] = d_out[
                    block(out_rows(to, place[2]), m_out), i * MW : (i + 1) * MW
                ]


def encoder_back_body(place, d0, d1, d2, d3, w_row, proj, normed_t, w, o_all, scales, *refs):
    rows, own, near, gain, outs = refs[:4], refs[4], refs[5], refs[6], refs[7:15]
    d_proj, d_z, up, d_out = refs[15:]
    lat = d_z.shape[0]
    half = lat // 4
    for j, d in enumerate((d0, d1, d2, d3)):
        d_z[j * half : (j + 1) * half, :] = d[...]
    up[...] = mm_nt(d_z[...], w_row[...]).astype(bf16)
    for h in range(MY):
        q = latent_rows(proj, head(0, h))
        k, v = proj[:, head(1, h)], proj[:, head(2, h)]
        u = up[:, head(0, h)]
        p = softmax(mm_nt(q, k) * FACTOR)
        dp = mm_nt(u, v)
        delta = jnp.sum(dp * p, axis=-1, keepdims=True)
        ds = (p * (dp - delta) * FACTOR).astype(bf16)
        dq = mm(ds, k).astype(bf16)
        for i in range(4):
            at = 2 * i * half
            d_proj[at : at + half, head(0, h)] = jnp.zeros((half, HD), bf16)
            d_proj[at + half : at + 2 * half, head(0, h)] = dq[i * half : (i + 1) * half]
        d_proj[:, head(1, h)] = mm_tn(ds, q).astype(bf16)
        d_proj[:, head(2, h)] = mm_tn(p.astype(bf16), u).astype(bf16)
    d_out[...] = mm_tn(o_all[...], d_z[:, block(place[2], d_out.shape[1])]).astype(bf16)
    weight_parts(place, normed_t, d_proj, d_out, outs, None)
    gain[...] = jnp.zeros(gain.shape, f32)
    sums_for_render(d_proj, w, 0, own, near, rows, scales, gain)


def decoder_back_body(place, d_proj, d_kvz, nz, normed_t, w, *refs):
    ups, os, z_gain, scales, rows = refs[:4], refs[4:8], refs[8], refs[9], refs[10:14]
    own, near, gain, outs, (nz_t, o_all, d_out, up) = *refs[14:17], refs[17:25], refs[25:]
    for at in range(0, nz.shape[1], 512):
        nz_t[at : at + 512, :] = nz[:, at : at + 512].T
    lay_out(o_all, os, None, True)
    n, cols = ups[0].shape[0], d_out.shape[1]
    for j, u in enumerate(ups):
        up[j * n : (j + 1) * n, :] = u[:, block(place[2], cols)]
    d_out[...] = mm_tn(o_all[...], up[...]).astype(bf16)
    weight_parts(place, normed_t, d_proj, d_out, outs, (nz_t, d_kvz))
    gain[...] = z_gain[...]
    sums_for_render(d_proj, w, 0, own, near, rows, scales, gain)


def decoder_body(place, gain, z0, z1, z2, z3, w, proj, up, *refs):
    out, d_proj, d_kvz, nz, scales, z_own, own, near, z_gain, z, kvz, acc = refs
    lat, width = z.shape
    half = lat // 4
    lay_out(z, (z0, z1, z2, z3), place[2], True)
    z_own[...] = z[:half, :]
    for i in range(4):
        rows = slice(i * half, (i + 1) * half)
        wide = z[rows, :].astype(f32)
        scale = lax.rsqrt(jnp.mean(wide * wide, axis=-1, keepdims=True) + NORM_EPSILON)
        nz[rows, :] = (wide * scale * gain[...]).astype(bf16)
        scales[rows, :] = scale
    kvz[...] = mm(nz[...], w[:, MW:]).astype(bf16)
    views = proj.shape[0] // 128
    for h in range(MY):
        kz, vz = kvz[:, head(0, h)], kvz[:, head(1, h)]
        for i in range(views):
            rows = slice(i * 128, (i + 1) * 128)
            q, k, v = [proj[rows, head(part, h)] for part in range(3)]
            u = up[rows, head(0, h)]
            s = mm_nt(q, kz) * FACTOR
            t = mm_nt(q, k) * FACTOR
            top = jnp.maximum(
                jnp.max(s, axis=-1, keepdims=True), jnp.max(t, axis=-1, keepdims=True)
            )
            s, t = jnp.exp(s - top), jnp.exp(t - top)
            total = jnp.sum(s, axis=-1, keepdims=True) + jnp.sum(t, axis=-1, keepdims=True)
            s, t = s * (1.0 / total), t * (1.0 / total)
            sb, tb = s.astype(bf16), t.astype(bf16)
            out[rows, head(0, h)] = (mm(sb, vz) + mm(tb, v)).astype(bf16)
            ds, dt = mm_nt(u, vz), mm_nt(u, v)
            delta = jnp.sum(ds * s, axis=-1, keepdims=True) + jnp.sum(dt * t, axis=-1, keepdims=True)
            ds = (s * (ds - delta) * FACTOR).astype(bf16)
            dt = (t * (dt - delta) * FACTOR).astype(bf16)
            d_proj[rows, head(0, h)] = (mm(ds, kz) + mm(dt, k)).astype(bf16)
            d_proj[rows, head(1, h)] = mm_tn(dt, q).astype(bf16)
            d_proj[rows, head(2, h)] = mm_tn(tb, u).astype(bf16)
            dkz, dvz = mm_tn(ds, q), mm_tn(sb, u)
            if i > 0:
                dkz, dvz = dkz + acc[:, head(0, h)], dvz + acc[:, head(1, h)]
            acc[:, head(0, h)], acc[:, head(1, h)] = dkz, dvz
    d_kvz[...] = acc[...].astype(bf16)
    z_gain[...] = jnp.zeros(z_gain.shape, f32)
    z_rows = [z.at[i * half : (i + 1) * half, :] for i in range(4)]
    sums_for_render(d_kvz, w, MW, own, near, z_rows, scales, z_gain)


def sums_for_render(grads, w, first, own, near, rows, scales, gain):
    n = grads.shape[0] // 4
    for at in range(0, w.shape[0], 512):
        cols = slice(at, at + 512)
        got = mm_nt(grads[...], w[cols, first:])
        for i, r in enumerate(rows):
            part = got[i * n : (i + 1) * n]
            term = part * (r[:, cols].astype(f32) * scales[i * n : (i + 1) * n, :])
            gain[:, cols] += jnp.sum(term, axis=0, keepdims=True)
            half = slice(i // 2 * n, (i // 2 + 1) * n)
            (near if i % 2 else own)[half, cols] = part.astype(bf16)


def totals_body(place, t0, t1, t2, t3, qkv, out):
    half = out.shape[0]
    for j, t in enumerate((t0, t1, t2, t3)):
        rank = place[2] ^ j
        for part in range(3):
            qkv[:, block(part * 4 + rank, MW)] = t[:, part * MW : (part + 1) * MW].astype(f32)
        for i in range(2):
            rows = slice(i * half, (i + 1) * half)
            out[:, block(rank * 2 + i, MW)] = t[rows, 3 * MW :].astype(f32)


def shards(section_tokens, w_qkv, w_out, gains, cotangent):
    tokens = section_tokens[0, 0]
    upstream = cotangent[0]
    rank = lax.axis_index("zl") * 2 + lax.axis_index("core")
    place = jnp.stack([lax.axis_index("y"), lax.axis_index("x"), rank]).astype(jnp.int32)
    is_encoder = lax.axis_index("section") == 0
    n, width = tokens.shape
    half, cols, count, lat = n // 2, width // 4, 4 * n, 2 * n

    own_cols = [
        lax.dynamic_slice_in_dim(w_qkv[0], part * 4 * MW + rank * MW, MW, 1) for part in range(3)
    ]
    own_out = [lax.dynamic_slice_in_dim(w_out[0], rank * cols + i * MW, MW, 1) for i in range(2)]
    near = gather_near(jnp.concatenate([*own_cols, jnp.concatenate(own_out, 0)], 1))
    rows = gather_rel(tokens)
    near, rows[2] = lax.optimization_barrier((near, rows[2]))
    w_parts = gather_far(near)
    normed, normed_t, scales = kernel_call(
        norm_body, place, [gains, *rows],
        [shape(count, width), shape(width, count), shape(count, 1, f32)], 8 * count * width,
    )
    ups = gather_rel(after(upstream, w_parts[2]))
    w_h, w_rel, projected, enc_o = kernel_call(
        project_body, place, [normed, *w_parts],
        [shape(width, 3 * MW), shape(4 * MW, cols), shape(count, 3 * MW), shape(lat, MW)],
        6 * count * width * MW + 4 * lat * count * MW,
    )
    w_row_blocks = spread_rel([w_rel[j * MW : (j + 1) * MW] for j in range(4)])
    enc_blocks = gather_rel(enc_o)
    enc_blocks[1], ups = lax.optimization_barrier((enc_blocks[1], ups))
    z_cols, enc_all = kernel_call(
        latents_body, place, [*rows, *enc_blocks, w_rel],
        [shape(lat, cols), shape(lat, 4 * MW)], 8 * lat * cols * MW,
    )
    z_crossed = cross_section(z_cols, 0)
    up_o, w_row = kernel_call(
        upstream_body, place, [*ups, *w_row_blocks],
        [shape(count, MW), shape(MW, width)], 2 * count * width * MW,
    )
    z_blocks = gather_rel(after(z_crossed, up_o))
    z_blocks = z_blocks[2:] + z_blocks[:2]

    decoder_shapes = [
        shape(count, MW), shape(count, 3 * MW), shape(lat, 2 * MW), shape(lat, width),
        shape(lat, 1, f32), shape(half, width), shape(2 * half, width), shape(2 * half, width),
        shape(1, width, f32),
    ]
    dec_o, d_proj, d_kvz, nz, z_scale, z_own, own, near, z_gain = lax.cond(
        is_encoder,
        lambda: tuple(jnp.zeros(s.shape, s.dtype) for s in decoder_shapes),
        lambda: tuple(kernel_call(
            decoder_body, place, [gains, *z_blocks, w_h, projected, up_o], decoder_shapes,
            8 * lat * width * MW + 12 * count * (lat + 128) * MW,
            [pltpu.VMEM((lat, width), bf16), pltpu.VMEM((lat, 2 * MW), bf16),
             pltpu.VMEM((lat, 2 * MW), f32)],
        )),
    )
    d_nz = sum_far(*sum_near(own, near))
    d_z = norm_back(z_own, z_scale[:half], gains[0], d_nz)
    d_z = d_z.astype(bf16)
    dec_blocks = gather_rel(after(dec_o, d_z))
    d_z = cross_section(d_z, 1)
    d_z_blocks = gather_rel(after(d_z, *dec_blocks))
    d_z_blocks = d_z_blocks[2:] + d_z_blocks[:2]
    d_z = d_z_blocks[0]

    back_shapes = [shape(2 * n, width)] * 2 + [shape(1, width, f32)] + [shape(2 * n, width // 2)] * 8
    back_flops = 12 * width * count * MW + 2 * lat * width * MW
    own, near, gain_part, *parts = lax.cond(
        is_encoder,
        lambda: tuple(kernel_call(
            encoder_back_body, place, [*d_z_blocks, w_row, projected, normed_t, w_h, enc_all, scales, *rows],
            back_shapes, back_flops + 2 * lat * width * MW + 10 * lat * count * MW,
            [pltpu.VMEM((count, 3 * MW), bf16), pltpu.VMEM((lat, width), bf16),
             pltpu.VMEM((lat, MW), bf16), pltpu.VMEM((4 * MW, cols), bf16)],
        )),
        lambda: tuple(kernel_call(
            decoder_back_body, place, [d_proj, d_kvz, nz, normed_t, w_h, *ups, *dec_blocks, z_gain, scales, *rows],
            back_shapes, back_flops + 4 * lat * width * MW,
            [pltpu.VMEM((width, lat), bf16), pltpu.VMEM((count, 4 * MW), bf16),
             pltpu.VMEM((4 * MW, cols), bf16), pltpu.VMEM((count, cols), bf16)],
        )),
    )
    d_n, far = sum_near(own, near)
    parts[2:4], far = lax.optimization_barrier((parts[2:4], far))
    d_n = sum_far(d_n, far)
    parts, first = ring_sum_far(parts)
    gain_total = sum_everywhere(after(gain_part, *first))
    parts[0] = after(parts[0], d_n)
    sums = ring_sum_near(parts)
    sums_far = after(z_swap(sums), gain_total)
    qkv_total, out_total = kernel_call(
        totals_body, place, [sums, core_swap(sums), sums_far, core_swap(sums_far)],
        [shape(n, 12 * MW, f32), shape(half, width, f32)], n * width,
    )
    back = norm_back(tokens, scales[:n], gains[0], d_n)
    residual = jnp.where(
        is_encoder,
        jnp.pad(d_z.astype(f32), ((half, 0), (0, 0))),
        upstream.astype(f32),
    )
    token_grad = (back + residual).astype(bf16)
    return token_grad[None, None], qkv_total[None], out_total[None], gain_total


def solution(mesh):
    fine = Mesh(mesh.devices.reshape(2, 2, 2, 4, 4), ("section", "zl", "core", "y", "x"))
    in_specs = (
        P("section", DP, RENDER, None),
        P("section", DP, None),
        P("section", DP, None),
        P("section", None),
        P(DP, RENDER, None),
    )
    out_specs = (
        P("section", DP, RENDER, None),
        P("section", DP, None),
        P("section", DP, None),
        P("section", None),
    )
    return jax.shard_map(shards, mesh=fine, in_specs=in_specs, out_specs=out_specs, check_vma=False)
```

```python
import math

import jax
import jax.numpy as jnp
from jax import lax
from jax.experimental import pallas as pl
from jax.experimental.pallas import tpu as pltpu
from jax.sharding import Mesh
from jax.sharding import PartitionSpec as P

HD = 128
MY = 2
MW = MY * HD
NORM_EPSILON = 1e-06
FACTOR = HD**-0.5
RENDER = ("zl", "core")
DP = ("y", "x")
SWAP = [(0, 1), (1, 0)]
DIAG = [(0, 3), (1, 2), (2, 1), (3, 0)]
bf16 = jnp.bfloat16
f32 = jnp.float32


def mm(left, right):
    return jnp.dot(left, right, preferred_element_type=f32)


def mm_tn(left, right):
    return lax.dot_general(left, right, (((0,), (0,)), ((), ())), preferred_element_type=f32)


def mm_nt(left, right):
    return lax.dot_general(left, right, (((1,), (1,)), ((), ())), preferred_element_type=f32)


def core_swap(t):
    return lax.ppermute(t, "core", SWAP)


def z_swap(t):
    return lax.ppermute(t, "zl", SWAP)


def gather_rel(t):
    z = z_swap(t)
    c = core_swap(t)
    return [t, c, z, core_swap(z)]


def spread_rel(b):
    return [b[0], core_swap(b[1]), z_swap(b[2]), lax.ppermute(b[3], RENDER, DIAG)]


def sum_near(own, near):
    n = own.shape[0] // 2
    near = core_swap(near)
    return own[:n].astype(f32) + near[:n].astype(f32), add(own[n:], near[n:])


def sum_far(mine, far):
    return (mine + z_swap(far).astype(f32)).astype(bf16)


def add(*terms):
    return sum(t.astype(f32) for t in terms).astype(bf16)


def step(t, stage, k):
    pairs = []
    for core in range(2):
        for y in range(4):
            for x in range(4):
                to = (y, (x + k) % 4) if core == stage else ((y + k) % 4, x)
                pairs.append((core * 16 + y * 4 + x, core * 16 + to[0] * 4 + to[1]))
    return lax.ppermute(t, ("core", "y", "x"), pairs)


def after(t, *others):
    return lax.optimization_barrier((t, *others))[0]


def gather_near(mine):
    near, far, other = [step(mine, 0, k) for k in (1, 2, 3)]
    return jnp.concatenate([mine, near], 0), jnp.concatenate([far, other], 0)


def gather_far(t):
    up = [step(h, 1, 1) for h in t]
    down = [step(h, 1, -1) for h in t[::-1]][::-1]
    far = [step(after(up[0], up[1]), 1, 1), step(after(down[1], down[0]), 1, -1)]
    return [*t, *up, *far, *down]


def ring_sum_far(blocks):
    own, after, far, before = blocks[:2], blocks[2:4], blocks[4:6], blocks[6:]
    far_up, far_down = step(far[0], 1, 1), step(far[1], 1, -1)
    up = [None, step(after[1], 1, 1)]
    down = [step(before[0], 1, -1), None]
    up[0] = step(add(after[0], far_up), 1, 1)
    down[1] = step(add(before[1], far_down), 1, -1)
    parts = []
    for m in range(4):
        n = own[0].shape[0] // 2
        rows = slice((m % 2) * n, (m % 2 + 1) * n)
        parts.append(add(*[t[m // 2][rows] for t in (own, up, down)]))
    return parts, (up[1], down[0])


def ring_sum_near(parts):
    return add(parts[0], *[step(parts[m], 0, m) for m in (1, 2, 3)])


def cross_section(t, source):
    pairs = [(source * 2 + i, (1 - source) * 2 + 1 - i) for i in range(2)]
    return lax.ppermute(t, ("section", "zl"), pairs)


def sum_over_dp(t):
    blocks = jnp.broadcast_to(t[None], (16, *t.shape))
    return lax.all_to_all(blocks, DP, 0, 0, tiled=True).sum(axis=0)


def sum_over_render(t):
    one, two, three = [
        lax.ppermute(t, RENDER, [(i, i ^ bits) for i in range(4)]) for bits in (1, 2, 3)
    ]
    return (t + one) + (two + three)


def norm_back(values, scale, gain_row, upstream):
    wide = values.astype(f32)
    grad = upstream.astype(f32)
    scaled = grad * gain_row
    inner = jnp.sum(scaled * wide, axis=-1, keepdims=True)
    result = scale * scaled - wide * scale**3 * inner / values.shape[-1]
    return result


def kernel_call(body, place, inputs, outputs, flops, scratch=()):
    moved = sum(t.size * t.dtype.itemsize for t in list(inputs) + list(outputs))
    vmem = pl.BlockSpec(memory_space=pltpu.VMEM)
    held = moved + sum(math.prod(t.shape) * 4 for t in scratch)
    return pl.pallas_call(
        body,
        out_shape=tuple(outputs),
        in_specs=[pl.BlockSpec(memory_space=pltpu.SMEM)] + [vmem] * len(inputs),
        out_specs=(vmem,) * len(outputs),
        scratch_shapes=scratch,
        compiler_params=pltpu.CompilerParams(vmem_limit_bytes=held + 6 * 2**20),
        cost_estimate=pl.CostEstimate(flops=flops, bytes_accessed=moved, transcendentals=0),
    )(place, *inputs)


def shape(rows, cols, dtype=bf16):
    return jax.ShapeDtypeStruct((rows, cols), dtype)


def block(i, n):
    return pl.ds(pl.multiple_of(i * n, n), n)


def head(part, h):
    at = part * MW + h * HD
    return slice(at, at + HD)


def lay_out(dst, blocks, rank, permuted):
    wide = blocks[0].shape[1]
    for j, b in enumerate(blocks):
        n = b.shape[0] // 4
        lanes = slice(j * wide, (j + 1) * wide) if rank is None else block(rank ^ j, wide)
        for i in range(4):
            at = (i ^ j if permuted else i) * n
            dst[i * n : (i + 1) * n, lanes] = b[at : at + n, :]


def out_rows(to, rank):
    return ((to >> 2) ^ rank) * 4 + (to & 3)


def norm_body(place, gain, t0, t1, t2, t3, normed, normed_t, scales):
    n = t0.shape[0]
    for j, t in enumerate((t0, t1, t2, t3)):
        wide = t[...].astype(f32)
        scale = lax.rsqrt(jnp.mean(wide * wide, axis=-1, keepdims=True) + NORM_EPSILON)
        out = (wide * scale * gain[...]).astype(bf16)
        normed[j * n : (j + 1) * n, :] = out
        normed_t[:, j * n : (j + 1) * n] = out.T
        scales[j * n : (j + 1) * n, :] = scale


def holder(place, k, m, sign):
    y, x, first = place[0], place[1], place[2] & 1
    dy, dx = jnp.where(first == 0, k, m), jnp.where(first == 0, m, k)
    return ((y + sign * dy) & 3) * 4 + ((x + sign * dx) & 3)


def project_body(place, normed, *refs):
    w, w_rel, out, enc_o = refs[8:]
    n, wide = refs[0].shape[0] // 2, w.shape[1]
    for k in range(4):
        for m in range(4):
            src, row = refs[2 * k + m // 2], (m % 2) * n
            to = holder(place, k, m, -1)
            w[block(to, n), :] = src[row : row + n, :wide]
            for i in range(2):
                w_rel[block(out_rows(to, place[2]), n // 2), i * MW : (i + 1) * MW] = src[
                    row + i * (n // 2) : row + (i + 1) * (n // 2), wide:
                ]
    for at in range(0, w.shape[1], 256):
        out[:, at : at + 256] = mm(normed[...], w[:, at : at + 256]).astype(bf16)
    for h in range(MY):
        q = latent_rows(out, head(0, h))
        p = softmax(mm_nt(q, out[:, head(1, h)]) * FACTOR)
        enc_o[:, head(0, h)] = mm(p.astype(bf16), out[:, head(2, h)]).astype(bf16)


def upstream_body(place, u0, u1, u2, u3, b0, b1, b2, b3, up_o, w_row):
    lay_out(w_row, (b0, b1, b2, b3), place[2], False)
    n = u0.shape[0]
    for j, u in enumerate((u0, u1, u2, u3)):
        up_o[j * n : (j + 1) * n, :] = mm_nt(u[...], w_row[...]).astype(bf16)


def latent_rows(ref, lanes):
    half = ref.shape[0] // 8
    return jnp.concatenate(
        [ref[(2 * i + 1) * half : (2 * i + 2) * half, lanes] for i in range(4)], 0
    )


def softmax(scores):
    raised = jnp.exp(scores - jnp.max(scores, axis=-1, keepdims=True))
    return raised * (1.0 / jnp.sum(raised, axis=-1, keepdims=True))


def latents_body(place, t0, t1, t2, t3, o0, o1, o2, o3, w_rel, z, o_all):
    rank = place[2]
    lay_out(o_all, (o0, o1, o2, o3), None, True)
    half, cols = t0.shape[0] // 2, z.shape[1]
    added = mm(o_all[...], w_rel[...])
    for j, t in enumerate((t0, t1, t2, t3)):
        rows = slice(j * half, (j + 1) * half)
        z[rows, :] = (t[half:, block(rank, cols)].astype(f32) + added[rows]).astype(bf16)


def weight_parts(place, normed_t, d_proj, d_out, outs, extra):
    n = outs[0].shape[0] // 2
    wide, m_out = d_proj.shape[1], n // 2
    for k in range(4):
        for m in range(4):
            to = holder(place, k, m, 1)
            part = mm(normed_t[block(to, n), :], d_proj[...])
            o, row = outs[2 * k + m // 2], (m % 2) * n
            if extra is not None:
                nz_t, d_kvz = extra
                more = mm(nz_t[block(to, n), :], d_kvz[...])
                part = jnp.concatenate([part[:, :MW], part[:, MW:] + more], 1)
            o[row : row + n, :wide] = part.astype(bf16)
            for i in range(2):
                o[row + i * m_out : row + (i + 1) * m_out, wide:] = d_out[
                    block(out_rows(to, place[2]), m_out), i * MW : (i + 1) * MW
                ]


def encoder_back_body(place, d0, d1, d2, d3, w_row, proj, normed_t, w, o_all, scales, *refs):
    rows, own, near, gain, outs = refs[:4], refs[4], refs[5], refs[6], refs[7:15]
    d_proj, d_z, up, d_out = refs[15:]
    lat = d_z.shape[0]
    half = lat // 4
    for j, d in enumerate((d0, d1, d2, d3)):
        d_z[j * half : (j + 1) * half, :] = d[...]
    up[...] = mm_nt(d_z[...], w_row[...]).astype(bf16)
    for h in range(MY):
        q = latent_rows(proj, head(0, h))
        k, v = proj[:, head(1, h)], proj[:, head(2, h)]
        u = up[:, head(0, h)]
        p = softmax(mm_nt(q, k) * FACTOR)
        dp = mm_nt(u, v)
        delta = jnp.sum(dp * p, axis=-1, keepdims=True)
        ds = (p * (dp - delta) * FACTOR).astype(bf16)
        dq = mm(ds, k).astype(bf16)
        for i in range(4):
            at = 2 * i * half
            d_proj[at : at + half, head(0, h)] = jnp.zeros((half, HD), bf16)
            d_proj[at + half : at + 2 * half, head(0, h)] = dq[i * half : (i + 1) * half]
        d_proj[:, head(1, h)] = mm_tn(ds, q).astype(bf16)
        d_proj[:, head(2, h)] = mm_tn(p.astype(bf16), u).astype(bf16)
    d_out[...] = mm_tn(o_all[...], d_z[:, block(place[2], d_out.shape[1])]).astype(bf16)
    weight_parts(place, normed_t, d_proj, d_out, outs, None)
    gain[...] = jnp.zeros(gain.shape, f32)
    sums_for_render(d_proj, w, 0, own, near, rows, scales, gain)


def decoder_back_body(place, d_proj, d_kvz, nz, normed_t, w, *refs):
    ups, os, z_gain, scales, rows = refs[:4], refs[4:8], refs[8], refs[9], refs[10:14]
    own, near, gain, outs, (nz_t, o_all, d_out, up) = *refs[14:17], refs[17:25], refs[25:]
    for at in range(0, nz.shape[1], 512):
        nz_t[at : at + 512, :] = nz[:, at : at + 512].T
    lay_out(o_all, os, None, True)
    n, cols = ups[0].shape[0], d_out.shape[1]
    for j, u in enumerate(ups):
        up[j * n : (j + 1) * n, :] = u[:, block(place[2], cols)]
    d_out[...] = mm_tn(o_all[...], up[...]).astype(bf16)
    weight_parts(place, normed_t, d_proj, d_out, outs, (nz_t, d_kvz))
    gain[...] = z_gain[...]
    sums_for_render(d_proj, w, 0, own, near, rows, scales, gain)


def decoder_body(place, gain, z0, z1, z2, z3, w, proj, up, *refs):
    out, d_proj, d_kvz, nz, scales, z_own, own, near, z_gain, z, kvz, acc = refs
    lat, width = z.shape
    half = lat // 4
    lay_out(z, (z0, z1, z2, z3), place[2], True)
    z_own[...] = z[:half, :]
    for i in range(4):
        rows = slice(i * half, (i + 1) * half)
        wide = z[rows, :].astype(f32)
        scale = lax.rsqrt(jnp.mean(wide * wide, axis=-1, keepdims=True) + NORM_EPSILON)
        nz[rows, :] = (wide * scale * gain[...]).astype(bf16)
        scales[rows, :] = scale
    kvz[...] = mm(nz[...], w[:, MW:]).astype(bf16)
    views = proj.shape[0] // 128
    for h in range(MY):
        kz, vz = kvz[:, head(0, h)], kvz[:, head(1, h)]
        for i in range(views):
            rows = slice(i * 128, (i + 1) * 128)
            q, k, v = [proj[rows, head(part, h)] for part in range(3)]
            u = up[rows, head(0, h)]
            s = mm_nt(q, kz) * FACTOR
            t = mm_nt(q, k) * FACTOR
            top = jnp.maximum(
                jnp.max(s, axis=-1, keepdims=True), jnp.max(t, axis=-1, keepdims=True)
            )
            s, t = jnp.exp(s - top), jnp.exp(t - top)
            total = jnp.sum(s, axis=-1, keepdims=True) + jnp.sum(t, axis=-1, keepdims=True)
            s, t = s * (1.0 / total), t * (1.0 / total)
            sb, tb = s.astype(bf16), t.astype(bf16)
            out[rows, head(0, h)] = (mm(sb, vz) + mm(tb, v)).astype(bf16)
            ds, dt = mm_nt(u, vz), mm_nt(u, v)
            delta = jnp.sum(ds * s, axis=-1, keepdims=True) + jnp.sum(dt * t, axis=-1, keepdims=True)
            ds = (s * (ds - delta) * FACTOR).astype(bf16)
            dt = (t * (dt - delta) * FACTOR).astype(bf16)
            d_proj[rows, head(0, h)] = (mm(ds, kz) + mm(dt, k)).astype(bf16)
            d_proj[rows, head(1, h)] = mm_tn(dt, q).astype(bf16)
            d_proj[rows, head(2, h)] = mm_tn(tb, u).astype(bf16)
            dkz, dvz = mm_tn(ds, q), mm_tn(sb, u)
            if i > 0:
                dkz, dvz = dkz + acc[:, head(0, h)], dvz + acc[:, head(1, h)]
            acc[:, head(0, h)], acc[:, head(1, h)] = dkz, dvz
    d_kvz[...] = acc[...].astype(bf16)
    z_gain[...] = jnp.zeros(z_gain.shape, f32)
    z_rows = [z.at[i * half : (i + 1) * half, :] for i in range(4)]
    sums_for_render(d_kvz, w, MW, own, near, z_rows, scales, z_gain)


def sums_for_render(grads, w, first, own, near, rows, scales, gain):
    n = grads.shape[0] // 4
    for at in range(0, w.shape[0], 512):
        cols = slice(at, at + 512)
        got = mm_nt(grads[...], w[cols, first:])
        for i, r in enumerate(rows):
            part = got[i * n : (i + 1) * n]
            term = part * (r[:, cols].astype(f32) * scales[i * n : (i + 1) * n, :])
            gain[:, cols] += jnp.sum(term, axis=0, keepdims=True)
            half = slice(i // 2 * n, (i // 2 + 1) * n)
            (near if i % 2 else own)[half, cols] = part.astype(bf16)


def totals_body(place, t0, t1, t2, t3, qkv, out):
    half = out.shape[0]
    for j, t in enumerate((t0, t1, t2, t3)):
        rank = place[2] ^ j
        for part in range(3):
            qkv[:, block(part * 4 + rank, MW)] = t[:, part * MW : (part + 1) * MW].astype(f32)
        for i in range(2):
            rows = slice(i * half, (i + 1) * half)
            out[:, block(rank * 2 + i, MW)] = t[rows, 3 * MW :].astype(f32)


def shards(section_tokens, w_qkv, w_out, gains, cotangent):
    tokens = section_tokens[0, 0]
    upstream = cotangent[0]
    rank = lax.axis_index("zl") * 2 + lax.axis_index("core")
    place = jnp.stack([lax.axis_index("y"), lax.axis_index("x"), rank]).astype(jnp.int32)
    is_encoder = lax.axis_index("section") == 0
    n, width = tokens.shape
    half, cols, count, lat = n // 2, width // 4, 4 * n, 2 * n

    own_cols = [
        lax.dynamic_slice_in_dim(w_qkv[0], part * 4 * MW + rank * MW, MW, 1) for part in range(3)
    ]
    own_out = [lax.dynamic_slice_in_dim(w_out[0], rank * cols + i * MW, MW, 1) for i in range(2)]
    near = gather_near(jnp.concatenate([*own_cols, jnp.concatenate(own_out, 0)], 1))
    rows = gather_rel(tokens)
    near, rows[2] = lax.optimization_barrier((near, rows[2]))
    w_parts = gather_far(near)
    normed, normed_t, scales = kernel_call(
        norm_body, place, [gains, *rows],
        [shape(count, width), shape(width, count), shape(count, 1, f32)], 8 * count * width,
    )
    ups = gather_rel(after(upstream, w_parts[2]))
    w_h, w_rel, projected, enc_o = kernel_call(
        project_body, place, [normed, *w_parts],
        [shape(width, 3 * MW), shape(4 * MW, cols), shape(count, 3 * MW), shape(lat, MW)],
        6 * count * width * MW + 4 * lat * count * MW,
    )
    w_row_blocks = spread_rel([w_rel[j * MW : (j + 1) * MW] for j in range(4)])
    enc_blocks = gather_rel(enc_o)
    enc_blocks[1], ups = lax.optimization_barrier((enc_blocks[1], ups))
    z_cols, enc_all = kernel_call(
        latents_body, place, [*rows, *enc_blocks, w_rel],
        [shape(lat, cols), shape(lat, 4 * MW)], 8 * lat * cols * MW,
    )
    z_crossed = cross_section(z_cols, 0)
    up_o, w_row = kernel_call(
        upstream_body, place, [*ups, *w_row_blocks],
        [shape(count, MW), shape(MW, width)], 2 * count * width * MW,
    )
    z_blocks = gather_rel(after(z_crossed, up_o))
    z_blocks = z_blocks[2:] + z_blocks[:2]

    decoder_shapes = [
        shape(count, MW), shape(count, 3 * MW), shape(lat, 2 * MW), shape(lat, width),
        shape(lat, 1, f32), shape(half, width), shape(2 * half, width), shape(2 * half, width),
        shape(1, width, f32),
    ]
    dec_o, d_proj, d_kvz, nz, z_scale, z_own, own, near, z_gain = lax.cond(
        is_encoder,
        lambda: tuple(jnp.zeros(s.shape, s.dtype) for s in decoder_shapes),
        lambda: tuple(kernel_call(
            decoder_body, place, [gains, *z_blocks, w_h, projected, up_o], decoder_shapes,
            8 * lat * width * MW + 12 * count * (lat + 128) * MW,
            [pltpu.VMEM((lat, width), bf16), pltpu.VMEM((lat, 2 * MW), bf16),
             pltpu.VMEM((lat, 2 * MW), f32)],
        )),
    )
    d_nz = sum_far(*sum_near(own, near))
    d_z = norm_back(z_own, z_scale[:half], gains[0], d_nz)
    d_z = d_z.astype(bf16)
    dec_blocks = gather_rel(after(dec_o, d_z))
    d_z = cross_section(d_z, 1)
    d_z_blocks = gather_rel(after(d_z, *dec_blocks))
    d_z_blocks = d_z_blocks[2:] + d_z_blocks[:2]
    d_z = d_z_blocks[0]

    back_shapes = [shape(2 * n, width)] * 2 + [shape(1, width, f32)] + [shape(2 * n, width // 2)] * 8
    back_flops = 12 * width * count * MW + 2 * lat * width * MW
    own, near, gain_part, *parts = lax.cond(
        is_encoder,
        lambda: tuple(kernel_call(
            encoder_back_body, place, [*d_z_blocks, w_row, projected, normed_t, w_h, enc_all, scales, *rows],
            back_shapes, back_flops + 2 * lat * width * MW + 10 * lat * count * MW,
            [pltpu.VMEM((count, 3 * MW), bf16), pltpu.VMEM((lat, width), bf16),
             pltpu.VMEM((lat, MW), bf16), pltpu.VMEM((4 * MW, cols), bf16)],
        )),
        lambda: tuple(kernel_call(
            decoder_back_body, place, [d_proj, d_kvz, nz, normed_t, w_h, *ups, *dec_blocks, z_gain, scales, *rows],
            back_shapes, back_flops + 4 * lat * width * MW,
            [pltpu.VMEM((width, lat), bf16), pltpu.VMEM((count, 4 * MW), bf16),
             pltpu.VMEM((4 * MW, cols), bf16), pltpu.VMEM((count, cols), bf16)],
        )),
    )
    d_n, far = sum_near(own, near)
    parts[2:4], far = lax.optimization_barrier((parts[2:4], far))
    d_n = sum_far(d_n, far)
    parts, first = ring_sum_far(parts)
    gain_total = sum_over_dp(after(gain_part, *first))
    parts[0], gain_total, d_n = lax.optimization_barrier((parts[0], gain_total, d_n))
    sums = ring_sum_near(parts)
    sums_far, sums_near = z_swap(sums), core_swap(sums)
    gain_total = sum_over_render(after(gain_total, sums_near))
    qkv_total, out_total = kernel_call(
        totals_body, place, [sums, sums_near, sums_far, core_swap(sums_far)],
        [shape(n, 12 * MW, f32), shape(half, width, f32)], n * width,
    )
    back = norm_back(tokens, scales[:n], gains[0], d_n)
    residual = jnp.where(
        is_encoder,
        jnp.pad(d_z.astype(f32), ((half, 0), (0, 0))),
        upstream.astype(f32),
    )
    token_grad = (back + residual).astype(bf16)
    return token_grad[None, None], qkv_total[None], out_total[None], gain_total


def solution(mesh):
    fine = Mesh(mesh.devices.reshape(2, 2, 2, 4, 4), ("section", "zl", "core", "y", "x"))
    in_specs = (
        P("section", DP, RENDER, None),
        P("section", DP, None),
        P("section", DP, None),
        P("section", None),
        P(DP, RENDER, None),
    )
    out_specs = (
        P("section", DP, RENDER, None),
        P("section", DP, None),
        P("section", DP, None),
        P("section", None),
    )
    return jax.shard_map(shards, mesh=fine, in_specs=in_specs, out_specs=out_specs, check_vma=False)
```

```python
import math

import jax
import jax.numpy as jnp
from jax import lax
from jax.experimental import pallas as pl
from jax.experimental.pallas import tpu as pltpu
from jax.sharding import Mesh
from jax.sharding import PartitionSpec as P

HD = 128
MY = 2
MW = MY * HD
NORM_EPSILON = 1e-06
FACTOR = HD**-0.5
RENDER = ("zl", "core")
DP = ("y", "x")
SWAP = [(0, 1), (1, 0)]
DIAG = [(0, 3), (1, 2), (2, 1), (3, 0)]
bf16 = jnp.bfloat16
f32 = jnp.float32


def mm(left, right):
    return jnp.dot(left, right, preferred_element_type=f32)


def mm_tn(left, right):
    return lax.dot_general(left, right, (((0,), (0,)), ((), ())), preferred_element_type=f32)


def mm_nt(left, right):
    return lax.dot_general(left, right, (((1,), (1,)), ((), ())), preferred_element_type=f32)


def core_swap(t):
    return lax.ppermute(t, "core", SWAP)


def z_swap(t):
    return lax.ppermute(t, "zl", SWAP)


def gather_rel(t):
    z = z_swap(t)
    c = core_swap(t)
    return [t, c, z, core_swap(z)]


def spread_rel(b):
    return [b[0], core_swap(b[1]), z_swap(b[2]), lax.ppermute(b[3], RENDER, DIAG)]


def sum_near(own, near):
    n = own.shape[0] // 2
    near = core_swap(near)
    return own[:n].astype(f32) + near[:n].astype(f32), add(own[n:], near[n:])


def sum_far(mine, far):
    return (mine + z_swap(far).astype(f32)).astype(bf16)


def add(*terms):
    return sum(t.astype(f32) for t in terms).astype(bf16)


def step(t, stage, k):
    pairs = []
    for core in range(2):
        for y in range(4):
            for x in range(4):
                to = (y, (x + k) % 4) if core == stage else ((y + k) % 4, x)
                pairs.append((core * 16 + y * 4 + x, core * 16 + to[0] * 4 + to[1]))
    return lax.ppermute(t, ("core", "y", "x"), pairs)


def after(t, *others):
    return lax.optimization_barrier((t, *others))[0]


def gather_near(mine):
    near, far, other = [step(mine, 0, k) for k in (1, 2, 3)]
    return jnp.concatenate([mine, near], 0), jnp.concatenate([far, other], 0)


def gather_far(t):
    up = [step(h, 1, 1) for h in t]
    down = [step(h, 1, -1) for h in t[::-1]][::-1]
    return [*t, *up, step(up[0], 1, 1), step(down[1], 1, -1), *down]


def ring_sum_far(blocks):
    own, after, far, before = blocks[:2], blocks[2:4], blocks[4:6], blocks[6:]
    far_up, far_down = step(far[0], 1, 1), step(far[1], 1, -1)
    up = [None, step(after[1], 1, 1)]
    down = [step(before[0], 1, -1), None]
    up[0] = step(add(after[0], far_up), 1, 1)
    down[1] = step(add(before[1], far_down), 1, -1)
    parts = []
    for m in range(4):
        n = own[0].shape[0] // 2
        rows = slice((m % 2) * n, (m % 2 + 1) * n)
        parts.append(add(*[t[m // 2][rows] for t in (own, up, down)]))
    return parts, (up[1], down[0])


def ring_sum_near(parts):
    return add(parts[0], *[step(parts[m], 0, m) for m in (1, 2, 3)])


def cross_section(t, source):
    pairs = [(source * 2 + i, (1 - source) * 2 + 1 - i) for i in range(2)]
    return lax.ppermute(t, ("section", "zl"), pairs)


def sum_over_dp(t):
    return lax.all_gather(t, DP, axis=0, tiled=True).sum(axis=0, keepdims=True)


def sum_over_render(t):
    one, two, three = [
        lax.ppermute(t, RENDER, [(i, i ^ bits) for i in range(4)]) for bits in (1, 2, 3)
    ]
    return (t + one) + (two + three)


def norm_back(values, scale, gain_row, upstream):
    wide = values.astype(f32)
    grad = upstream.astype(f32)
    scaled = grad * gain_row
    inner = jnp.sum(scaled * wide, axis=-1, keepdims=True)
    result = scale * scaled - wide * scale**3 * inner / values.shape[-1]
    return result


def kernel_call(body, place, inputs, outputs, flops, scratch=()):
    moved = sum(t.size * t.dtype.itemsize for t in list(inputs) + list(outputs))
    vmem = pl.BlockSpec(memory_space=pltpu.VMEM)
    held = moved + sum(math.prod(t.shape) * 4 for t in scratch)
    return pl.pallas_call(
        body,
        out_shape=tuple(outputs),
        in_specs=[pl.BlockSpec(memory_space=pltpu.SMEM)] + [vmem] * len(inputs),
        out_specs=(vmem,) * len(outputs),
        scratch_shapes=scratch,
        compiler_params=pltpu.CompilerParams(vmem_limit_bytes=held + 6 * 2**20),
        cost_estimate=pl.CostEstimate(flops=flops, bytes_accessed=moved, transcendentals=0),
    )(place, *inputs)


def shape(rows, cols, dtype=bf16):
    return jax.ShapeDtypeStruct((rows, cols), dtype)


def block(i, n):
    return pl.ds(pl.multiple_of(i * n, n), n)


def head(part, h):
    at = part * MW + h * HD
    return slice(at, at + HD)


def lay_out(dst, blocks, rank, permuted):
    wide = blocks[0].shape[1]
    for j, b in enumerate(blocks):
        n = b.shape[0] // 4
        lanes = slice(j * wide, (j + 1) * wide) if rank is None else block(rank ^ j, wide)
        for i in range(4):
            at = (i ^ j if permuted else i) * n
            dst[i * n : (i + 1) * n, lanes] = b[at : at + n, :]


def out_rows(to, rank):
    return ((to >> 2) ^ rank) * 4 + (to & 3)


def norm_body(place, gain, t0, t1, t2, t3, normed, normed_t, scales):
    n = t0.shape[0]
    for j, t in enumerate((t0, t1, t2, t3)):
        wide = t[...].astype(f32)
        scale = lax.rsqrt(jnp.mean(wide * wide, axis=-1, keepdims=True) + NORM_EPSILON)
        out = (wide * scale * gain[...]).astype(bf16)
        normed[j * n : (j + 1) * n, :] = out
        normed_t[:, j * n : (j + 1) * n] = out.T
        scales[j * n : (j + 1) * n, :] = scale


def holder(place, k, m, sign):
    y, x, first = place[0], place[1], place[2] & 1
    dy, dx = jnp.where(first == 0, k, m), jnp.where(first == 0, m, k)
    return ((y + sign * dy) & 3) * 4 + ((x + sign * dx) & 3)


def project_body(place, normed, *refs):
    w, w_rel, out, enc_o = refs[8:]
    n, wide = refs[0].shape[0] // 2, w.shape[1]
    for k in range(4):
        for m in range(4):
            src, row = refs[2 * k + m // 2], (m % 2) * n
            to = holder(place, k, m, -1)
            w[block(to, n), :] = src[row : row + n, :wide]
            for i in range(2):
                w_rel[block(out_rows(to, place[2]), n // 2), i * MW : (i + 1) * MW] = src[
                    row + i * (n // 2) : row + (i + 1) * (n // 2), wide:
                ]
    for at in range(0, w.shape[1], 256):
        out[:, at : at + 256] = mm(normed[...], w[:, at : at + 256]).astype(bf16)
    for h in range(MY):
        q = latent_rows(out, head(0, h))
        p = softmax(mm_nt(q, out[:, head(1, h)]) * FACTOR)
        enc_o[:, head(0, h)] = mm(p.astype(bf16), out[:, head(2, h)]).astype(bf16)


def upstream_body(place, u0, u1, u2, u3, b0, b1, b2, b3, up_o, w_row):
    lay_out(w_row, (b0, b1, b2, b3), place[2], False)
    n = u0.shape[0]
    for j, u in enumerate((u0, u1, u2, u3)):
        up_o[j * n : (j + 1) * n, :] = mm_nt(u[...], w_row[...]).astype(bf16)


def latent_rows(ref, lanes):
    half = ref.shape[0] // 8
    return jnp.concatenate(
        [ref[(2 * i + 1) * half : (2 * i + 2) * half, lanes] for i in range(4)], 0
    )


def softmax(scores):
    raised = jnp.exp(scores - jnp.max(scores, axis=-1, keepdims=True))
    return raised * (1.0 / jnp.sum(raised, axis=-1, keepdims=True))


def latents_body(place, t0, t1, t2, t3, o0, o1, o2, o3, w_rel, z, o_all):
    rank = place[2]
    lay_out(o_all, (o0, o1, o2, o3), None, True)
    half, cols = t0.shape[0] // 2, z.shape[1]
    added = mm(o_all[...], w_rel[...])
    for j, t in enumerate((t0, t1, t2, t3)):
        rows = slice(j * half, (j + 1) * half)
        z[rows, :] = (t[half:, block(rank, cols)].astype(f32) + added[rows]).astype(bf16)


def weight_parts(place, normed_t, d_proj, d_out, outs, extra):
    n = outs[0].shape[0] // 2
    wide, m_out = d_proj.shape[1], n // 2
    for k in range(4):
        for m in range(4):
            to = holder(place, k, m, 1)
            part = mm(normed_t[block(to, n), :], d_proj[...])
            o, row = outs[2 * k + m // 2], (m % 2) * n
            if extra is not None:
                nz_t, d_kvz = extra
                more = mm(nz_t[block(to, n), :], d_kvz[...])
                part = jnp.concatenate([part[:, :MW], part[:, MW:] + more], 1)
            o[row : row + n, :wide] = part.astype(bf16)
            for i in range(2):
                o[row + i * m_out : row + (i + 1) * m_out, wide:] = d_out[
                    block(out_rows(to, place[2]), m_out), i * MW : (i + 1) * MW
                ]


def encoder_back_body(place, d0, d1, d2, d3, w_row, proj, normed_t, w, o_all, scales, *refs):
    rows, own, near, gain, outs = refs[:4], refs[4], refs[5], refs[6], refs[7:15]
    d_proj, d_z, up, d_out = refs[15:]
    lat = d_z.shape[0]
    half = lat // 4
    for j, d in enumerate((d0, d1, d2, d3)):
        d_z[j * half : (j + 1) * half, :] = d[...]
    up[...] = mm_nt(d_z[...], w_row[...]).astype(bf16)
    for h in range(MY):
        q = latent_rows(proj, head(0, h))
        k, v = proj[:, head(1, h)], proj[:, head(2, h)]
        u = up[:, head(0, h)]
        p = softmax(mm_nt(q, k) * FACTOR)
        dp = mm_nt(u, v)
        delta = jnp.sum(dp * p, axis=-1, keepdims=True)
        ds = (p * (dp - delta) * FACTOR).astype(bf16)
        dq = mm(ds, k).astype(bf16)
        for i in range(4):
            at = 2 * i * half
            d_proj[at : at + half, head(0, h)] = jnp.zeros((half, HD), bf16)
            d_proj[at + half : at + 2 * half, head(0, h)] = dq[i * half : (i + 1) * half]
        d_proj[:, head(1, h)] = mm_tn(ds, q).astype(bf16)
        d_proj[:, head(2, h)] = mm_tn(p.astype(bf16), u).astype(bf16)
    d_out[...] = mm_tn(o_all[...], d_z[:, block(place[2], d_out.shape[1])]).astype(bf16)
    weight_parts(place, normed_t, d_proj, d_out, outs, None)
    gain[...] = jnp.zeros(gain.shape, f32)
    sums_for_render(d_proj, w, 0, own, near, rows, scales, gain)


def decoder_back_body(place, d_proj, d_kvz, nz, normed_t, w, *refs):
    ups, os, z_gain, scales, rows = refs[:4], refs[4:8], refs[8], refs[9], refs[10:14]
    own, near, gain, outs, (nz_t, o_all, d_out, up) = *refs[14:17], refs[17:25], refs[25:]
    for at in range(0, nz.shape[1], 512):
        nz_t[at : at + 512, :] = nz[:, at : at + 512].T
    lay_out(o_all, os, None, True)
    n, cols = ups[0].shape[0], d_out.shape[1]
    for j, u in enumerate(ups):
        up[j * n : (j + 1) * n, :] = u[:, block(place[2], cols)]
    d_out[...] = mm_tn(o_all[...], up[...]).astype(bf16)
    weight_parts(place, normed_t, d_proj, d_out, outs, (nz_t, d_kvz))
    gain[...] = z_gain[...]
    sums_for_render(d_proj, w, 0, own, near, rows, scales, gain)


def decoder_body(place, gain, z0, z1, z2, z3, w, proj, up, *refs):
    out, d_proj, d_kvz, nz, scales, z_own, own, near, z_gain, z, kvz, acc = refs
    lat, width = z.shape
    half = lat // 4
    lay_out(z, (z0, z1, z2, z3), place[2], True)
    z_own[...] = z[:half, :]
    for i in range(4):
        rows = slice(i * half, (i + 1) * half)
        wide = z[rows, :].astype(f32)
        scale = lax.rsqrt(jnp.mean(wide * wide, axis=-1, keepdims=True) + NORM_EPSILON)
        nz[rows, :] = (wide * scale * gain[...]).astype(bf16)
        scales[rows, :] = scale
    kvz[...] = mm(nz[...], w[:, MW:]).astype(bf16)
    views = proj.shape[0] // 128
    for h in range(MY):
        kz, vz = kvz[:, head(0, h)], kvz[:, head(1, h)]
        for i in range(views):
            rows = slice(i * 128, (i + 1) * 128)
            q, k, v = [proj[rows, head(part, h)] for part in range(3)]
            u = up[rows, head(0, h)]
            s = mm_nt(q, kz) * FACTOR
            t = mm_nt(q, k) * FACTOR
            top = jnp.maximum(
                jnp.max(s, axis=-1, keepdims=True), jnp.max(t, axis=-1, keepdims=True)
            )
            s, t = jnp.exp(s - top), jnp.exp(t - top)
            total = jnp.sum(s, axis=-1, keepdims=True) + jnp.sum(t, axis=-1, keepdims=True)
            s, t = s * (1.0 / total), t * (1.0 / total)
            sb, tb = s.astype(bf16), t.astype(bf16)
            out[rows, head(0, h)] = (mm(sb, vz) + mm(tb, v)).astype(bf16)
            ds, dt = mm_nt(u, vz), mm_nt(u, v)
            delta = jnp.sum(ds * s, axis=-1, keepdims=True) + jnp.sum(dt * t, axis=-1, keepdims=True)
            ds = (s * (ds - delta) * FACTOR).astype(bf16)
            dt = (t * (dt - delta) * FACTOR).astype(bf16)
            d_proj[rows, head(0, h)] = (mm(ds, kz) + mm(dt, k)).astype(bf16)
            d_proj[rows, head(1, h)] = mm_tn(dt, q).astype(bf16)
            d_proj[rows, head(2, h)] = mm_tn(tb, u).astype(bf16)
            dkz, dvz = mm_tn(ds, q), mm_tn(sb, u)
            if i > 0:
                dkz, dvz = dkz + acc[:, head(0, h)], dvz + acc[:, head(1, h)]
            acc[:, head(0, h)], acc[:, head(1, h)] = dkz, dvz
    d_kvz[...] = acc[...].astype(bf16)
    z_gain[...] = jnp.zeros(z_gain.shape, f32)
    z_rows = [z.at[i * half : (i + 1) * half, :] for i in range(4)]
    sums_for_render(d_kvz, w, MW, own, near, z_rows, scales, z_gain)


def sums_for_render(grads, w, first, own, near, rows, scales, gain):
    n = grads.shape[0] // 4
    for at in range(0, w.shape[0], 512):
        cols = slice(at, at + 512)
        got = mm_nt(grads[...], w[cols, first:])
        for i, r in enumerate(rows):
            part = got[i * n : (i + 1) * n]
            term = part * (r[:, cols].astype(f32) * scales[i * n : (i + 1) * n, :])
            gain[:, cols] += jnp.sum(term.reshape(n // 8, 8, 512), axis=0)
            half = slice(i // 2 * n, (i // 2 + 1) * n)
            (near if i % 2 else own)[half, cols] = part.astype(bf16)


def totals_body(place, t0, t1, t2, t3, qkv, out):
    half = out.shape[0]
    for j, t in enumerate((t0, t1, t2, t3)):
        rank = place[2] ^ j
        for part in range(3):
            qkv[:, block(part * 4 + rank, MW)] = t[:, part * MW : (part + 1) * MW].astype(f32)
        for i in range(2):
            rows = slice(i * half, (i + 1) * half)
            out[:, block(rank * 2 + i, MW)] = t[rows, 3 * MW :].astype(f32)


def shards(section_tokens, w_qkv, w_out, gains, cotangent):
    tokens = section_tokens[0, 0]
    upstream = cotangent[0]
    rank = lax.axis_index("zl") * 2 + lax.axis_index("core")
    place = jnp.stack([lax.axis_index("y"), lax.axis_index("x"), rank]).astype(jnp.int32)
    is_encoder = lax.axis_index("section") == 0
    n, width = tokens.shape
    half, cols, count, lat = n // 2, width // 4, 4 * n, 2 * n

    own_cols = [
        lax.dynamic_slice_in_dim(w_qkv[0], part * 4 * MW + rank * MW, MW, 1) for part in range(3)
    ]
    own_out = [lax.dynamic_slice_in_dim(w_out[0], rank * cols + i * MW, MW, 1) for i in range(2)]
    near = gather_near(jnp.concatenate([*own_cols, jnp.concatenate(own_out, 0)], 1))
    rows = gather_rel(tokens)
    near, rows[2] = lax.optimization_barrier((near, rows[2]))
    w_parts = gather_far(near)
    normed, normed_t, scales = kernel_call(
        norm_body, place, [gains, *rows],
        [shape(count, width), shape(width, count), shape(count, 1, f32)], 8 * count * width,
    )
    ups = gather_rel(after(upstream, w_parts[2]))
    w_h, w_rel, projected, enc_o = kernel_call(
        project_body, place, [normed, *w_parts],
        [shape(width, 3 * MW), shape(4 * MW, cols), shape(count, 3 * MW), shape(lat, MW)],
        6 * count * width * MW + 4 * lat * count * MW,
    )
    w_row_blocks = spread_rel([w_rel[j * MW : (j + 1) * MW] for j in range(4)])
    enc_blocks = gather_rel(enc_o)
    enc_blocks[1], ups = lax.optimization_barrier((enc_blocks[1], ups))
    z_cols, enc_all = kernel_call(
        latents_body, place, [*rows, *enc_blocks, w_rel],
        [shape(lat, cols), shape(lat, 4 * MW)], 8 * lat * cols * MW,
    )
    z_crossed = cross_section(z_cols, 0)
    up_o, w_row = kernel_call(
        upstream_body, place, [*ups, *w_row_blocks],
        [shape(count, MW), shape(MW, width)], 2 * count * width * MW,
    )
    z_blocks = gather_rel(after(z_crossed, up_o))
    z_blocks = z_blocks[2:] + z_blocks[:2]

    decoder_shapes = [
        shape(count, MW), shape(count, 3 * MW), shape(lat, 2 * MW), shape(lat, width),
        shape(lat, 1, f32), shape(half, width), shape(2 * half, width), shape(2 * half, width),
        shape(8, width, f32),
    ]
    dec_o, d_proj, d_kvz, nz, z_scale, z_own, own, near, z_gain = lax.cond(
        is_encoder,
        lambda: tuple(jnp.zeros(s.shape, s.dtype) for s in decoder_shapes),
        lambda: tuple(kernel_call(
            decoder_body, place, [gains, *z_blocks, w_h, projected, up_o], decoder_shapes,
            8 * lat * width * MW + 12 * count * (lat + 128) * MW,
            [pltpu.VMEM((lat, width), bf16), pltpu.VMEM((lat, 2 * MW), bf16),
             pltpu.VMEM((lat, 2 * MW), f32)],
        )),
    )
    d_nz = sum_far(*sum_near(own, near))
    d_z = norm_back(z_own, z_scale[:half], gains[0], d_nz)
    d_z = d_z.astype(bf16)
    dec_blocks = gather_rel(after(dec_o, d_z))
    d_z = cross_section(d_z, 1)
    d_z_blocks = gather_rel(after(d_z, *dec_blocks))
    d_z_blocks = d_z_blocks[2:] + d_z_blocks[:2]
    d_z = d_z_blocks[0]

    back_shapes = [shape(2 * n, width)] * 2 + [shape(8, width, f32)] + [shape(2 * n, width // 2)] * 8
    back_flops = 12 * width * count * MW + 2 * lat * width * MW
    own, near, gain_part, *parts = lax.cond(
        is_encoder,
        lambda: tuple(kernel_call(
            encoder_back_body, place, [*d_z_blocks, w_row, projected, normed_t, w_h, enc_all, scales, *rows],
            back_shapes, back_flops + 2 * lat * width * MW + 10 * lat * count * MW,
            [pltpu.VMEM((count, 3 * MW), bf16), pltpu.VMEM((lat, width), bf16),
             pltpu.VMEM((lat, MW), bf16), pltpu.VMEM((4 * MW, cols), bf16)],
        )),
        lambda: tuple(kernel_call(
            decoder_back_body, place, [d_proj, d_kvz, nz, normed_t, w_h, *ups, *dec_blocks, z_gain, scales, *rows],
            back_shapes, back_flops + 4 * lat * width * MW,
            [pltpu.VMEM((width, lat), bf16), pltpu.VMEM((count, 4 * MW), bf16),
             pltpu.VMEM((4 * MW, cols), bf16), pltpu.VMEM((count, cols), bf16)],
        )),
    )
    d_n, far = sum_near(own, near)
    parts[2:4], far = lax.optimization_barrier((parts[2:4], far))
    parts, first = ring_sum_far(parts)
    d_n = sum_far(d_n, after(far, *first))
    gain_total = sum_over_dp(gain_part)
    parts[0] = after(parts[0], d_n)
    sums = ring_sum_near(parts)
    sums_far, sums_near = z_swap(sums), core_swap(sums)
    gain_total = sum_over_render(after(gain_total, sums_near))
    qkv_total, out_total = kernel_call(
        totals_body, place, [sums, sums_near, sums_far, core_swap(sums_far)],
        [shape(n, 12 * MW, f32), shape(half, width, f32)], n * width,
    )
    back = norm_back(tokens, scales[:n], gains[0], d_n)
    residual = jnp.where(
        is_encoder,
        jnp.pad(d_z.astype(f32), ((half, 0), (0, 0))),
        upstream.astype(f32),
    )
    token_grad = (back + residual).astype(bf16)
    return token_grad[None, None], qkv_total[None], out_total[None], gain_total


def solution(mesh):
    fine = Mesh(mesh.devices.reshape(2, 2, 2, 4, 4), ("section", "zl", "core", "y", "x"))
    in_specs = (
        P("section", DP, RENDER, None),
        P("section", DP, None),
        P("section", DP, None),
        P("section", None),
        P(DP, RENDER, None),
    )
    out_specs = (
        P("section", DP, RENDER, None),
        P("section", DP, None),
        P("section", DP, None),
        P("section", None),
    )
    return jax.shard_map(shards, mesh=fine, in_specs=in_specs, out_specs=out_specs, check_vma=False)
```

```python
import math

import jax
import jax.numpy as jnp
from jax import lax
from jax.experimental import pallas as pl
from jax.experimental.pallas import tpu as pltpu
from jax.sharding import Mesh
from jax.sharding import PartitionSpec as P

HD = 128
MY = 2
MW = MY * HD
NORM_EPSILON = 1e-06
FACTOR = HD**-0.5
RENDER = ("zl", "core")
DP = ("y", "x")
SWAP = [(0, 1), (1, 0)]
DIAG = [(0, 3), (1, 2), (2, 1), (3, 0)]
bf16 = jnp.bfloat16
f32 = jnp.float32


def mm(left, right):
    return jnp.dot(left, right, preferred_element_type=f32)


def mm_tn(left, right):
    return lax.dot_general(left, right, (((0,), (0,)), ((), ())), preferred_element_type=f32)


def mm_nt(left, right):
    return lax.dot_general(left, right, (((1,), (1,)), ((), ())), preferred_element_type=f32)


def core_swap(t):
    return lax.ppermute(t, "core", SWAP)


def z_swap(t):
    return lax.ppermute(t, "zl", SWAP)


def gather_rel(t):
    z = z_swap(t)
    c = core_swap(t)
    return [t, c, z, core_swap(z)]


def spread_rel(b):
    return [b[0], core_swap(b[1]), z_swap(b[2]), lax.ppermute(b[3], RENDER, DIAG)]


def sum_near(own, near):
    n = own.shape[0] // 2
    near = core_swap(near)
    return own[:n].astype(f32) + near[:n].astype(f32), add(own[n:], near[n:])


def sum_far(mine, far):
    return (mine + z_swap(far).astype(f32)).astype(bf16)


def add(*terms):
    return sum(t.astype(f32) for t in terms).astype(bf16)


def step(t, stage, k):
    pairs = []
    for core in range(2):
        for y in range(4):
            for x in range(4):
                to = (y, (x + k) % 4) if core == stage else ((y + k) % 4, x)
                pairs.append((core * 16 + y * 4 + x, core * 16 + to[0] * 4 + to[1]))
    return lax.ppermute(t, ("core", "y", "x"), pairs)


def after(t, *others):
    return lax.optimization_barrier((t, *others))[0]


def gather_near(mine):
    near, far, other = [step(mine, 0, k) for k in (1, 2, 3)]
    return jnp.concatenate([mine, near], 0), jnp.concatenate([far, other], 0)


def gather_far(t):
    up = [step(h, 1, 1) for h in t]
    down = [step(h, 1, -1) for h in t[::-1]][::-1]
    return [*t, *up, step(up[0], 1, 1), step(down[1], 1, -1), *down]


def ring_sum_far(blocks):
    own, after, far, before = blocks[:2], blocks[2:4], blocks[4:6], blocks[6:]
    far_up, far_down = step(far[0], 1, 1), step(far[1], 1, -1)
    up = [None, step(after[1], 1, 1)]
    down = [step(before[0], 1, -1), None]
    summed = add(after[0], far_up), add(before[1], far_down)
    up[0], down[1] = step(summed[0], 1, 1), step(summed[1], 1, -1)
    parts = []
    for m in range(4):
        n = own[0].shape[0] // 2
        rows = slice((m % 2) * n, (m % 2 + 1) * n)
        parts.append(add(*[t[m // 2][rows] for t in (own, up, down)]))
    return parts


def ring_sum_near(parts):
    return add(parts[0], *[step(parts[m], 0, m) for m in (1, 2, 3)])


def cross_section(t, source):
    pairs = [(source * 2 + i, (1 - source) * 2 + 1 - i) for i in range(2)]
    return lax.ppermute(t, ("section", "zl"), pairs)


def sum_everywhere(t):
    peers = 64
    blocks = jnp.broadcast_to(t[None], (peers, *t.shape))
    return lax.all_to_all(blocks, RENDER + DP, 0, 0, tiled=True).sum(axis=0)


def norm_back(values, scale, gain_row, upstream):
    wide = values.astype(f32)
    grad = upstream.astype(f32)
    scaled = grad * gain_row
    inner = jnp.sum(scaled * wide, axis=-1, keepdims=True)
    result = scale * scaled - wide * scale**3 * inner / values.shape[-1]
    return result


def kernel_call(body, place, inputs, outputs, flops, scratch=()):
    moved = sum(t.size * t.dtype.itemsize for t in list(inputs) + list(outputs))
    vmem = pl.BlockSpec(memory_space=pltpu.VMEM)
    held = moved + sum(math.prod(t.shape) * 4 for t in scratch)
    return pl.pallas_call(
        body,
        out_shape=tuple(outputs),
        in_specs=[pl.BlockSpec(memory_space=pltpu.SMEM)] + [vmem] * len(inputs),
        out_specs=(vmem,) * len(outputs),
        scratch_shapes=scratch,
        compiler_params=pltpu.CompilerParams(vmem_limit_bytes=held + 6 * 2**20),
        cost_estimate=pl.CostEstimate(flops=flops, bytes_accessed=moved, transcendentals=0),
    )(place, *inputs)


def shape(rows, cols, dtype=bf16):
    return jax.ShapeDtypeStruct((rows, cols), dtype)


def block(i, n):
    return pl.ds(pl.multiple_of(i * n, n), n)


def head(part, h):
    at = part * MW + h * HD
    return slice(at, at + HD)


def lay_out(dst, blocks, rank, permuted):
    wide = blocks[0].shape[1]
    for j, b in enumerate(blocks):
        n = b.shape[0] // 4
        lanes = slice(j * wide, (j + 1) * wide) if rank is None else block(rank ^ j, wide)
        for i in range(4):
            at = (i ^ j if permuted else i) * n
            dst[i * n : (i + 1) * n, lanes] = b[at : at + n, :]


def out_rows(to, rank):
    return ((to >> 2) ^ rank) * 4 + (to & 3)


def norm_body(place, gain, t0, t1, t2, t3, normed, normed_t, scales):
    n = t0.shape[0]
    for j, t in enumerate((t0, t1, t2, t3)):
        wide = t[...].astype(f32)
        scale = lax.rsqrt(jnp.mean(wide * wide, axis=-1, keepdims=True) + NORM_EPSILON)
        out = (wide * scale * gain[...]).astype(bf16)
        normed[j * n : (j + 1) * n, :] = out
        normed_t[:, j * n : (j + 1) * n] = out.T
        scales[j * n : (j + 1) * n, :] = scale


def holder(place, k, m, sign):
    y, x, first = place[0], place[1], place[2] & 1
    dy, dx = jnp.where(first == 0, k, m), jnp.where(first == 0, m, k)
    return ((y + sign * dy) & 3) * 4 + ((x + sign * dx) & 3)


def project_body(place, normed, *refs):
    w, w_rel, out, enc_o = refs[8:]
    n, wide = refs[0].shape[0] // 2, w.shape[1]
    for k in range(4):
        for m in range(4):
            src, row = refs[2 * k + m // 2], (m % 2) * n
            to = holder(place, k, m, -1)
            w[block(to, n), :] = src[row : row + n, :wide]
            for i in range(2):
                w_rel[block(out_rows(to, place[2]), n // 2), i * MW : (i + 1) * MW] = src[
                    row + i * (n // 2) : row + (i + 1) * (n // 2), wide:
                ]
    for at in range(0, w.shape[1], 256):
        out[:, at : at + 256] = mm(normed[...], w[:, at : at + 256]).astype(bf16)
    for h in range(MY):
        q = latent_rows(out, head(0, h))
        p = softmax(mm_nt(q, out[:, head(1, h)]) * FACTOR)
        enc_o[:, head(0, h)] = mm(p.astype(bf16), out[:, head(2, h)]).astype(bf16)


def upstream_body(place, u0, u1, u2, u3, b0, b1, b2, b3, up_o, w_row):
    lay_out(w_row, (b0, b1, b2, b3), place[2], False)
    n = u0.shape[0]
    for j, u in enumerate((u0, u1, u2, u3)):
        up_o[j * n : (j + 1) * n, :] = mm_nt(u[...], w_row[...]).astype(bf16)


def latent_rows(ref, lanes):
    half = ref.shape[0] // 8
    return jnp.concatenate(
        [ref[(2 * i + 1) * half : (2 * i + 2) * half, lanes] for i in range(4)], 0
    )


def softmax(scores):
    raised = jnp.exp(scores - jnp.max(scores, axis=-1, keepdims=True))
    return raised * (1.0 / jnp.sum(raised, axis=-1, keepdims=True))


def latents_body(place, t0, t1, t2, t3, o0, o1, o2, o3, w_rel, z, o_all):
    rank = place[2]
    lay_out(o_all, (o0, o1, o2, o3), None, True)
    half, cols = t0.shape[0] // 2, z.shape[1]
    added = mm(o_all[...], w_rel[...])
    for j, t in enumerate((t0, t1, t2, t3)):
        rows = slice(j * half, (j + 1) * half)
        z[rows, :] = (t[half:, block(rank, cols)].astype(f32) + added[rows]).astype(bf16)


def weight_parts(place, normed_t, d_proj, d_out, outs, extra):
    n = outs[0].shape[0] // 2
    wide, m_out = d_proj.shape[1], n // 2
    for k in range(4):
        for m in range(4):
            to = holder(place, k, m, 1)
            part = mm(normed_t[block(to, n), :], d_proj[...])
            o, row = outs[2 * k + m // 2], (m % 2) * n
            if extra is not None:
                nz_t, d_kvz = extra
                more = mm(nz_t[block(to, n), :], d_kvz[...])
                part = jnp.concatenate([part[:, :MW], part[:, MW:] + more], 1)
            o[row : row + n, :wide] = part.astype(bf16)
            for i in range(2):
                o[row + i * m_out : row + (i + 1) * m_out, wide:] = d_out[
                    block(out_rows(to, place[2]), m_out), i * MW : (i + 1) * MW
                ]


def encoder_back_body(place, d0, d1, d2, d3, w_row, proj, normed_t, o_all, *refs):
    d_proj, outs, (d_z, up, d_out) = refs[0], refs[1:9], refs[9:]
    lat = d_z.shape[0]
    half = lat // 4
    for j, d in enumerate((d0, d1, d2, d3)):
        d_z[j * half : (j + 1) * half, :] = d[...]
    up[...] = mm_nt(d_z[...], w_row[...]).astype(bf16)
    for h in range(MY):
        q = latent_rows(proj, head(0, h))
        k, v = proj[:, head(1, h)], proj[:, head(2, h)]
        u = up[:, head(0, h)]
        p = softmax(mm_nt(q, k) * FACTOR)
        dp = mm_nt(u, v)
        delta = jnp.sum(dp * p, axis=-1, keepdims=True)
        ds = (p * (dp - delta) * FACTOR).astype(bf16)
        dq = mm(ds, k).astype(bf16)
        for i in range(4):
            at = 2 * i * half
            d_proj[at : at + half, head(0, h)] = jnp.zeros((half, HD), bf16)
            d_proj[at + half : at + 2 * half, head(0, h)] = dq[i * half : (i + 1) * half]
        d_proj[:, head(1, h)] = mm_tn(ds, q).astype(bf16)
        d_proj[:, head(2, h)] = mm_tn(p.astype(bf16), u).astype(bf16)
    d_out[...] = mm_tn(o_all[...], d_z[:, block(place[2], d_out.shape[1])]).astype(bf16)
    weight_parts(place, normed_t, d_proj, d_out, outs, None)


def decoder_back_body(place, d_proj, d_kvz, nz, normed_t, *refs):
    ups, os, outs, (nz_t, o_all, d_out, up) = refs[:4], refs[4:8], refs[8:16], refs[16:]
    for at in range(0, nz.shape[1], 512):
        nz_t[at : at + 512, :] = nz[:, at : at + 512].T
    lay_out(o_all, os, None, True)
    n, cols = ups[0].shape[0], d_out.shape[1]
    for j, u in enumerate(ups):
        up[j * n : (j + 1) * n, :] = u[:, block(place[2], cols)]
    d_out[...] = mm_tn(o_all[...], up[...]).astype(bf16)
    weight_parts(place, normed_t, d_proj, d_out, outs, (nz_t, d_kvz))


def decoder_body(place, gain, z0, z1, z2, z3, w, proj, up, *refs):
    out, d_proj, d_kvz, nz, scales, z_own, own, near, z_gain, z, kvz, acc = refs
    lat, width = z.shape
    half = lat // 4
    lay_out(z, (z0, z1, z2, z3), place[2], True)
    z_own[...] = z[:half, :]
    for i in range(4):
        rows = slice(i * half, (i + 1) * half)
        wide = z[rows, :].astype(f32)
        scale = lax.rsqrt(jnp.mean(wide * wide, axis=-1, keepdims=True) + NORM_EPSILON)
        nz[rows, :] = (wide * scale * gain[...]).astype(bf16)
        scales[rows, :] = scale
    kvz[...] = mm(nz[...], w[:, MW:]).astype(bf16)
    views = proj.shape[0] // 128
    for h in range(MY):
        kz, vz = kvz[:, head(0, h)], kvz[:, head(1, h)]
        for i in range(views):
            rows = slice(i * 128, (i + 1) * 128)
            q, k, v = [proj[rows, head(part, h)] for part in range(3)]
            u = up[rows, head(0, h)]
            s = mm_nt(q, kz) * FACTOR
            t = mm_nt(q, k) * FACTOR
            top = jnp.maximum(
                jnp.max(s, axis=-1, keepdims=True), jnp.max(t, axis=-1, keepdims=True)
            )
            s, t = jnp.exp(s - top), jnp.exp(t - top)
            total = jnp.sum(s, axis=-1, keepdims=True) + jnp.sum(t, axis=-1, keepdims=True)
            s, t = s * (1.0 / total), t * (1.0 / total)
            sb, tb = s.astype(bf16), t.astype(bf16)
            out[rows, head(0, h)] = (mm(sb, vz) + mm(tb, v)).astype(bf16)
            ds, dt = mm_nt(u, vz), mm_nt(u, v)
            delta = jnp.sum(ds * s, axis=-1, keepdims=True) + jnp.sum(dt * t, axis=-1, keepdims=True)
            ds = (s * (ds - delta) * FACTOR).astype(bf16)
            dt = (t * (dt - delta) * FACTOR).astype(bf16)
            d_proj[rows, head(0, h)] = (mm(ds, kz) + mm(dt, k)).astype(bf16)
            d_proj[rows, head(1, h)] = mm_tn(dt, q).astype(bf16)
            d_proj[rows, head(2, h)] = mm_tn(tb, u).astype(bf16)
            dkz, dvz = mm_tn(ds, q), mm_tn(sb, u)
            if i > 0:
                dkz, dvz = dkz + acc[:, head(0, h)], dvz + acc[:, head(1, h)]
            acc[:, head(0, h)], acc[:, head(1, h)] = dkz, dvz
    d_kvz[...] = acc[...].astype(bf16)
    z_gain[...] = jnp.zeros(z_gain.shape, f32)
    z_rows = [z.at[i * half : (i + 1) * half, :] for i in range(4)]
    sums_for_render(d_kvz, w, MW, own, near, z_rows, scales, z_gain)


def sums_for_render(grads, w, first, own, near, rows, scales, gain):
    n = grads.shape[0] // 4
    for at in range(0, w.shape[0], 512):
        cols = slice(at, at + 512)
        got = mm_nt(grads[...], w[cols, first:])
        for i, r in enumerate(rows):
            part = got[i * n : (i + 1) * n]
            term = part * (r[:, cols].astype(f32) * scales[i * n : (i + 1) * n, :])
            gain[:, cols] += jnp.sum(term, axis=0, keepdims=True)
            half = slice(i // 2 * n, (i // 2 + 1) * n)
            (near if i % 2 else own)[half, cols] = part.astype(bf16)


def input_grads_body(place, d_proj, w, scales, z_gain, t0, t1, t2, t3, own, near, gain):
    gain[...] = z_gain[...]
    sums_for_render(d_proj, w, 0, own, near, (t0, t1, t2, t3), scales, gain)


def totals_body(place, t0, t1, t2, t3, qkv, out):
    half = out.shape[0]
    for j, t in enumerate((t0, t1, t2, t3)):
        rank = place[2] ^ j
        for part in range(3):
            qkv[:, block(part * 4 + rank, MW)] = t[:, part * MW : (part + 1) * MW].astype(f32)
        for i in range(2):
            rows = slice(i * half, (i + 1) * half)
            out[:, block(rank * 2 + i, MW)] = t[rows, 3 * MW :].astype(f32)


def shards(section_tokens, w_qkv, w_out, gains, cotangent):
    tokens = section_tokens[0, 0]
    upstream = cotangent[0]
    rank = lax.axis_index("zl") * 2 + lax.axis_index("core")
    place = jnp.stack([lax.axis_index("y"), lax.axis_index("x"), rank]).astype(jnp.int32)
    is_encoder = lax.axis_index("section") == 0
    n, width = tokens.shape
    half, cols, count, lat = n // 2, width // 4, 4 * n, 2 * n

    own_cols = [
        lax.dynamic_slice_in_dim(w_qkv[0], part * 4 * MW + rank * MW, MW, 1) for part in range(3)
    ]
    own_out = [lax.dynamic_slice_in_dim(w_out[0], rank * cols + i * MW, MW, 1) for i in range(2)]
    near = gather_near(jnp.concatenate([*own_cols, jnp.concatenate(own_out, 0)], 1))
    rows = gather_rel(tokens)
    near, rows[2] = lax.optimization_barrier((near, rows[2]))
    w_parts = gather_far(near)
    normed, normed_t, scales = kernel_call(
        norm_body, place, [gains, *rows],
        [shape(count, width), shape(width, count), shape(count, 1, f32)], 8 * count * width,
    )
    ups = gather_rel(after(upstream, w_parts[2]))
    w_h, w_rel, projected, enc_o = kernel_call(
        project_body, place, [normed, *w_parts],
        [shape(width, 3 * MW), shape(4 * MW, cols), shape(count, 3 * MW), shape(lat, MW)],
        6 * count * width * MW + 4 * lat * count * MW,
    )
    w_row_blocks = spread_rel([w_rel[j * MW : (j + 1) * MW] for j in range(4)])
    enc_blocks = gather_rel(enc_o)
    enc_blocks[1], ups = lax.optimization_barrier((enc_blocks[1], ups))
    z_cols, enc_all = kernel_call(
        latents_body, place, [*rows, *enc_blocks, w_rel],
        [shape(lat, cols), shape(lat, 4 * MW)], 8 * lat * cols * MW,
    )
    z_crossed = cross_section(z_cols, 0)
    up_o, w_row = kernel_call(
        upstream_body, place, [*ups, *w_row_blocks],
        [shape(count, MW), shape(MW, width)], 2 * count * width * MW,
    )
    z_blocks = gather_rel(after(z_crossed, up_o))
    z_blocks = z_blocks[2:] + z_blocks[:2]

    decoder_shapes = [
        shape(count, MW), shape(count, 3 * MW), shape(lat, 2 * MW), shape(lat, width),
        shape(lat, 1, f32), shape(half, width), shape(2 * half, width), shape(2 * half, width),
        shape(1, width, f32),
    ]
    dec_o, d_proj, d_kvz, nz, z_scale, z_own, own, near, z_gain = lax.cond(
        is_encoder,
        lambda: tuple(jnp.zeros(s.shape, s.dtype) for s in decoder_shapes),
        lambda: tuple(kernel_call(
            decoder_body, place, [gains, *z_blocks, w_h, projected, up_o], decoder_shapes,
            8 * lat * width * MW + 12 * count * (lat + 128) * MW,
            [pltpu.VMEM((lat, width), bf16), pltpu.VMEM((lat, 2 * MW), bf16),
             pltpu.VMEM((lat, 2 * MW), f32)],
        )),
    )
    d_nz = sum_far(*sum_near(own, near))
    d_z = norm_back(z_own, z_scale[:half], gains[0], d_nz)
    d_z = d_z.astype(bf16)
    dec_blocks = gather_rel(after(dec_o, d_z))
    d_z = cross_section(d_z, 1)
    d_z_blocks = gather_rel(after(d_z, *dec_blocks))
    d_z_blocks = d_z_blocks[2:] + d_z_blocks[:2]
    d_z = d_z_blocks[0]

    part_shapes = [shape(2 * n, width // 2)] * 8
    back_flops = 6 * width * count * MW + 2 * lat * width * MW
    d_proj, *parts = lax.cond(
        is_encoder,
        lambda: tuple(kernel_call(
            encoder_back_body, place, [*d_z_blocks, w_row, projected, normed_t, enc_all],
            [shape(count, 3 * MW)] + part_shapes, back_flops + 2 * lat * width * MW + 10 * lat * count * MW,
            [pltpu.VMEM((lat, width), bf16), pltpu.VMEM((lat, MW), bf16),
             pltpu.VMEM((4 * MW, cols), bf16)],
        )),
        lambda: (d_proj, *kernel_call(
            decoder_back_body, place, [d_proj, d_kvz, nz, normed_t, *ups, *dec_blocks],
            part_shapes, back_flops + 4 * lat * width * MW,
            [pltpu.VMEM((width, lat), bf16), pltpu.VMEM((count, 4 * MW), bf16),
             pltpu.VMEM((4 * MW, cols), bf16), pltpu.VMEM((count, cols), bf16)],
        )),
    )
    parts = ring_sum_far(parts)
    own, near, gain_part = kernel_call(
        input_grads_body, place, [d_proj, w_h, scales, z_gain, *rows],
        [shape(2 * n, width)] * 2 + [shape(1, width, f32)], 6 * count * width * MW,
    )
    d_n, far = sum_near(own, near)
    parts, far = lax.optimization_barrier((parts, far))
    d_n = sum_far(d_n, far)
    gain_total = sum_everywhere(gain_part)
    sums = ring_sum_near(parts)
    sums_far, gain_total, d_n = lax.optimization_barrier((z_swap(sums), gain_total, d_n))
    qkv_total, out_total = kernel_call(
        totals_body, place, [sums, core_swap(sums), sums_far, core_swap(sums_far)],
        [shape(n, 12 * MW, f32), shape(half, width, f32)], n * width,
    )
    back = norm_back(tokens, scales[:n], gains[0], d_n)
    residual = jnp.where(
        is_encoder,
        jnp.pad(d_z.astype(f32), ((half, 0), (0, 0))),
        upstream.astype(f32),
    )
    token_grad = (back + residual).astype(bf16)
    return token_grad[None, None], qkv_total[None], out_total[None], gain_total


def solution(mesh):
    fine = Mesh(mesh.devices.reshape(2, 2, 2, 4, 4), ("section", "zl", "core", "y", "x"))
    in_specs = (
        P("section", DP, RENDER, None),
        P("section", DP, None),
        P("section", DP, None),
        P("section", None),
        P(DP, RENDER, None),
    )
    out_specs = (
        P("section", DP, RENDER, None),
        P("section", DP, None),
        P("section", DP, None),
        P("section", None),
    )
    return jax.shard_map(shards, mesh=fine, in_specs=in_specs, out_specs=out_specs, check_vma=False)
```

```python
import math

import jax
import jax.numpy as jnp
from jax import lax
from jax.experimental import pallas as pl
from jax.experimental.pallas import tpu as pltpu
from jax.sharding import Mesh
from jax.sharding import PartitionSpec as P

HD = 128
MY = 2
MW = MY * HD
NORM_EPSILON = 1e-06
FACTOR = HD**-0.5
RENDER = ("zl", "core")
DP = ("y", "x")
SWAP = [(0, 1), (1, 0)]
DIAG = [(0, 3), (1, 2), (2, 1), (3, 0)]
bf16 = jnp.bfloat16
f32 = jnp.float32


def mm(left, right):
    return jnp.dot(left, right, preferred_element_type=f32)


def mm_tn(left, right):
    return lax.dot_general(left, right, (((0,), (0,)), ((), ())), preferred_element_type=f32)


def mm_nt(left, right):
    return lax.dot_general(left, right, (((1,), (1,)), ((), ())), preferred_element_type=f32)


def core_swap(t):
    return lax.ppermute(t, "core", SWAP)


def z_swap(t):
    return lax.ppermute(t, "zl", SWAP)


def gather_rel(t):
    z = z_swap(t)
    c = core_swap(t)
    return [t, c, z, core_swap(z)]


def spread_rel(b):
    return [b[0], core_swap(b[1]), z_swap(b[2]), lax.ppermute(b[3], RENDER, DIAG)]


def sum_near(own, near):
    n = own.shape[0] // 2
    near = core_swap(near)
    return own[:n].astype(f32) + near[:n].astype(f32), add(own[n:], near[n:])


def sum_far(mine, far):
    return (mine + z_swap(far).astype(f32)).astype(bf16)


def add(*terms):
    return sum(t.astype(f32) for t in terms).astype(bf16)


def step(t, stage, k):
    pairs = []
    for core in range(2):
        for y in range(4):
            for x in range(4):
                to = (y, (x + k) % 4) if core == stage else ((y + k) % 4, x)
                pairs.append((core * 16 + y * 4 + x, core * 16 + to[0] * 4 + to[1]))
    return lax.ppermute(t, ("core", "y", "x"), pairs)


def after(t, *others):
    return lax.optimization_barrier((t, *others))[0]


def gather_near(mine):
    near, far, other = [step(mine, 0, k) for k in (1, 2, 3)]
    return jnp.concatenate([mine, near], 0), jnp.concatenate([far, other], 0)


def gather_far(t):
    up = [step(h, 1, 1) for h in t]
    down = [step(h, 1, -1) for h in t[::-1]][::-1]
    return [*t, *up, step(up[0], 1, 1), step(down[1], 1, -1), *down]


def ring_sum_far(blocks):
    own, after, far, before = blocks[:2], blocks[2:4], blocks[4:6], blocks[6:]
    far_up, far_down = step(far[0], 1, 1), step(far[1], 1, -1)
    up = [None, step(after[1], 1, 1)]
    down = [step(before[0], 1, -1), None]
    summed = add(after[0], far_up), add(before[1], far_down)
    up[0], down[1] = step(summed[0], 1, 1), step(summed[1], 1, -1)
    parts = []
    for m in range(4):
        n = own[0].shape[0] // 2
        rows = slice((m % 2) * n, (m % 2 + 1) * n)
        parts.append(add(*[t[m // 2][rows] for t in (own, up, down)]))
    return parts


def ring_sum_near(parts):
    return add(parts[0], *[step(parts[m], 0, m) for m in (1, 2, 3)])


def cross_section(t, source):
    pairs = [(source * 2 + i, (1 - source) * 2 + 1 - i) for i in range(2)]
    return lax.ppermute(t, ("section", "zl"), pairs)


def sum_everywhere(t):
    for axes in (RENDER, "x", "y"):
        one, two, three = [
            lax.ppermute(t, axes, [(i, i ^ bits) for i in range(4)]) for bits in (1, 2, 3)
        ]
        t = (t + one) + (two + three)
    return t


def norm_back(values, scale, gain_row, upstream):
    wide = values.astype(f32)
    grad = upstream.astype(f32)
    scaled = grad * gain_row
    inner = jnp.sum(scaled * wide, axis=-1, keepdims=True)
    result = scale * scaled - wide * scale**3 * inner / values.shape[-1]
    return result


def kernel_call(body, place, inputs, outputs, flops, scratch=()):
    moved = sum(t.size * t.dtype.itemsize for t in list(inputs) + list(outputs))
    vmem = pl.BlockSpec(memory_space=pltpu.VMEM)
    held = moved + sum(math.prod(t.shape) * 4 for t in scratch)
    return pl.pallas_call(
        body,
        out_shape=tuple(outputs),
        in_specs=[pl.BlockSpec(memory_space=pltpu.SMEM)] + [vmem] * len(inputs),
        out_specs=(vmem,) * len(outputs),
        scratch_shapes=scratch,
        compiler_params=pltpu.CompilerParams(vmem_limit_bytes=held + 6 * 2**20),
        cost_estimate=pl.CostEstimate(flops=flops, bytes_accessed=moved, transcendentals=0),
    )(place, *inputs)


def shape(rows, cols, dtype=bf16):
    return jax.ShapeDtypeStruct((rows, cols), dtype)


def block(i, n):
    return pl.ds(pl.multiple_of(i * n, n), n)


def head(part, h):
    at = part * MW + h * HD
    return slice(at, at + HD)


def lay_out(dst, blocks, rank, permuted):
    wide = blocks[0].shape[1]
    for j, b in enumerate(blocks):
        n = b.shape[0] // 4
        lanes = slice(j * wide, (j + 1) * wide) if rank is None else block(rank ^ j, wide)
        for i in range(4):
            at = (i ^ j if permuted else i) * n
            dst[i * n : (i + 1) * n, lanes] = b[at : at + n, :]


def out_rows(to, rank):
    return ((to >> 2) ^ rank) * 4 + (to & 3)


def norm_body(place, gain, t0, t1, t2, t3, normed, normed_t, scales):
    n = t0.shape[0]
    for j, t in enumerate((t0, t1, t2, t3)):
        wide = t[...].astype(f32)
        scale = lax.rsqrt(jnp.mean(wide * wide, axis=-1, keepdims=True) + NORM_EPSILON)
        out = (wide * scale * gain[...]).astype(bf16)
        normed[j * n : (j + 1) * n, :] = out
        normed_t[:, j * n : (j + 1) * n] = out.T
        scales[j * n : (j + 1) * n, :] = scale


def holder(place, k, m, sign):
    y, x, first = place[0], place[1], place[2] & 1
    dy, dx = jnp.where(first == 0, k, m), jnp.where(first == 0, m, k)
    return ((y + sign * dy) & 3) * 4 + ((x + sign * dx) & 3)


def project_body(place, normed, *refs):
    w, w_rel, out, enc_o = refs[8:]
    n, wide = refs[0].shape[0] // 2, w.shape[1]
    for k in range(4):
        for m in range(4):
            src, row = refs[2 * k + m // 2], (m % 2) * n
            to = holder(place, k, m, -1)
            w[block(to, n), :] = src[row : row + n, :wide]
            for i in range(2):
                w_rel[block(out_rows(to, place[2]), n // 2), i * MW : (i + 1) * MW] = src[
                    row + i * (n // 2) : row + (i + 1) * (n // 2), wide:
                ]
    for at in range(0, w.shape[1], 256):
        out[:, at : at + 256] = mm(normed[...], w[:, at : at + 256]).astype(bf16)
    for h in range(MY):
        q = latent_rows(out, head(0, h))
        p = softmax(mm_nt(q, out[:, head(1, h)]) * FACTOR)
        enc_o[:, head(0, h)] = mm(p.astype(bf16), out[:, head(2, h)]).astype(bf16)


def upstream_body(place, u0, u1, u2, u3, b0, b1, b2, b3, up_o, w_row):
    lay_out(w_row, (b0, b1, b2, b3), place[2], False)
    n = u0.shape[0]
    for j, u in enumerate((u0, u1, u2, u3)):
        up_o[j * n : (j + 1) * n, :] = mm_nt(u[...], w_row[...]).astype(bf16)


def latent_rows(ref, lanes):
    half = ref.shape[0] // 8
    return jnp.concatenate(
        [ref[(2 * i + 1) * half : (2 * i + 2) * half, lanes] for i in range(4)], 0
    )


def softmax(scores):
    raised = jnp.exp(scores - jnp.max(scores, axis=-1, keepdims=True))
    return raised * (1.0 / jnp.sum(raised, axis=-1, keepdims=True))


def latents_body(place, t0, t1, t2, t3, o0, o1, o2, o3, w_rel, z, o_all):
    rank = place[2]
    lay_out(o_all, (o0, o1, o2, o3), None, True)
    half, cols = t0.shape[0] // 2, z.shape[1]
    added = mm(o_all[...], w_rel[...])
    for j, t in enumerate((t0, t1, t2, t3)):
        rows = slice(j * half, (j + 1) * half)
        z[rows, :] = (t[half:, block(rank, cols)].astype(f32) + added[rows]).astype(bf16)


def weight_parts(place, normed_t, d_proj, d_out, outs, extra):
    n = outs[0].shape[0] // 2
    wide, m_out = d_proj.shape[1], n // 2
    for k in range(4):
        for m in range(4):
            to = holder(place, k, m, 1)
            part = mm(normed_t[block(to, n), :], d_proj[...])
            o, row = outs[2 * k + m // 2], (m % 2) * n
            if extra is not None:
                nz_t, d_kvz = extra
                more = mm(nz_t[block(to, n), :], d_kvz[...])
                part = jnp.concatenate([part[:, :MW], part[:, MW:] + more], 1)
            o[row : row + n, :wide] = part.astype(bf16)
            for i in range(2):
                o[row + i * m_out : row + (i + 1) * m_out, wide:] = d_out[
                    block(out_rows(to, place[2]), m_out), i * MW : (i + 1) * MW
                ]


def encoder_back_body(place, d0, d1, d2, d3, w_row, proj, normed_t, o_all, *refs):
    d_proj, outs, (d_z, up, d_out) = refs[0], refs[1:9], refs[9:]
    lat = d_z.shape[0]
    half = lat // 4
    for j, d in enumerate((d0, d1, d2, d3)):
        d_z[j * half : (j + 1) * half, :] = d[...]
    up[...] = mm_nt(d_z[...], w_row[...]).astype(bf16)
    for h in range(MY):
        q = latent_rows(proj, head(0, h))
        k, v = proj[:, head(1, h)], proj[:, head(2, h)]
        u = up[:, head(0, h)]
        p = softmax(mm_nt(q, k) * FACTOR)
        dp = mm_nt(u, v)
        delta = jnp.sum(dp * p, axis=-1, keepdims=True)
        ds = (p * (dp - delta) * FACTOR).astype(bf16)
        dq = mm(ds, k).astype(bf16)
        for i in range(4):
            at = 2 * i * half
            d_proj[at : at + half, head(0, h)] = jnp.zeros((half, HD), bf16)
            d_proj[at + half : at + 2 * half, head(0, h)] = dq[i * half : (i + 1) * half]
        d_proj[:, head(1, h)] = mm_tn(ds, q).astype(bf16)
        d_proj[:, head(2, h)] = mm_tn(p.astype(bf16), u).astype(bf16)
    d_out[...] = mm_tn(o_all[...], d_z[:, block(place[2], d_out.shape[1])]).astype(bf16)
    weight_parts(place, normed_t, d_proj, d_out, outs, None)


def decoder_back_body(place, d_proj, d_kvz, nz, normed_t, *refs):
    ups, os, outs, (nz_t, o_all, d_out, up) = refs[:4], refs[4:8], refs[8:16], refs[16:]
    for at in range(0, nz.shape[1], 512):
        nz_t[at : at + 512, :] = nz[:, at : at + 512].T
    lay_out(o_all, os, None, True)
    n, cols = ups[0].shape[0], d_out.shape[1]
    for j, u in enumerate(ups):
        up[j * n : (j + 1) * n, :] = u[:, block(place[2], cols)]
    d_out[...] = mm_tn(o_all[...], up[...]).astype(bf16)
    weight_parts(place, normed_t, d_proj, d_out, outs, (nz_t, d_kvz))


def decoder_body(place, gain, z0, z1, z2, z3, w, proj, up, *refs):
    out, d_proj, d_kvz, nz, scales, z_own, own, near, z_gain, z, kvz, acc = refs
    lat, width = z.shape
    half = lat // 4
    lay_out(z, (z0, z1, z2, z3), place[2], True)
    z_own[...] = z[:half, :]
    for i in range(4):
        rows = slice(i * half, (i + 1) * half)
        wide = z[rows, :].astype(f32)
        scale = lax.rsqrt(jnp.mean(wide * wide, axis=-1, keepdims=True) + NORM_EPSILON)
        nz[rows, :] = (wide * scale * gain[...]).astype(bf16)
        scales[rows, :] = scale
    kvz[...] = mm(nz[...], w[:, MW:]).astype(bf16)
    views = proj.shape[0] // 128
    for h in range(MY):
        kz, vz = kvz[:, head(0, h)], kvz[:, head(1, h)]
        for i in range(views):
            rows = slice(i * 128, (i + 1) * 128)
            q, k, v = [proj[rows, head(part, h)] for part in range(3)]
            u = up[rows, head(0, h)]
            s = mm_nt(q, kz) * FACTOR
            t = mm_nt(q, k) * FACTOR
            top = jnp.maximum(
                jnp.max(s, axis=-1, keepdims=True), jnp.max(t, axis=-1, keepdims=True)
            )
            s, t = jnp.exp(s - top), jnp.exp(t - top)
            total = jnp.sum(s, axis=-1, keepdims=True) + jnp.sum(t, axis=-1, keepdims=True)
            s, t = s * (1.0 / total), t * (1.0 / total)
            sb, tb = s.astype(bf16), t.astype(bf16)
            out[rows, head(0, h)] = (mm(sb, vz) + mm(tb, v)).astype(bf16)
            ds, dt = mm_nt(u, vz), mm_nt(u, v)
            delta = jnp.sum(ds * s, axis=-1, keepdims=True) + jnp.sum(dt * t, axis=-1, keepdims=True)
            ds = (s * (ds - delta) * FACTOR).astype(bf16)
            dt = (t * (dt - delta) * FACTOR).astype(bf16)
            d_proj[rows, head(0, h)] = (mm(ds, kz) + mm(dt, k)).astype(bf16)
            d_proj[rows, head(1, h)] = mm_tn(dt, q).astype(bf16)
            d_proj[rows, head(2, h)] = mm_tn(tb, u).astype(bf16)
            dkz, dvz = mm_tn(ds, q), mm_tn(sb, u)
            if i > 0:
                dkz, dvz = dkz + acc[:, head(0, h)], dvz + acc[:, head(1, h)]
            acc[:, head(0, h)], acc[:, head(1, h)] = dkz, dvz
    d_kvz[...] = acc[...].astype(bf16)
    z_gain[...] = jnp.zeros(z_gain.shape, f32)
    z_rows = [z.at[i * half : (i + 1) * half, :] for i in range(4)]
    sums_for_render(d_kvz, w, MW, own, near, z_rows, scales, z_gain)


def sums_for_render(grads, w, first, own, near, rows, scales, gain):
    n = grads.shape[0] // 4
    for at in range(0, w.shape[0], 512):
        cols = slice(at, at + 512)
        got = mm_nt(grads[...], w[cols, first:])
        for i, r in enumerate(rows):
            part = got[i * n : (i + 1) * n]
            term = part * (r[:, cols].astype(f32) * scales[i * n : (i + 1) * n, :])
            gain[:, cols] += jnp.sum(term, axis=0, keepdims=True)
            half = slice(i // 2 * n, (i // 2 + 1) * n)
            (near if i % 2 else own)[half, cols] = part.astype(bf16)


def input_grads_body(place, d_proj, w, scales, z_gain, t0, t1, t2, t3, own, near, gain):
    gain[...] = z_gain[...]
    sums_for_render(d_proj, w, 0, own, near, (t0, t1, t2, t3), scales, gain)


def totals_body(place, t0, t1, t2, t3, qkv, out):
    half = out.shape[0]
    for j, t in enumerate((t0, t1, t2, t3)):
        rank = place[2] ^ j
        for part in range(3):
            qkv[:, block(part * 4 + rank, MW)] = t[:, part * MW : (part + 1) * MW].astype(f32)
        for i in range(2):
            rows = slice(i * half, (i + 1) * half)
            out[:, block(rank * 2 + i, MW)] = t[rows, 3 * MW :].astype(f32)


def shards(section_tokens, w_qkv, w_out, gains, cotangent):
    tokens = section_tokens[0, 0]
    upstream = cotangent[0]
    rank = lax.axis_index("zl") * 2 + lax.axis_index("core")
    place = jnp.stack([lax.axis_index("y"), lax.axis_index("x"), rank]).astype(jnp.int32)
    is_encoder = lax.axis_index("section") == 0
    n, width = tokens.shape
    half, cols, count, lat = n // 2, width // 4, 4 * n, 2 * n

    own_cols = [
        lax.dynamic_slice_in_dim(w_qkv[0], part * 4 * MW + rank * MW, MW, 1) for part in range(3)
    ]
    own_out = [lax.dynamic_slice_in_dim(w_out[0], rank * cols + i * MW, MW, 1) for i in range(2)]
    near = gather_near(jnp.concatenate([*own_cols, jnp.concatenate(own_out, 0)], 1))
    rows = gather_rel(tokens)
    near, rows[2] = lax.optimization_barrier((near, rows[2]))
    w_parts = gather_far(near)
    normed, normed_t, scales = kernel_call(
        norm_body, place, [gains, *rows],
        [shape(count, width), shape(width, count), shape(count, 1, f32)], 8 * count * width,
    )
    ups = gather_rel(after(upstream, w_parts[2]))
    w_h, w_rel, projected, enc_o = kernel_call(
        project_body, place, [normed, *w_parts],
        [shape(width, 3 * MW), shape(4 * MW, cols), shape(count, 3 * MW), shape(lat, MW)],
        6 * count * width * MW + 4 * lat * count * MW,
    )
    w_row_blocks = spread_rel([w_rel[j * MW : (j + 1) * MW] for j in range(4)])
    enc_blocks = gather_rel(enc_o)
    enc_blocks[1], ups = lax.optimization_barrier((enc_blocks[1], ups))
    z_cols, enc_all = kernel_call(
        latents_body, place, [*rows, *enc_blocks, w_rel],
        [shape(lat, cols), shape(lat, 4 * MW)], 8 * lat * cols * MW,
    )
    z_crossed = cross_section(z_cols, 0)
    up_o, w_row = kernel_call(
        upstream_body, place, [*ups, *w_row_blocks],
        [shape(count, MW), shape(MW, width)], 2 * count * width * MW,
    )
    z_blocks = gather_rel(after(z_crossed, up_o))
    z_blocks = z_blocks[2:] + z_blocks[:2]

    decoder_shapes = [
        shape(count, MW), shape(count, 3 * MW), shape(lat, 2 * MW), shape(lat, width),
        shape(lat, 1, f32), shape(half, width), shape(2 * half, width), shape(2 * half, width),
        shape(1, width, f32),
    ]
    dec_o, d_proj, d_kvz, nz, z_scale, z_own, own, near, z_gain = lax.cond(
        is_encoder,
        lambda: tuple(jnp.zeros(s.shape, s.dtype) for s in decoder_shapes),
        lambda: tuple(kernel_call(
            decoder_body, place, [gains, *z_blocks, w_h, projected, up_o], decoder_shapes,
            8 * lat * width * MW + 12 * count * (lat + 128) * MW,
            [pltpu.VMEM((lat, width), bf16), pltpu.VMEM((lat, 2 * MW), bf16),
             pltpu.VMEM((lat, 2 * MW), f32)],
        )),
    )
    d_nz = sum_far(*sum_near(own, near))
    d_z = norm_back(z_own, z_scale[:half], gains[0], d_nz)
    d_z = d_z.astype(bf16)
    dec_blocks = gather_rel(after(dec_o, d_z))
    d_z = cross_section(d_z, 1)
    d_z_blocks = gather_rel(after(d_z, *dec_blocks))
    d_z_blocks = d_z_blocks[2:] + d_z_blocks[:2]
    d_z = d_z_blocks[0]

    part_shapes = [shape(2 * n, width // 2)] * 8
    back_flops = 6 * width * count * MW + 2 * lat * width * MW
    d_proj, *parts = lax.cond(
        is_encoder,
        lambda: tuple(kernel_call(
            encoder_back_body, place, [*d_z_blocks, w_row, projected, normed_t, enc_all],
            [shape(count, 3 * MW)] + part_shapes, back_flops + 2 * lat * width * MW + 10 * lat * count * MW,
            [pltpu.VMEM((lat, width), bf16), pltpu.VMEM((lat, MW), bf16),
             pltpu.VMEM((4 * MW, cols), bf16)],
        )),
        lambda: (d_proj, *kernel_call(
            decoder_back_body, place, [d_proj, d_kvz, nz, normed_t, *ups, *dec_blocks],
            part_shapes, back_flops + 4 * lat * width * MW,
            [pltpu.VMEM((width, lat), bf16), pltpu.VMEM((count, 4 * MW), bf16),
             pltpu.VMEM((4 * MW, cols), bf16), pltpu.VMEM((count, cols), bf16)],
        )),
    )
    parts = ring_sum_far(parts)
    own, near, gain_part = kernel_call(
        input_grads_body, place, [d_proj, w_h, scales, z_gain, *rows],
        [shape(2 * n, width)] * 2 + [shape(1, width, f32)], 6 * count * width * MW,
    )
    d_n, far = sum_near(own, near)
    parts, far, gain_part = lax.optimization_barrier((parts, far, gain_part))
    d_n = sum_far(d_n, far)
    sums = ring_sum_near(parts)
    gain_total = sum_everywhere(after(gain_part, sums))
    sums_far, d_n = lax.optimization_barrier((z_swap(sums), d_n))
    qkv_total, out_total = kernel_call(
        totals_body, place, [sums, core_swap(sums), sums_far, core_swap(sums_far)],
        [shape(n, 12 * MW, f32), shape(half, width, f32)], n * width,
    )
    back = norm_back(tokens, scales[:n], gains[0], d_n)
    residual = jnp.where(
        is_encoder,
        jnp.pad(d_z.astype(f32), ((half, 0), (0, 0))),
        upstream.astype(f32),
    )
    token_grad = (back + residual).astype(bf16)
    return token_grad[None, None], qkv_total[None], out_total[None], gain_total


def solution(mesh):
    fine = Mesh(mesh.devices.reshape(2, 2, 2, 4, 4), ("section", "zl", "core", "y", "x"))
    in_specs = (
        P("section", DP, RENDER, None),
        P("section", DP, None),
        P("section", DP, None),
        P("section", None),
        P(DP, RENDER, None),
    )
    out_specs = (
        P("section", DP, RENDER, None),
        P("section", DP, None),
        P("section", DP, None),
        P("section", None),
    )
    return jax.shard_map(shards, mesh=fine, in_specs=in_specs, out_specs=out_specs, check_vma=False)
```

```python
import math

import jax
import jax.numpy as jnp
from jax import lax
from jax.experimental import pallas as pl
from jax.experimental.pallas import tpu as pltpu
from jax.sharding import Mesh
from jax.sharding import PartitionSpec as P

HD = 128
MY = 2
MW = MY * HD
NORM_EPSILON = 1e-06
FACTOR = HD**-0.5
RENDER = ("zl", "core")
DP = ("y", "x")
SWAP = [(0, 1), (1, 0)]
DIAG = [(0, 3), (1, 2), (2, 1), (3, 0)]
bf16 = jnp.bfloat16
f32 = jnp.float32


def mm(left, right):
    return jnp.dot(left, right, preferred_element_type=f32)


def mm_tn(left, right):
    return lax.dot_general(left, right, (((0,), (0,)), ((), ())), preferred_element_type=f32)


def mm_nt(left, right):
    return lax.dot_general(left, right, (((1,), (1,)), ((), ())), preferred_element_type=f32)


def core_swap(t):
    return lax.ppermute(t, "core", SWAP)


def z_swap(t):
    return lax.ppermute(t, "zl", SWAP)


def gather_rel(t):
    z = z_swap(t)
    c = core_swap(t)
    return [t, c, z, core_swap(z)]


def spread_rel(b):
    return [b[0], core_swap(b[1]), z_swap(b[2]), lax.ppermute(b[3], RENDER, DIAG)]


def sum_near(own, near):
    n = own.shape[0] // 2
    near = core_swap(near)
    return own[:n].astype(f32) + near[:n].astype(f32), add(own[n:], near[n:])


def sum_far(mine, far):
    return (mine + z_swap(far).astype(f32)).astype(bf16)


def add(*terms):
    return sum(t.astype(f32) for t in terms).astype(bf16)


def step(t, stage, k):
    pairs = []
    for core in range(2):
        for y in range(4):
            for x in range(4):
                to = (y, (x + k) % 4) if core == stage else ((y + k) % 4, x)
                pairs.append((core * 16 + y * 4 + x, core * 16 + to[0] * 4 + to[1]))
    return lax.ppermute(t, ("core", "y", "x"), pairs)


def after(t, *others):
    return lax.optimization_barrier((t, *others))[0]


def gather_near(mine):
    near, far, other = [step(mine, 0, k) for k in (1, 2, 3)]
    return jnp.concatenate([mine, near], 0), jnp.concatenate([far, other], 0)


def gather_far(t):
    up = [step(h, 1, 1) for h in t]
    down = [step(h, 1, -1) for h in t[::-1]][::-1]
    return [*t, *up, step(up[0], 1, 1), step(down[1], 1, -1), *down]


def ring_sum_far(blocks):
    own, after, far, before = blocks[:2], blocks[2:4], blocks[4:6], blocks[6:]
    far_up, far_down = step(far[0], 1, 1), step(far[1], 1, -1)
    up = [None, step(after[1], 1, 1)]
    down = [step(before[0], 1, -1), None]
    summed = add(after[0], far_up), add(before[1], far_down)
    up[0], down[1] = step(summed[0], 1, 1), step(summed[1], 1, -1)
    parts = []
    for m in range(4):
        n = own[0].shape[0] // 2
        rows = slice((m % 2) * n, (m % 2 + 1) * n)
        parts.append(add(*[t[m // 2][rows] for t in (own, up, down)]))
    return parts


def ring_sum_near(parts):
    return add(parts[0], *[step(parts[m], 0, m) for m in (1, 2, 3)])


def cross_section(t, source):
    pairs = [(source * 2 + i, (1 - source) * 2 + 1 - i) for i in range(2)]
    return lax.ppermute(t, ("section", "zl"), pairs)


def sum_over_render(t):
    t = t + core_swap(t)
    return t + z_swap(t)


def sum_over_dp(t):
    blocks = jnp.broadcast_to(t[None], (16, *t.shape))
    return lax.all_to_all(blocks, DP, 0, 0, tiled=True).sum(axis=0)


def norm_back(values, scale, gain_row, upstream):
    wide = values.astype(f32)
    grad = upstream.astype(f32)
    scaled = grad * gain_row
    inner = jnp.sum(scaled * wide, axis=-1, keepdims=True)
    result = scale * scaled - wide * scale**3 * inner / values.shape[-1]
    return result


def kernel_call(body, place, inputs, outputs, flops, scratch=()):
    moved = sum(t.size * t.dtype.itemsize for t in list(inputs) + list(outputs))
    vmem = pl.BlockSpec(memory_space=pltpu.VMEM)
    held = moved + sum(math.prod(t.shape) * 4 for t in scratch)
    return pl.pallas_call(
        body,
        out_shape=tuple(outputs),
        in_specs=[pl.BlockSpec(memory_space=pltpu.SMEM)] + [vmem] * len(inputs),
        out_specs=(vmem,) * len(outputs),
        scratch_shapes=scratch,
        compiler_params=pltpu.CompilerParams(vmem_limit_bytes=held + 6 * 2**20),
        cost_estimate=pl.CostEstimate(flops=flops, bytes_accessed=moved, transcendentals=0),
    )(place, *inputs)


def shape(rows, cols, dtype=bf16):
    return jax.ShapeDtypeStruct((rows, cols), dtype)


def block(i, n):
    return pl.ds(pl.multiple_of(i * n, n), n)


def head(part, h):
    at = part * MW + h * HD
    return slice(at, at + HD)


def lay_out(dst, blocks, rank, permuted):
    wide = blocks[0].shape[1]
    for j, b in enumerate(blocks):
        n = b.shape[0] // 4
        lanes = slice(j * wide, (j + 1) * wide) if rank is None else block(rank ^ j, wide)
        for i in range(4):
            at = (i ^ j if permuted else i) * n
            dst[i * n : (i + 1) * n, lanes] = b[at : at + n, :]


def out_rows(to, rank):
    return ((to >> 2) ^ rank) * 4 + (to & 3)


def norm_body(place, gain, t0, t1, t2, t3, normed, normed_t, scales):
    n = t0.shape[0]
    for j, t in enumerate((t0, t1, t2, t3)):
        wide = t[...].astype(f32)
        scale = lax.rsqrt(jnp.mean(wide * wide, axis=-1, keepdims=True) + NORM_EPSILON)
        out = (wide * scale * gain[...]).astype(bf16)
        normed[j * n : (j + 1) * n, :] = out
        normed_t[:, j * n : (j + 1) * n] = out.T
        scales[j * n : (j + 1) * n, :] = scale


def holder(place, k, m, sign):
    y, x, first = place[0], place[1], place[2] & 1
    dy, dx = jnp.where(first == 0, k, m), jnp.where(first == 0, m, k)
    return ((y + sign * dy) & 3) * 4 + ((x + sign * dx) & 3)


def project_body(place, normed, *refs):
    w, w_rel, out, enc_o = refs[8:]
    n, wide = refs[0].shape[0] // 2, w.shape[1]
    for k in range(4):
        for m in range(4):
            src, row = refs[2 * k + m // 2], (m % 2) * n
            to = holder(place, k, m, -1)
            w[block(to, n), :] = src[row : row + n, :wide]
            for i in range(2):
                w_rel[block(out_rows(to, place[2]), n // 2), i * MW : (i + 1) * MW] = src[
                    row + i * (n // 2) : row + (i + 1) * (n // 2), wide:
                ]
    for at in range(0, w.shape[1], 256):
        out[:, at : at + 256] = mm(normed[...], w[:, at : at + 256]).astype(bf16)
    for h in range(MY):
        q = latent_rows(out, head(0, h))
        p = softmax(mm_nt(q, out[:, head(1, h)]) * FACTOR)
        enc_o[:, head(0, h)] = mm(p.astype(bf16), out[:, head(2, h)]).astype(bf16)


def upstream_body(place, u0, u1, u2, u3, b0, b1, b2, b3, up_o, w_row):
    lay_out(w_row, (b0, b1, b2, b3), place[2], False)
    n = u0.shape[0]
    for j, u in enumerate((u0, u1, u2, u3)):
        up_o[j * n : (j + 1) * n, :] = mm_nt(u[...], w_row[...]).astype(bf16)


def latent_rows(ref, lanes):
    half = ref.shape[0] // 8
    return jnp.concatenate(
        [ref[(2 * i + 1) * half : (2 * i + 2) * half, lanes] for i in range(4)], 0
    )


def softmax(scores):
    raised = jnp.exp(scores - jnp.max(scores, axis=-1, keepdims=True))
    return raised * (1.0 / jnp.sum(raised, axis=-1, keepdims=True))


def latents_body(place, t0, t1, t2, t3, o0, o1, o2, o3, w_rel, z, o_all):
    rank = place[2]
    lay_out(o_all, (o0, o1, o2, o3), None, True)
    half, cols = t0.shape[0] // 2, z.shape[1]
    added = mm(o_all[...], w_rel[...])
    for j, t in enumerate((t0, t1, t2, t3)):
        rows = slice(j * half, (j + 1) * half)
        z[rows, :] = (t[half:, block(rank, cols)].astype(f32) + added[rows]).astype(bf16)


def weight_parts(place, normed_t, d_proj, d_out, outs, extra):
    n = outs[0].shape[0] // 2
    wide, m_out = d_proj.shape[1], n // 2
    for k in range(4):
        for m in range(4):
            to = holder(place, k, m, 1)
            part = mm(normed_t[block(to, n), :], d_proj[...])
            o, row = outs[2 * k + m // 2], (m % 2) * n
            if extra is not None:
                nz_t, d_kvz = extra
                more = mm(nz_t[block(to, n), :], d_kvz[...])
                part = jnp.concatenate([part[:, :MW], part[:, MW:] + more], 1)
            o[row : row + n, :wide] = part.astype(bf16)
            for i in range(2):
                o[row + i * m_out : row + (i + 1) * m_out, wide:] = d_out[
                    block(out_rows(to, place[2]), m_out), i * MW : (i + 1) * MW
                ]


def encoder_back_body(place, d0, d1, d2, d3, w_row, proj, normed_t, o_all, *refs):
    d_proj, outs, (d_z, up, d_out) = refs[0], refs[1:9], refs[9:]
    lat = d_z.shape[0]
    half = lat // 4
    for j, d in enumerate((d0, d1, d2, d3)):
        d_z[j * half : (j + 1) * half, :] = d[...]
    up[...] = mm_nt(d_z[...], w_row[...]).astype(bf16)
    for h in range(MY):
        q = latent_rows(proj, head(0, h))
        k, v = proj[:, head(1, h)], proj[:, head(2, h)]
        u = up[:, head(0, h)]
        p = softmax(mm_nt(q, k) * FACTOR)
        dp = mm_nt(u, v)
        delta = jnp.sum(dp * p, axis=-1, keepdims=True)
        ds = (p * (dp - delta) * FACTOR).astype(bf16)
        dq = mm(ds, k).astype(bf16)
        for i in range(4):
            at = 2 * i * half
            d_proj[at : at + half, head(0, h)] = jnp.zeros((half, HD), bf16)
            d_proj[at + half : at + 2 * half, head(0, h)] = dq[i * half : (i + 1) * half]
        d_proj[:, head(1, h)] = mm_tn(ds, q).astype(bf16)
        d_proj[:, head(2, h)] = mm_tn(p.astype(bf16), u).astype(bf16)
    d_out[...] = mm_tn(o_all[...], d_z[:, block(place[2], d_out.shape[1])]).astype(bf16)
    weight_parts(place, normed_t, d_proj, d_out, outs, None)


def decoder_back_body(place, d_proj, d_kvz, nz, normed_t, *refs):
    ups, os, outs, (nz_t, o_all, d_out, up) = refs[:4], refs[4:8], refs[8:16], refs[16:]
    for at in range(0, nz.shape[1], 512):
        nz_t[at : at + 512, :] = nz[:, at : at + 512].T
    lay_out(o_all, os, None, True)
    n, cols = ups[0].shape[0], d_out.shape[1]
    for j, u in enumerate(ups):
        up[j * n : (j + 1) * n, :] = u[:, block(place[2], cols)]
    d_out[...] = mm_tn(o_all[...], up[...]).astype(bf16)
    weight_parts(place, normed_t, d_proj, d_out, outs, (nz_t, d_kvz))


def decoder_body(place, gain, z0, z1, z2, z3, w, proj, up, *refs):
    out, d_proj, d_kvz, nz, scales, z_own, own, near, z_gain, z, kvz, acc = refs
    lat, width = z.shape
    half = lat // 4
    lay_out(z, (z0, z1, z2, z3), place[2], True)
    z_own[...] = z[:half, :]
    for i in range(4):
        rows = slice(i * half, (i + 1) * half)
        wide = z[rows, :].astype(f32)
        scale = lax.rsqrt(jnp.mean(wide * wide, axis=-1, keepdims=True) + NORM_EPSILON)
        nz[rows, :] = (wide * scale * gain[...]).astype(bf16)
        scales[rows, :] = scale
    kvz[...] = mm(nz[...], w[:, MW:]).astype(bf16)
    views = proj.shape[0] // 128
    for h in range(MY):
        kz, vz = kvz[:, head(0, h)], kvz[:, head(1, h)]
        for i in range(views):
            rows = slice(i * 128, (i + 1) * 128)
            q, k, v = [proj[rows, head(part, h)] for part in range(3)]
            u = up[rows, head(0, h)]
            s = mm_nt(q, kz) * FACTOR
            t = mm_nt(q, k) * FACTOR
            top = jnp.maximum(
                jnp.max(s, axis=-1, keepdims=True), jnp.max(t, axis=-1, keepdims=True)
            )
            s, t = jnp.exp(s - top), jnp.exp(t - top)
            total = jnp.sum(s, axis=-1, keepdims=True) + jnp.sum(t, axis=-1, keepdims=True)
            s, t = s * (1.0 / total), t * (1.0 / total)
            sb, tb = s.astype(bf16), t.astype(bf16)
            out[rows, head(0, h)] = (mm(sb, vz) + mm(tb, v)).astype(bf16)
            ds, dt = mm_nt(u, vz), mm_nt(u, v)
            delta = jnp.sum(ds * s, axis=-1, keepdims=True) + jnp.sum(dt * t, axis=-1, keepdims=True)
            ds = (s * (ds - delta) * FACTOR).astype(bf16)
            dt = (t * (dt - delta) * FACTOR).astype(bf16)
            d_proj[rows, head(0, h)] = (mm(ds, kz) + mm(dt, k)).astype(bf16)
            d_proj[rows, head(1, h)] = mm_tn(dt, q).astype(bf16)
            d_proj[rows, head(2, h)] = mm_tn(tb, u).astype(bf16)
            dkz, dvz = mm_tn(ds, q), mm_tn(sb, u)
            if i > 0:
                dkz, dvz = dkz + acc[:, head(0, h)], dvz + acc[:, head(1, h)]
            acc[:, head(0, h)], acc[:, head(1, h)] = dkz, dvz
    d_kvz[...] = acc[...].astype(bf16)
    z_gain[...] = jnp.zeros(z_gain.shape, f32)
    z_rows = [z.at[i * half : (i + 1) * half, :] for i in range(4)]
    sums_for_render(d_kvz, w, MW, own, near, z_rows, scales, z_gain)


def sums_for_render(grads, w, first, own, near, rows, scales, gain):
    n = grads.shape[0] // 4
    for at in range(0, w.shape[0], 512):
        cols = slice(at, at + 512)
        got = mm_nt(grads[...], w[cols, first:])
        for i, r in enumerate(rows):
            part = got[i * n : (i + 1) * n]
            term = part * (r[:, cols].astype(f32) * scales[i * n : (i + 1) * n, :])
            gain[:, cols] += jnp.sum(term, axis=0, keepdims=True)
            half = slice(i // 2 * n, (i // 2 + 1) * n)
            (near if i % 2 else own)[half, cols] = part.astype(bf16)


def input_grads_body(place, d_proj, w, scales, z_gain, t0, t1, t2, t3, own, near, gain):
    gain[...] = z_gain[...]
    sums_for_render(d_proj, w, 0, own, near, (t0, t1, t2, t3), scales, gain)


def totals_body(place, t0, t1, t2, t3, qkv, out):
    half = out.shape[0]
    for j, t in enumerate((t0, t1, t2, t3)):
        rank = place[2] ^ j
        for part in range(3):
            qkv[:, block(part * 4 + rank, MW)] = t[:, part * MW : (part + 1) * MW].astype(f32)
        for i in range(2):
            rows = slice(i * half, (i + 1) * half)
            out[:, block(rank * 2 + i, MW)] = t[rows, 3 * MW :].astype(f32)


def shards(section_tokens, w_qkv, w_out, gains, cotangent):
    tokens = section_tokens[0, 0]
    upstream = cotangent[0]
    rank = lax.axis_index("zl") * 2 + lax.axis_index("core")
    place = jnp.stack([lax.axis_index("y"), lax.axis_index("x"), rank]).astype(jnp.int32)
    is_encoder = lax.axis_index("section") == 0
    n, width = tokens.shape
    half, cols, count, lat = n // 2, width // 4, 4 * n, 2 * n

    own_cols = [
        lax.dynamic_slice_in_dim(w_qkv[0], part * 4 * MW + rank * MW, MW, 1) for part in range(3)
    ]
    own_out = [lax.dynamic_slice_in_dim(w_out[0], rank * cols + i * MW, MW, 1) for i in range(2)]
    near = gather_near(jnp.concatenate([*own_cols, jnp.concatenate(own_out, 0)], 1))
    rows = gather_rel(tokens)
    near, rows[2] = lax.optimization_barrier((near, rows[2]))
    w_parts = gather_far(near)
    normed, normed_t, scales = kernel_call(
        norm_body, place, [gains, *rows],
        [shape(count, width), shape(width, count), shape(count, 1, f32)], 8 * count * width,
    )
    ups = gather_rel(after(upstream, w_parts[2]))
    w_h, w_rel, projected, enc_o = kernel_call(
        project_body, place, [normed, *w_parts],
        [shape(width, 3 * MW), shape(4 * MW, cols), shape(count, 3 * MW), shape(lat, MW)],
        6 * count * width * MW + 4 * lat * count * MW,
    )
    w_row_blocks = spread_rel([w_rel[j * MW : (j + 1) * MW] for j in range(4)])
    enc_blocks = gather_rel(enc_o)
    enc_blocks[1], ups = lax.optimization_barrier((enc_blocks[1], ups))
    z_cols, enc_all = kernel_call(
        latents_body, place, [*rows, *enc_blocks, w_rel],
        [shape(lat, cols), shape(lat, 4 * MW)], 8 * lat * cols * MW,
    )
    z_crossed = cross_section(z_cols, 0)
    up_o, w_row = kernel_call(
        upstream_body, place, [*ups, *w_row_blocks],
        [shape(count, MW), shape(MW, width)], 2 * count * width * MW,
    )
    z_blocks = gather_rel(after(z_crossed, up_o))
    z_blocks = z_blocks[2:] + z_blocks[:2]

    decoder_shapes = [
        shape(count, MW), shape(count, 3 * MW), shape(lat, 2 * MW), shape(lat, width),
        shape(lat, 1, f32), shape(half, width), shape(2 * half, width), shape(2 * half, width),
        shape(1, width, f32),
    ]
    dec_o, d_proj, d_kvz, nz, z_scale, z_own, own, near, z_gain = lax.cond(
        is_encoder,
        lambda: tuple(jnp.zeros(s.shape, s.dtype) for s in decoder_shapes),
        lambda: tuple(kernel_call(
            decoder_body, place, [gains, *z_blocks, w_h, projected, up_o], decoder_shapes,
            8 * lat * width * MW + 12 * count * (lat + 128) * MW,
            [pltpu.VMEM((lat, width), bf16), pltpu.VMEM((lat, 2 * MW), bf16),
             pltpu.VMEM((lat, 2 * MW), f32)],
        )),
    )
    d_nz = sum_far(*sum_near(own, near))
    d_z = norm_back(z_own, z_scale[:half], gains[0], d_nz)
    d_z = d_z.astype(bf16)
    dec_blocks = gather_rel(after(dec_o, d_z))
    d_z = cross_section(d_z, 1)
    d_z_blocks = gather_rel(after(d_z, *dec_blocks))
    d_z_blocks = d_z_blocks[2:] + d_z_blocks[:2]
    d_z = d_z_blocks[0]

    part_shapes = [shape(2 * n, width // 2)] * 8
    back_flops = 6 * width * count * MW + 2 * lat * width * MW
    d_proj, *parts = lax.cond(
        is_encoder,
        lambda: tuple(kernel_call(
            encoder_back_body, place, [*d_z_blocks, w_row, projected, normed_t, enc_all],
            [shape(count, 3 * MW)] + part_shapes, back_flops + 2 * lat * width * MW + 10 * lat * count * MW,
            [pltpu.VMEM((lat, width), bf16), pltpu.VMEM((lat, MW), bf16),
             pltpu.VMEM((4 * MW, cols), bf16)],
        )),
        lambda: (d_proj, *kernel_call(
            decoder_back_body, place, [d_proj, d_kvz, nz, normed_t, *ups, *dec_blocks],
            part_shapes, back_flops + 4 * lat * width * MW,
            [pltpu.VMEM((width, lat), bf16), pltpu.VMEM((count, 4 * MW), bf16),
             pltpu.VMEM((4 * MW, cols), bf16), pltpu.VMEM((count, cols), bf16)],
        )),
    )
    parts = ring_sum_far(parts)
    own, near, gain_part = kernel_call(
        input_grads_body, place, [d_proj, w_h, scales, z_gain, *rows],
        [shape(2 * n, width)] * 2 + [shape(1, width, f32)], 6 * count * width * MW,
    )
    d_n, far = sum_near(own, near)
    gain_part = sum_over_render(gain_part)
    parts, far, gain_part = lax.optimization_barrier((parts, far, gain_part))
    gain_total = sum_over_dp(gain_part)
    parts[0], gain_total = lax.optimization_barrier((parts[0], gain_total))
    d_n = sum_far(d_n, far)
    sums = ring_sum_near(parts)
    sums_far, d_n = lax.optimization_barrier((z_swap(sums), d_n))
    qkv_total, out_total = kernel_call(
        totals_body, place, [sums, core_swap(sums), sums_far, core_swap(sums_far)],
        [shape(n, 12 * MW, f32), shape(half, width, f32)], n * width,
    )
    back = norm_back(tokens, scales[:n], gains[0], d_n)
    residual = jnp.where(
        is_encoder,
        jnp.pad(d_z.astype(f32), ((half, 0), (0, 0))),
        upstream.astype(f32),
    )
    token_grad = (back + residual).astype(bf16)
    return token_grad[None, None], qkv_total[None], out_total[None], gain_total


def solution(mesh):
    fine = Mesh(mesh.devices.reshape(2, 2, 2, 4, 4), ("section", "zl", "core", "y", "x"))
    in_specs = (
        P("section", DP, RENDER, None),
        P("section", DP, None),
        P("section", DP, None),
        P("section", None),
        P(DP, RENDER, None),
    )
    out_specs = (
        P("section", DP, RENDER, None),
        P("section", DP, None),
        P("section", DP, None),
        P("section", None),
    )
    return jax.shard_map(shards, mesh=fine, in_specs=in_specs, out_specs=out_specs, check_vma=False)
```
